32 devices in a mesh: vec: 4 (over y, core), lat: 2 (over x), lon: 4 (over z).
Axes of the slice: x: 2, y: 2, z: 4, core: 2. Of those that a mesh axis runs over, the one named last changes fastest.
Arguments:
- basis: bfloat16 [4, 5, 48, 16, 512], P('vec', None, None, 'lat', 'lon'), may hold values from -4 to 4
- trajectory: bfloat16 [4, 5, 48, 16, 512], P('vec', None, None, 'lat', 'lon'), may hold values from -4 to 4
- slice_owner: int32 [4], replicated, may hold values from 0 to 3, each once
- diffusion: float32 [5, 47], replicated, may hold values from 0.05 to 2
- energy_weight: float32 [5], replicated, may hold values from 0.5 to 2
Outputs:
- residual_block: float32 [4, 5, 48, 16, 512], P('vec', None, None, 'lat', 'lon')
- coupling: float32 [4, 4], replicated
The draws below stay inside these ranges and needn't reach their ends.
Inputs may be any that keep to these rules, and one draw needn't show every extreme that they name: `slice_owner`: a permutation: each vector group holds the slice of exactly one timestep.
All inputs are finite; a program needn't handle non-finite values.
Results may differ from the reference program's by a relative error of at most 0.0024.
Values may be sent and summed in bfloat16 or wider, within the bound.
A program may use at most 64 MiB of HBM per device.

```python
import math
import jax
import jax.numpy as jnp
from jax import lax

F = 5
LEV = 48
STEPS = 2
VECS = 4
GROUPS = 4
NLAT = 16
NLON = 512


def pattern_phases(key):
    key = jax.random.fold_in(key, 101)
    return jax.random.randint(key, (2,), 0, 4)


def envelope_table(position):
    return jnp.where(position == 0, 1.4, jnp.where(position == 2, 0.4, 1.0)).astype(jnp.float32)


def wave_table(position):
    return jnp.where(position == 1, 1.0, jnp.where(position == 3, -1.0, 0.0)).astype(jnp.float32)


def draw_basis(key, part):
    phases = pattern_phases(key)
    key = jax.random.fold_in(key, 7)
    shape = (VECS, F, LEV, NLAT, NLON)
    amplitude = jax.random.uniform(jax.random.fold_in(key, 1), (VECS, 1, 1, 1, 1), jnp.float32, 0.3, 0.6)
    common = jax.random.normal(jax.random.fold_in(key, 2), shape[1:], jnp.float32)
    private = 0.6 * jax.random.normal(jax.random.fold_in(key, 3), shape, jnp.float32)
    values = amplitude * common[None] + private
    lon_pos = jnp.arange(NLON)
    lat_pos = jnp.arange(NLAT)
    lon_env = envelope_table((lon_pos + phases[0]) % 4)
    lat_env = envelope_table((lat_pos + phases[1]) % 4)
    ramp = 0.4 + 1.2 * (lon_pos.astype(jnp.float32) + 0.5) / NLON
    blocks = jnp.exp(jax.random.uniform(jax.random.fold_in(key, 4), (8, 8), jnp.float32, math.log(0.7), math.log(1.3)))
    lat_block = lat_pos * 8 // NLAT
    lon_block = lon_pos * 8 // NLON
    block_factor = blocks[lat_block][:, lon_block]
    envelope = lat_env[:, None] * lon_env[None, :] * ramp[None, :] * block_factor
    values = values * envelope
    return jnp.clip(values, -4.0, 4.0).astype(jnp.bfloat16)


def draw_trajectory(key, part):
    phases = pattern_phases(key)
    key = jax.random.fold_in(key, 11)
    shape = (GROUPS, F, LEV, NLAT, NLON)
    noise = jax.random.normal(jax.random.fold_in(key, 1), shape, jnp.float32)
    lon_pos = jnp.arange(NLON)
    lat_pos = jnp.arange(NLAT)
    lon_ramp = 1.0 + 2.6 * (lon_pos.astype(jnp.float32) + 0.5) / NLON
    u_pattern = lon_ramp * wave_table((lon_pos + phases[0]) % 4)
    v_pattern = 3.0 * wave_table((lat_pos + phases[1]) % 4)
    field_ids = jnp.arange(F)[None, :, None, None, None]
    noise_scale = jnp.where(field_ids < 2, 0.3, 1.0)
    pattern = jnp.where(field_ids == 0, u_pattern[None, None, None, None, :], jnp.where(field_ids == 1, v_pattern[None, None, None, :, None], 0.0))
    values = pattern + noise_scale * noise
    return jnp.clip(values, -4.0, 4.0).astype(jnp.bfloat16)


def setup_inputs(seed: int = 0) -> dict:
    key_list = jax.random.split(jax.random.key(seed), 6)
    basis = draw_basis(jax.random.fold_in(key_list[5], 71), 0)
    trajectory = draw_trajectory(jax.random.fold_in(key_list[5], 71), 0)
    slice_owner = jax.random.permutation(key_list[2], GROUPS).astype(jnp.int32)
    diffusion = jnp.clip(jnp.exp(jax.random.uniform(key_list[3], (F, LEV - 1), jnp.float32, math.log(0.05), math.log(2.0))), 0.05, 2.0)
    energy_weight = jnp.clip(jnp.exp(jax.random.uniform(key_list[4], (F,), jnp.float32, math.log(0.5), math.log(2.0))), 0.5, 2.0)
    return dict(basis=basis, trajectory=trajectory, slice_owner=slice_owner, diffusion=diffusion, energy_weight=energy_weight)


COURANT = 0.25
HIGH = lax.Precision.HIGHEST

def implicit_inverse(diffusion):
    level_count = diffusion.shape[1] + 1
    below_k = jnp.pad(diffusion, ((0, 0), (0, 1)))
    above_k = jnp.pad(diffusion, ((0, 0), (1, 0)))
    levels = jnp.arange(level_count)
    above_diag = (levels[:, None] + 1 == levels[None, :]).astype(jnp.float32)[None] * below_k[:, :, None]
    identity_mat = jnp.eye(level_count, dtype=jnp.float32)
    matrix = identity_mat[None] * (1.0 + below_k + above_k)[:, :, None] - above_diag - jnp.swapaxes(above_diag, 1, 2)
    factor = jnp.linalg.cholesky(matrix)
    inverse_factor = lax.linalg.triangular_solve(factor, jnp.broadcast_to(identity_mat, matrix.shape), left_side=True, lower=True)
    return jnp.einsum('fkl,fkm->flm', inverse_factor, inverse_factor, precision=HIGH)

def tendency(field, field_lat, field_lon, state, state_lat, state_lon):
    field_dlon = (field_lon[..., 2:] - field_lon[..., :-2]) * 0.5
    field_dlat = (field_lat[..., 2:, :] - field_lat[..., :-2, :]) * 0.5
    state_dlon = (state_lon[..., 2:] - state_lon[..., :-2]) * 0.5
    state_dlat = (state_lat[..., 2:, :] - state_lat[..., :-2, :]) * 0.5
    wind_u = state[0]
    wind_v = state[1]
    return wind_u * field_dlon + wind_v * field_dlat + field[:, 0:1] * state_dlon + field[:, 1:2] * state_dlat

def reference(basis, trajectory, slice_owner, diffusion, energy_weight):
    inverse = implicit_inverse(diffusion)
    field = basis.astype(jnp.float32)
    for timestep in range(STEPS):
        state = lax.dynamic_index_in_dim(trajectory, slice_owner[timestep], 0, keepdims=False).astype(jnp.float32)
        field_lat = jnp.pad(field, ((0, 0), (0, 0), (0, 0), (1, 1), (0, 0)))
        field_lon = jnp.concatenate([field[..., -1:], field, field[..., :1]], axis=4)
        state_lat = jnp.pad(state, ((0, 0), (0, 0), (1, 1), (0, 0)))
        state_lon = jnp.concatenate([state[..., -1:], state, state[..., :1]], axis=3)
        moved = field - COURANT * tendency(field, field_lat, field_lon, state, state_lat, state_lon)
        field = jnp.einsum('fkl,vflyx->vfkyx', inverse, moved, precision=HIGH)
    latitude = (jnp.arange(NLAT).astype(jnp.float32) + 0.5) * (jnp.pi / NLAT) - jnp.pi / 2
    total = float(F * LEV * NLAT * NLON)
    scale = energy_weight[:, None, None, None] * jnp.cos(latitude)[None, None, :, None] / total
    weighted = field * scale
    basis_wide = basis.astype(jnp.float32)
    coupling = jnp.einsum('iflyx,jflyx->ij', basis_wide, weighted, precision=HIGH)
    residual_block = field - jnp.einsum('iflyx,ij->jflyx', basis_wide, coupling, precision=HIGH)
    return (residual_block, coupling)
```

```python
import functools
import math

import jax
import jax.numpy as jnp
from jax import lax
from jax.experimental import pallas as pl
from jax.experimental.pallas import tpu as pltpu
from jax.sharding import PartitionSpec as P

STEPS = 2
COURANT = 0.25
MESH = pl.DeviceIdType.MESH
F32 = jnp.float32
BF16 = jnp.bfloat16


def copy_names(pairs, tiles, groups):
    names = ["traj", "basis"]
    for d in range(1, pairs):
        names += [(kind, k, d) for kind in ("cross", "relay") for k in range(2)]
        names += [(kind, t, d) for kind in ("slice", "pass") for t in range(STEPS)]
    for t in range(STEPS):
        names += [(kind, t, s) for kind in ("flon", "flat", "slon", "slat") for s in range(2)]
    names += [("sum", k) for k in range(1, tiles)]
    names += [("col", k) for k in range(1, groups)]
    return {name: i for i, name in enumerate(names)}


def kernel(
    shape,
    counts,
    ids,
    basis_ref,
    traj_ref,
    owner_ref,
    diff_ref,
    weight_ref,
    out_ref,
    coup_ref,
    sib_traj,
    sel,
    rcv,
    allb,
    field,
    state,
    coef,
    lon_out,
    lon_in,
    lat_out,
    lat_in,
    lon_mix,
    sums,
    cols,
    send_sem,
    recv_sem,
):
    fields, levels, rows, lanes = shape
    groups, lats, lons = counts
    pairs, tiles = groups // 2, lats * lons
    size = fields * levels * rows
    per_field = levels * rows
    half = size // 2
    vec = lax.axis_index("vec")
    lat = lax.axis_index("lat")
    lon = lax.axis_index("lon")
    core = lax.rem(vec, 2)
    pair = vec // 2
    sibling = vec + 1 - 2 * core
    me = lat * lons + lon

    def other_tile(k):
        index = lax.rem(me + k, tiles)
        return {"lat": index // lons, "lon": lax.rem(index, lons)}

    def other_vec(k):
        return {"vec": lax.rem(vec + k, groups)}

    def partner(d):
        return {"vec": 2 * lax.rem(pair + d, pairs) + core}

    def remote(name, src, dst, device):
        return pltpu.make_async_remote_copy(
            src_ref=src,
            dst_ref=dst,
            send_sem=send_sem.at[ids[name]],
            recv_sem=recv_sem.at[ids[name]],
            device_id=device,
            device_id_type=MESH,
        )

    barrier = pltpu.get_barrier_semaphore()
    for k in range(1, tiles):
        pl.semaphore_signal(barrier, inc=1, device_id=other_tile(k), device_id_type=MESH)
    for k in range(1, groups):
        pl.semaphore_signal(barrier, inc=1, device_id=other_vec(k), device_id_type=MESH)
    pl.semaphore_wait(barrier, tiles + groups - 2)

    parts = ((0, per_field), (per_field, size - per_field))
    to_sibling = {"vec": sibling}
    own_half = pl.ds(pl.multiple_of(core * half, 16), half)

    traj_copy = remote("traj", traj_ref, sib_traj, to_sibling)
    traj_copy.start()
    cross = {}
    relay = {}
    for d in range(1, pairs):
        source = 2 * lax.rem(pair + pairs - d, pairs) + core
        for k, (first, count) in enumerate(parts):
            chunk = pl.ds(first, count)
            cross[k, d] = remote(
                ("cross", k, d), basis_ref.at[chunk], allb.at[vec, chunk], partner(d)
            )
            relay[k, d] = remote(
                ("relay", k, d), allb.at[source, chunk], allb.at[source, chunk], to_sibling
            )
    for d in range(1, pairs):
        cross[0, d].start()
    basis_copy = remote("basis", basis_ref, allb.at[vec], to_sibling)
    basis_copy.start()

    lane = lax.broadcasted_iota(jnp.int32, (rows, lanes), 1)
    row = lax.broadcasted_iota(jnp.int32, (rows, lanes), 0)

    def edge_copies(kind, slot, t):
        east = {"lon": lax.rem(lon + 1, lons)}
        west = {"lon": lax.rem(lon + lons - 1, lons)}
        up = {"lat": lax.rem(lat + 1, lats)}
        down = {"lat": lax.rem(lat + lats - 1, lats)}
        return (
            remote((kind + "lon", t, 0), lon_out.at[slot], lon_in.at[slot, 0], east),
            remote((kind + "lon", t, 1), lon_out.at[slot], lon_in.at[slot, 1], west),
            remote((kind + "lat", t, 0), lat_out.at[slot, 1], lat_in.at[slot, 0], up),
            remote((kind + "lat", t, 1), lat_out.at[slot, 0], lat_in.at[slot, 1], down),
        )

    def start_edges(copies):
        copies[0].start()
        copies[1].start()

        @pl.when(lat < lats - 1)
        def _():
            copies[2].start()

        @pl.when(lat > 0)
        def _():
            copies[3].start()

    def await_edges(copies, slot):
        copies[0].wait_recv()
        copies[1].wait_recv()

        @pl.when(lat > 0)
        def _():
            copies[2].wait_recv()

        @pl.when(lat < lats - 1)
        def _():
            copies[3].wait_recv()

        for f in range(fields):
            lon_mix[slot, f] = jnp.where(
                lax.rem(lane, 2) == 0,
                pltpu.roll(lon_in[slot, 0, f], 1, 1),
                pltpu.roll(lon_in[slot, 1, f], lanes - 1, 1),
            )

    def await_edges_sent(copies):
        copies[0].wait_send()
        copies[1].wait_send()

        @pl.when(lat < lats - 1)
        def _():
            copies[2].wait_send()

        @pl.when(lat > 0)
        def _():
            copies[3].wait_send()

    def note_edges(slot, f, level, tile, packed):
        lat_out[slot, 0, f, level] = tile[0:1]
        lat_out[slot, 1, f, level] = tile[rows - 1 : rows]
        spot = 2 * level
        here = (lane == spot) | (lane == lax.rem(spot + lanes - 1, lanes))
        return jnp.where(here, pltpu.roll(tile, spot, 1), packed)

    no_tiles = tuple(jnp.zeros((rows, lanes), F32) for _ in range(fields))

    def spread(load, store, slot):
        def body(m, packed):
            done = []
            for f in range(fields):
                first = pl.multiple_of(f * per_field + m * 2 * rows, 2 * rows)
                both = load(pl.ds(first, 2 * rows))
                p = packed[f]
                for i in range(2):
                    tile = both[i * rows : (i + 1) * rows]
                    store(f, 2 * m + i, tile)
                    p = note_edges(slot, f, 2 * m + i, tile, p)
                done.append(p)
            return tuple(done)

        packed = lax.fori_loop(0, levels // 2, body, no_tiles)
        for f in range(fields):
            lon_out[slot, f] = packed[f]

    for slot in range(2 * STEPS):

        @pl.when(lat == 0)
        def _():
            lat_in[slot, 0] = jnp.zeros((fields, levels, 1, lanes), F32)

        @pl.when(lat == lats - 1)
        def _():
            lat_in[slot, 1] = jnp.zeros((fields, levels, 1, lanes), F32)

    def load_basis(where):
        block = basis_ref[where, :]
        allb[vec, where, :] = block
        return block.astype(F32)

    def store_field(f, level, tile):
        field[f, level] = tile

    spread(load_basis, store_field, 0)
    field_edges = [edge_copies("f", t, t) for t in range(STEPS)]
    state_edges = [edge_copies("s", STEPS + t, t) for t in range(STEPS)]
    start_edges(field_edges[0])

    traj_copy.wait_recv()
    slices = {}
    passes = {}
    for t in range(STEPS):
        sel[t] = jnp.where(
            owner_ref[t] == vec, traj_ref[...].astype(F32), sib_traj[...].astype(F32)
        ).astype(BF16)
        for d in range(1, pairs):
            slices[t, d] = remote(
                ("slice", t, d), sel.at[t, own_half], rcv.at[t, d - 1, own_half], partner(d)
            )
            passes[t, d] = remote(
                ("pass", t, d), rcv.at[t, d - 1, own_half], rcv.at[t, d - 1, own_half], to_sibling
            )
            slices[t, d].start()

    def pivots(level, carry):
        done = []
        for f in range(fields):
            above, ratio = carry[f]
            below = jnp.full((rows, lanes), diff_ref[f, level], F32)
            inv = 1.0 / (1.0 + below + above - above * ratio)
            coef[0, f, level] = inv
            coef[1, f, level] = above * inv
            coef[2, f, level] = below * inv
            done.append((below, below * inv))
        return tuple(done)

    zero = jnp.zeros((rows, lanes), F32)
    carry = lax.fori_loop(0, levels - 1, pivots, tuple((zero, zero) for _ in range(fields)))
    for f in range(fields):
        above, ratio = carry[f]
        inv = 1.0 / (1.0 + above - above * ratio)
        coef[0, f, levels - 1] = inv
        coef[1, f, levels - 1] = above * inv
        coef[2, f, levels - 1] = zero

    def take_state(t):
        for d in range(1, pairs):
            slices[t, d].wait_recv()
            passes[t, d].start()

    def build_state(t):
        for d in range(1, pairs):
            passes[t, d].wait_recv()
        holder = owner_ref[t] // 2

        def load_state(where):
            block = sel[t, where, :].astype(F32)
            for d in range(1, pairs):
                source = lax.rem(pair + pairs - d, pairs)
                block = jnp.where(holder == source, rcv[t, d - 1, where, :].astype(F32), block)
            return block

        def store_state(f, level, tile):
            state[t, f, level] = tile

        spread(load_state, store_state, STEPS + t)
        start_edges(state_edges[t])

    def dlon(tile, mix, shift):
        mix = pltpu.roll(mix, shift, 1)
        after = jnp.where(lane == lanes - 1, mix, pltpu.roll(tile, lanes - 1, 1))
        before = jnp.where(lane == 0, mix, pltpu.roll(tile, 1, 1))
        return after - before

    def dlat(tile, low, high):
        after = jnp.where(row == rows - 1, high, pltpu.roll(tile, rows - 1, 0))
        before = jnp.where(row == 0, low, pltpu.roll(tile, 1, 0))
        return after - before

    def step(t):
        fslot, sslot = t, STEPS + t

        def forward(level, solved):
            wind_u, wind_v = state[t, 0, level], state[t, 1, level]
            pert_u, pert_v = field[0, level], field[1, level]
            shift = lax.rem(lanes - 2 * level, lanes)
            done = []
            for f in range(fields):
                a, s = field[f, level], state[t, f, level]
                change = wind_u * dlon(a, lon_mix[fslot, f], shift)
                change += wind_v * dlat(a, lat_in[fslot, 0, f, level], lat_in[fslot, 1, f, level])
                change += pert_u * dlon(s, lon_mix[sslot, f], shift)
                change += pert_v * dlat(s, lat_in[sslot, 0, f, level], lat_in[sslot, 1, f, level])
                moved = a - (0.5 * COURANT) * change
                done.append(moved * coef[0, f, level] + solved[f] * coef[1, f, level])
            for f in range(fields):
                field[f, level] = done[f]
            return tuple(done)

        lax.fori_loop(0, levels, forward, no_tiles)
        last = t == STEPS - 1

        def backward(k, carry):
            level = levels - 1 - k
            above, packed = carry
            done, edges = [], []
            for f in range(fields):
                x = field[f, level] + coef[2, f, level] * above[f]
                field[f, level] = x
                done.append(x)
                if not last:
                    edges.append(note_edges(t + 1, f, level, x, packed[f]))
            return tuple(done), tuple(edges)

        _, packed = lax.fori_loop(0, levels, backward, (no_tiles, () if last else no_tiles))
        if not last:
            for f in range(fields):
                lon_out[t + 1, f] = packed[f]
            start_edges(field_edges[t + 1])

    for t in range(STEPS):
        take_state(t)
        if t == 0:
            for d in range(1, pairs):
                cross[1, d].start()
        build_state(t)
        if t == 0:
            for d in range(1, pairs):
                cross[0, d].wait_recv()
                relay[0, d].start()
        await_edges(field_edges[t], t)
        await_edges(state_edges[t], STEPS + t)
        step(t)

    basis_copy.wait_recv()
    for d in range(1, pairs):
        cross[1, d].wait_recv()
        relay[1, d].start()
    for d in range(1, pairs):
        relay[0, d].wait_recv()
        relay[1, d].wait_recv()

    total_rows = rows * lats
    total = float(fields * levels * total_rows * lanes * lons)
    row_ids = (lat * rows + row).astype(F32)
    cosine = jnp.cos((row_ids + 0.5) * (math.pi / total_rows) - math.pi / 2)

    def load_vector(i, f, m):
        first = pl.multiple_of(f * per_field + m * 2 * rows, 2 * rows)
        return allb[i, pl.ds(first, 2 * rows), :].astype(F32)

    def gram(m, acc):
        acc = list(acc)
        for f in range(fields):
            scale = weight_ref[f] * cosine / total
            low = field[f, 2 * m] * scale
            high = field[f, 2 * m + 1] * scale
            for i in range(groups):
                b = load_vector(i, f, m)
                acc[i] += b[:rows] * low + b[rows:] * high
        return tuple(acc)

    acc = lax.fori_loop(0, levels // 2, gram, tuple(zero for _ in range(groups)))
    part = jnp.zeros((8, lanes), F32)
    part_row = lax.broadcasted_iota(jnp.int32, (8, lanes), 0)
    for i in range(groups):
        part = jnp.where(part_row == i, jnp.sum(acc[i], axis=0, keepdims=True), part)
    sums[me] = part
    sum_copies = []
    for k in range(1, tiles):
        copy = remote(("sum", k), sums.at[me], sums.at[me], other_tile(k))
        copy.start()
        sum_copies.append(copy)
    for copy in sum_copies:
        copy.wait_recv()
    whole = sums[0]
    for k in range(1, tiles):
        whole += sums[k]
    column = jnp.sum(whole, axis=1, keepdims=True)
    cols[vec] = jnp.broadcast_to(column, (8, lanes))
    col_copies = []
    for k in range(1, groups):
        copy = remote(("col", k), cols.at[vec], cols.at[vec], other_vec(k))
        copy.start()
        col_copies.append(copy)
    factor = [jnp.broadcast_to(column[i : i + 1], (rows, lanes)) for i in range(groups)]

    def residual(m, carry):
        for f in range(fields):
            low, high = field[f, 2 * m], field[f, 2 * m + 1]
            for i in range(groups):
                b = load_vector(i, f, m)
                low -= b[:rows] * factor[i]
                high -= b[rows:] * factor[i]
            out_ref[f, 2 * m] = low
            out_ref[f, 2 * m + 1] = high
        return carry

    lax.fori_loop(0, levels // 2, residual, 0)
    for copy in col_copies:
        copy.wait_recv()
    table = jnp.zeros((8, lanes), F32)
    wide_lane = lax.broadcasted_iota(jnp.int32, (8, lanes), 1)
    for j in range(groups):
        table = jnp.where(wide_lane == j, cols[j], table)
    coup_ref[...] = table[:groups, :groups]

    traj_copy.wait_send()
    basis_copy.wait_send()
    for d in range(1, pairs):
        for k in range(2):
            cross[k, d].wait_send()
            relay[k, d].wait_send()
        for t in range(STEPS):
            slices[t, d].wait_send()
            passes[t, d].wait_send()
    for t in range(STEPS):
        await_edges_sent(field_edges[t])
        await_edges_sent(state_edges[t])
    for copy in sum_copies + col_copies:
        copy.wait_send()


def solution(mesh):
    groups, lats, lons = mesh.shape["vec"], mesh.shape["lat"], mesh.shape["lon"]

    def per_device(basis, trajectory, slice_owner, diffusion, energy_weight):
        _, fields, levels, rows, lanes = basis.shape
        size = fields * levels * rows
        pairs, tiles = groups // 2, lats * lons
        ids = copy_names(pairs, tiles, groups)
        slots = 2 * STEPS
        vmem = pl.BlockSpec(memory_space=pltpu.VMEM)
        smem = pl.BlockSpec(memory_space=pltpu.SMEM)
        residual_block, coupling = pl.pallas_call(
            functools.partial(kernel, (fields, levels, rows, lanes), (groups, lats, lons), ids),
            out_shape=(
                jax.ShapeDtypeStruct((fields, levels, rows, lanes), F32),
                jax.ShapeDtypeStruct((groups, groups), F32),
            ),
            in_specs=[vmem, vmem, smem, smem, smem],
            out_specs=(vmem, vmem),
            scratch_shapes=[
                pltpu.VMEM((size, lanes), BF16),
                pltpu.VMEM((STEPS, size, lanes), BF16),
                pltpu.VMEM((STEPS, max(pairs - 1, 1), size, lanes), BF16),
                pltpu.VMEM((groups, size, lanes), BF16),
                pltpu.VMEM((fields, levels, rows, lanes), F32),
                pltpu.VMEM((STEPS, fields, levels, rows, lanes), F32),
                pltpu.VMEM((3, fields, levels, rows, lanes), F32),
                pltpu.VMEM((slots, fields, rows, lanes), F32),
                pltpu.VMEM((slots, 2, fields, rows, lanes), F32),
                pltpu.VMEM((slots, 2, fields, levels, 1, lanes), F32),
                pltpu.VMEM((slots, 2, fields, levels, 1, lanes), F32),
                pltpu.VMEM((slots, fields, rows, lanes), F32),
                pltpu.VMEM((tiles, 8, lanes), F32),
                pltpu.VMEM((groups, 8, lanes), F32),
                pltpu.SemaphoreType.DMA((len(ids),)),
                pltpu.SemaphoreType.DMA((len(ids),)),
            ],
            compiler_params=pltpu.CompilerParams(
                collective_id=0, has_side_effects=True, vmem_limit_bytes=48 * 1024 * 1024
            ),
        )(
            basis.reshape(size, lanes),
            trajectory.reshape(size, lanes),
            slice_owner,
            diffusion,
            energy_weight,
        )
        return residual_block[None], coupling

    return jax.shard_map(
        per_device,
        mesh=mesh,
        in_specs=(
            P("vec", None, None, "lat", "lon"),
            P("vec", None, None, "lat", "lon"),
            P(),
            P(),
            P(),
        ),
        out_specs=(P("vec", None, None, "lat", "lon"), P()),
        check_vma=False,
    )
```

```python
import functools
import math

import jax
import jax.numpy as jnp
from jax import lax
from jax.experimental import pallas as pl
from jax.experimental.pallas import tpu as pltpu
from jax.sharding import PartitionSpec as P

STEPS = 2
COURANT = 0.25
MESH = pl.DeviceIdType.MESH
F32 = jnp.float32
BF16 = jnp.bfloat16


def copy_names(pairs, tiles, groups, fields):
    names = [("traj", 0), ("traj", 1), "basis"]
    for d in range(1, pairs):
        names += [(kind, k, d) for kind in ("cross", "relay") for k in range(fields)]
        names += [(kind, t, d) for kind in ("slice", "pass") for t in range(STEPS)]
    for t in range(STEPS):
        names += [(kind, t, s) for kind in ("flon", "flat", "slon", "slat") for s in range(2)]
    names += [("sum", k) for k in range(1, tiles)]
    names += [("col", k) for k in range(1, groups)]
    return {name: i for i, name in enumerate(names)}


def kernel(
    shape,
    counts,
    ids,
    basis_ref,
    traj_ref,
    owner_in,
    diff_in,
    weight_in,
    out_ref,
    coup_ref,
    owner_ref,
    diff_ref,
    weight_ref,
    own_traj,
    sib_traj,
    sel,
    rcv,
    allb,
    field,
    state,
    coef,
    lon_out,
    lon_in,
    lat_out,
    lat_in,
    lat_wide,
    lon_mix,
    lat_rows,
    sums,
    cols,
    local_sem,
    send_sem,
    recv_sem,
):
    fields, levels, rows, lanes = shape
    groups, lats, lons = counts
    pairs, tiles = groups // 2, lats * lons
    size = fields * levels * rows
    per_field = levels * rows
    half = size // 2
    vec = lax.axis_index("vec")
    lat = lax.axis_index("lat")
    lon = lax.axis_index("lon")
    core = lax.rem(vec, 2)
    pair = vec // 2
    sibling = vec + 1 - 2 * core
    me = lat * lons + lon

    def other_tile(k):
        index = lax.rem(me + k, tiles)
        return {"lat": index // lons, "lon": lax.rem(index, lons)}

    def other_vec(k):
        return {"vec": lax.rem(vec + k, groups)}

    def partner(d):
        return {"vec": 2 * lax.rem(pair + d, pairs) + core}

    def remote(name, src, dst, device):
        return pltpu.make_async_remote_copy(
            src_ref=src,
            dst_ref=dst,
            send_sem=send_sem.at[ids[name]],
            recv_sem=recv_sem.at[ids[name]],
            device_id=device,
            device_id_type=MESH,
        )

    local = [
        pltpu.make_async_copy(source, target, local_sem.at[i])
        for i, (source, target) in enumerate(
            (
                (basis_ref, allb.at[vec]),
                (traj_ref, own_traj),
                (owner_in, owner_ref),
                (diff_in, diff_ref),
                (weight_in, weight_ref),
            )
        )
    ]
    for copy in local:
        copy.start()

    barrier = pltpu.get_barrier_semaphore()
    for k in range(1, tiles):
        pl.semaphore_signal(barrier, inc=1, device_id=other_tile(k), device_id_type=MESH)
    for k in range(1, groups):
        pl.semaphore_signal(barrier, inc=1, device_id=other_vec(k), device_id_type=MESH)
    pl.semaphore_wait(barrier, tiles + groups - 2)

    to_sibling = {"vec": sibling}
    own_half = pl.ds(pl.multiple_of(core * half, 16), half)
    far_half = pl.ds(pl.multiple_of((1 - core) * half, 16), half)

    traj_copies = [
        remote(("traj", i), traj_ref.at[part], sib_traj.at[part], to_sibling)
        for i, part in enumerate((far_half, own_half))
    ]
    traj_copies[0].start()
    cross = {}
    relay = {}
    for d in range(1, pairs):
        source = 2 * lax.rem(pair + pairs - d, pairs) + core
        for f in range(fields):
            chunk = pl.ds(f * per_field, per_field)
            cross[f, d] = remote(
                ("cross", f, d), basis_ref.at[chunk], allb.at[vec, chunk], partner(d)
            )
            relay[f, d] = remote(
                ("relay", f, d), allb.at[source, chunk], allb.at[source, chunk], to_sibling
            )
    for d in range(1, pairs):
        cross[0, d].start()
    traj_copies[1].start()
    basis_copy = remote("basis", basis_ref, allb.at[vec], to_sibling)
    basis_copy.start()

    lane = lax.broadcasted_iota(jnp.int32, (rows, lanes), 1)
    row = lax.broadcasted_iota(jnp.int32, (rows, lanes), 0)

    def edge_copies(kind, slot, t):
        east = {"lon": lax.rem(lon + 1, lons)}
        west = {"lon": lax.rem(lon + lons - 1, lons)}
        up = {"lat": lax.rem(lat + 1, lats)}
        down = {"lat": lax.rem(lat + lats - 1, lats)}
        narrow = kind == "s" or t == 0
        source = lat_out.at[slot] if narrow else lat_wide.at[t - 1]
        target = lat_in.at[slot] if narrow else lat_rows.at[slot]
        return (
            remote((kind + "lon", t, 0), lon_out.at[slot], lon_in.at[slot, 0], east),
            remote((kind + "lon", t, 1), lon_out.at[slot], lon_in.at[slot, 1], west),
            remote((kind + "lat", t, 0), source.at[1], target.at[0], up),
            remote((kind + "lat", t, 1), source.at[0], target.at[1], down),
        )

    def start_edges(copies):
        copies[0].start()
        copies[1].start()

        @pl.when(lat < lats - 1)
        def _():
            copies[2].start()

        @pl.when(lat > 0)
        def _():
            copies[3].start()

    def await_edges(copies, slot):
        narrow = slot == 0 or slot >= STEPS
        copies[0].wait_recv()
        copies[1].wait_recv()

        def settle(copy, side, present):
            @pl.when(present)
            def _():
                copy.wait_recv()
                if narrow:
                    lat_rows[slot, side] = lat_in[slot, side].astype(F32)

            @pl.when(jnp.logical_not(present))
            def _():
                lat_rows[slot, side] = jnp.zeros((fields * levels, lanes), F32)

        settle(copies[2], 0, lat > 0)
        settle(copies[3], 1, lat < lats - 1)

        for f in range(fields):
            lon_mix[slot, f] = jnp.where(
                lax.rem(lane, 2) == 0,
                pltpu.roll(lon_in[slot, 0, f], 1, 1),
                pltpu.roll(lon_in[slot, 1, f], lanes - 1, 1),
            )

    def await_edges_sent(copies):
        copies[0].wait_send()
        copies[1].wait_send()

        @pl.when(lat < lats - 1)
        def _():
            copies[2].wait_send()

        @pl.when(lat > 0)
        def _():
            copies[3].wait_send()

    def at(f, level):
        return pl.ds(pl.multiple_of(f * per_field + level * rows, rows), rows)

    def note_edges(level, tile, packed):
        spot = 2 * level
        here = (lane == spot) | (lane == lax.rem(spot + lanes - 1, lanes))
        return jnp.where(here, pltpu.roll(tile, spot, 1), packed)

    def pack_rows(tiles_ref, target):
        for f in range(fields):
            for side in range(2):
                first = f * per_field + side * (rows - 1)
                edge = tiles_ref[pl.ds(first, levels, stride=rows), :]
                target[side, f * levels : (f + 1) * levels, :] = edge.astype(target.dtype)

    no_tiles = tuple(jnp.zeros((rows, lanes), F32) for _ in range(fields))

    def spread(load, tiles_ref, slot):
        def body(m, packed):
            done = []
            for f in range(fields):
                first = pl.multiple_of(f * per_field + m * 2 * rows, 2 * rows)
                both = load(pl.ds(first, 2 * rows))
                tiles_ref[pl.ds(first, 2 * rows), :] = both
                p = packed[f]
                for i in range(2):
                    p = note_edges(2 * m + i, both[i * rows : (i + 1) * rows], p)
                done.append(p)
            return tuple(done)

        packed = lax.fori_loop(0, levels // 2, body, no_tiles, unroll=4)
        for f in range(fields):
            lon_out[slot, f] = packed[f]
        pack_rows(tiles_ref, lat_out.at[slot])

    for copy in local:
        copy.wait()
    spread(lambda where: allb[vec, where, :].astype(F32), field, 0)
    field_edges = [edge_copies("f", t, t) for t in range(STEPS)]
    state_edges = [edge_copies("s", STEPS + t, t) for t in range(STEPS)]
    start_edges(field_edges[0])

    traj_copies[0].wait_recv()
    slices = {}
    passes = {}
    for t in range(STEPS):
        sel[t] = jnp.where(
            owner_ref[t] == vec,
            own_traj[own_half, :].astype(F32),
            sib_traj[own_half, :].astype(F32),
        ).astype(BF16)
        for d in range(1, pairs):
            slices[t, d] = remote(
                ("slice", t, d), sel.at[t], rcv.at[t, d - 1, own_half], partner(d)
            )
            passes[t, d] = remote(
                ("pass", t, d), rcv.at[t, d - 1, own_half], rcv.at[t, d - 1, own_half], to_sibling
            )
            slices[t, d].start()

    def pivots(level, carry):
        done = []
        for f in range(fields):
            above, ratio = carry[f]
            below = jnp.full((rows, lanes), diff_ref[f, level], F32)
            inv = 1.0 / (1.0 + below + above - above * ratio)
            coef[0, at(f, level), :] = inv
            coef[1, at(f, level), :] = above * inv
            coef[2, at(f, level), :] = below * inv
            done.append((below, below * inv))
        return tuple(done)

    zero = jnp.zeros((rows, lanes), F32)
    carry = lax.fori_loop(0, levels - 1, pivots, tuple((zero, zero) for _ in range(fields)))
    for f in range(fields):
        above, ratio = carry[f]
        inv = 1.0 / (1.0 + above - above * ratio)
        coef[0, at(f, levels - 1), :] = inv
        coef[1, at(f, levels - 1), :] = above * inv
        coef[2, at(f, levels - 1), :] = zero

    def take_state(t):
        for d in range(1, pairs):
            slices[t, d].wait_recv()
            passes[t, d].start()

    def build_state(t):
        for d in range(1, pairs):
            passes[t, d].wait_recv()
        holder = owner_ref[t] // 2
        mine = owner_ref[t] == vec

        def load_state(where):
            block = jnp.where(
                mine, own_traj[where, :].astype(F32), sib_traj[where, :].astype(F32)
            )
            for d in range(1, pairs):
                source = lax.rem(pair + pairs - d, pairs)
                block = jnp.where(holder == source, rcv[t, d - 1, where, :].astype(F32), block)
            return block

        spread(load_state, state.at[t], STEPS + t)
        start_edges(state_edges[t])

    def dlon(tile, mix, shift):
        mix = pltpu.roll(mix, shift, 1)
        after = jnp.where(lane == lanes - 1, mix, pltpu.roll(tile, lanes - 1, 1))
        before = jnp.where(lane == 0, mix, pltpu.roll(tile, 1, 1))
        return after - before

    def dlat(tile, slot, f, level):
        low = lat_rows[slot, 0, pl.ds(f * levels + level, 1), :]
        high = lat_rows[slot, 1, pl.ds(f * levels + level, 1), :]
        after = jnp.where(row == rows - 1, high, pltpu.roll(tile, rows - 1, 0))
        before = jnp.where(row == 0, low, pltpu.roll(tile, 1, 0))
        return after - before

    def step(t):
        fslot, sslot = t, STEPS + t

        def forward(level, solved):
            tiles = [field[at(f, level), :] for f in range(fields)]
            states = [state[t, at(f, level), :] for f in range(fields)]
            wind_u, wind_v = states[:2]
            pert_u, pert_v = tiles[:2]
            shift = lax.rem(lanes - 2 * level, lanes)
            done = []
            for f in range(fields):
                a, s = tiles[f], states[f]
                change = wind_u * dlon(a, lon_mix[fslot, f], shift)
                change += wind_v * dlat(a, fslot, f, level)
                change += pert_u * dlon(s, lon_mix[sslot, f], shift)
                change += pert_v * dlat(s, sslot, f, level)
                moved = a - (0.5 * COURANT) * change
                done.append(moved * coef[0, at(f, level), :] + solved[f] * coef[1, at(f, level), :])
            for f in range(fields):
                field[at(f, level), :] = done[f]
            return tuple(done)

        lax.fori_loop(0, levels, forward, no_tiles, unroll=8)
        if t + 1 < STEPS:
            take_state(t + 1)
        last = t == STEPS - 1

        def backward(k, carry):
            level = levels - 1 - k
            above, packed = carry
            done, edges = [], []
            for f in range(fields):
                x = field[at(f, level), :] + coef[2, at(f, level), :] * above[f]
                field[at(f, level), :] = x
                done.append(x)
                if not last:
                    edges.append(note_edges(level, x, packed[f]))
            return tuple(done), tuple(edges)

        _, packed = lax.fori_loop(0, levels, backward, (no_tiles, () if last else no_tiles), unroll=8)
        if not last:
            for f in range(fields):
                lon_out[t + 1, f] = packed[f]
            pack_rows(field, lat_wide.at[t])
            start_edges(field_edges[t + 1])

    def relay_field(f):
        for d in range(1, pairs):
            cross[f, d].wait_recv()
            relay[f, d].start()

    take_state(0)
    for d in range(1, pairs):
        for f in range(1, fields):
            cross[f, d].start()
    traj_copies[1].wait_recv()
    relayed = 0
    for t in range(STEPS):
        build_state(t)
        if t == STEPS - 1:
            while relayed < fields - 1:
                relay_field(relayed)
                relayed += 1
        await_edges(field_edges[t], t)
        await_edges(state_edges[t], STEPS + t)
        step(t)
    while relayed < fields:
        relay_field(relayed)
        relayed += 1
    basis_copy.wait_recv()

    total_rows = rows * lats
    total = float(fields * levels * total_rows * lanes * lons)
    row_ids = (lat * rows + row).astype(F32)
    cosine = jnp.cos((row_ids + 0.5) * (math.pi / total_rows) - math.pi / 2)

    def load_vector(i, f, m):
        first = pl.multiple_of(f * per_field + m * 2 * rows, 2 * rows)
        return allb[i, pl.ds(first, 2 * rows), :].astype(F32)

    acc = tuple(zero for _ in range(groups))
    for f in range(fields):
        for d in range(1, pairs):
            relay[f, d].wait_recv()
        scale = weight_ref[f] * cosine / total

        def gram(m, acc):
            acc = list(acc)
            low = field[at(f, 2 * m), :] * scale
            high = field[at(f, 2 * m + 1), :] * scale
            for i in range(groups):
                b = load_vector(i, f, m)
                acc[i] += b[:rows] * low + b[rows:] * high
            return tuple(acc)

        acc = lax.fori_loop(0, levels // 2, gram, acc, unroll=8)
    part = jnp.zeros((8, lanes), F32)
    part_row = lax.broadcasted_iota(jnp.int32, (8, lanes), 0)
    for i in range(groups):
        part = jnp.where(part_row == i, jnp.sum(acc[i], axis=0, keepdims=True), part)
    sums[me] = part
    sum_copies = []
    for k in range(1, tiles):
        copy = remote(("sum", k), sums.at[me], sums.at[me], other_tile(k))
        copy.start()
        sum_copies.append(copy)
    for copy in sum_copies:
        copy.wait_recv()
    whole = sums[0]
    for k in range(1, tiles):
        whole += sums[k]
    column = jnp.sum(whole, axis=1, keepdims=True)
    cols[vec] = jnp.broadcast_to(column, (8, lanes))
    col_copies = []
    for k in range(1, groups):
        copy = remote(("col", k), cols.at[vec], cols.at[vec], other_vec(k))
        copy.start()
        col_copies.append(copy)
    factor = [jnp.broadcast_to(column[i : i + 1], (rows, lanes)) for i in range(groups)]

    def residual(m, carry):
        for f in range(fields):
            low, high = field[at(f, 2 * m), :], field[at(f, 2 * m + 1), :]
            for i in range(groups):
                b = load_vector(i, f, m)
                low -= b[:rows] * factor[i]
                high -= b[rows:] * factor[i]
            out_ref[f, 2 * m] = low
            out_ref[f, 2 * m + 1] = high
        return carry

    lax.fori_loop(0, levels // 2, residual, 0, unroll=4)
    for copy in col_copies:
        copy.wait_recv()
    table = jnp.zeros((8, lanes), F32)
    wide_lane = lax.broadcasted_iota(jnp.int32, (8, lanes), 1)
    for j in range(groups):
        table = jnp.where(wide_lane == j, cols[j], table)
    coup_ref[...] = table[:groups, :groups]

    for copy in traj_copies:
        copy.wait_send()
    basis_copy.wait_send()
    for d in range(1, pairs):
        for f in range(fields):
            cross[f, d].wait_send()
            relay[f, d].wait_send()
        for t in range(STEPS):
            slices[t, d].wait_send()
            passes[t, d].wait_send()
    for t in range(STEPS):
        await_edges_sent(field_edges[t])
        await_edges_sent(state_edges[t])
    for copy in sum_copies + col_copies:
        copy.wait_send()


def solution(mesh):
    groups, lats, lons = mesh.shape["vec"], mesh.shape["lat"], mesh.shape["lon"]

    def per_device(basis, trajectory, slice_owner, diffusion, energy_weight):
        _, fields, levels, rows, lanes = basis.shape
        size = fields * levels * rows
        pairs, tiles = groups // 2, lats * lons
        ids = copy_names(pairs, tiles, groups, fields)
        slots = 2 * STEPS
        vmem = pl.BlockSpec(memory_space=pltpu.VMEM)
        hbm = pl.BlockSpec(memory_space=pltpu.HBM)
        residual_block, coupling = pl.pallas_call(
            functools.partial(kernel, (fields, levels, rows, lanes), (groups, lats, lons), ids),
            out_shape=(
                jax.ShapeDtypeStruct((fields, levels, rows, lanes), F32),
                jax.ShapeDtypeStruct((groups, groups), F32),
            ),
            in_specs=[hbm] * 5,
            out_specs=(vmem, vmem),
            scratch_shapes=[
                pltpu.SMEM(slice_owner.shape, jnp.int32),
                pltpu.SMEM(diffusion.shape, F32),
                pltpu.SMEM(energy_weight.shape, F32),
                pltpu.VMEM((size, lanes), BF16),
                pltpu.VMEM((size, lanes), BF16),
                pltpu.VMEM((STEPS, size // 2, lanes), BF16),
                pltpu.VMEM((STEPS, max(pairs - 1, 1), size, lanes), BF16),
                pltpu.VMEM((groups, size, lanes), BF16),
                pltpu.VMEM((size, lanes), F32),
                pltpu.VMEM((STEPS, size, lanes), F32),
                pltpu.VMEM((3, size, lanes), F32),
                pltpu.VMEM((slots, fields, rows, lanes), F32),
                pltpu.VMEM((slots, 2, fields, rows, lanes), F32),
                pltpu.VMEM((slots, 2, fields * levels, lanes), BF16),
                pltpu.VMEM((slots, 2, fields * levels, lanes), BF16),
                pltpu.VMEM((STEPS - 1, 2, fields * levels, lanes), F32),
                pltpu.VMEM((slots, fields, rows, lanes), F32),
                pltpu.VMEM((slots, 2, fields * levels, lanes), F32),
                pltpu.VMEM((tiles, 8, lanes), F32),
                pltpu.VMEM((groups, 8, lanes), F32),
                pltpu.SemaphoreType.DMA((5,)),
                pltpu.SemaphoreType.DMA((len(ids),)),
                pltpu.SemaphoreType.DMA((len(ids),)),
            ],
            compiler_params=pltpu.CompilerParams(
                collective_id=0, has_side_effects=True, vmem_limit_bytes=48 * 1024 * 1024
            ),
        )(
            basis.reshape(size, lanes),
            trajectory.reshape(size, lanes),
            slice_owner,
            diffusion,
            energy_weight,
        )
        return residual_block[None], coupling

    return jax.shard_map(
        per_device,
        mesh=mesh,
        in_specs=(
            P("vec", None, None, "lat", "lon"),
            P("vec", None, None, "lat", "lon"),
            P(),
            P(),
            P(),
        ),
        out_specs=(P("vec", None, None, "lat", "lon"), P()),
        check_vma=False,
    )
```

```python
import functools
import math

import jax
import jax.numpy as jnp
from jax import lax
from jax.experimental import pallas as pl
from jax.experimental.pallas import tpu as pltpu
from jax.sharding import PartitionSpec as P

STEPS = 2
COURANT = 0.25
MESH = pl.DeviceIdType.MESH
F32 = jnp.float32
BF16 = jnp.bfloat16


def copy_names(pairs, tiles, groups, fields):
    names = [("traj", 0), ("traj", 1), "basis"]
    for d in range(1, pairs):
        names += [(kind, k, d) for kind in ("cross", "relay") for k in range(fields)]
        names += [(kind, t, d) for kind in ("slice", "pass") for t in range(STEPS)]
    for t in range(STEPS):
        names += [(kind, t, s) for kind in ("flon", "flat", "slon", "slat") for s in range(2)]
    names += [("sum", k) for k in range(1, tiles)]
    names += [("col", k) for k in range(1, groups)]
    return {name: i for i, name in enumerate(names)}


def kernel(
    shape,
    counts,
    ids,
    basis_ref,
    traj_ref,
    owner_in,
    diff_in,
    weight_in,
    out_ref,
    coup_ref,
    owner_ref,
    diff_ref,
    weight_ref,
    own_traj,
    sib_traj,
    sel,
    rcv,
    allb,
    field,
    state,
    coef,
    lon_out,
    lon_in,
    lat_out,
    lat_in,
    lon_mix,
    lat_rows,
    sums,
    cols,
    local_sem,
    send_sem,
    recv_sem,
):
    fields, levels, rows, lanes = shape
    groups, lats, lons = counts
    pairs, tiles = groups // 2, lats * lons
    size = fields * levels * rows
    per_field = levels * rows
    half = size // 2
    vec = lax.axis_index("vec")
    lat = lax.axis_index("lat")
    lon = lax.axis_index("lon")
    core = lax.rem(vec, 2)
    pair = vec // 2
    sibling = vec + 1 - 2 * core
    me = lat * lons + lon

    def other_tile(k):
        index = lax.rem(me + k, tiles)
        return {"lat": index // lons, "lon": lax.rem(index, lons)}

    def other_vec(k):
        return {"vec": lax.rem(vec + k, groups)}

    def partner(d):
        return {"vec": 2 * lax.rem(pair + d, pairs) + core}

    def remote(name, src, dst, device):
        return pltpu.make_async_remote_copy(
            src_ref=src,
            dst_ref=dst,
            send_sem=send_sem.at[ids[name]],
            recv_sem=recv_sem.at[ids[name]],
            device_id=device,
            device_id_type=MESH,
        )

    local = [
        pltpu.make_async_copy(source, target, local_sem.at[i])
        for i, (source, target) in enumerate(
            (
                (basis_ref, allb.at[vec]),
                (traj_ref, own_traj),
                (owner_in, owner_ref),
                (diff_in, diff_ref),
                (weight_in, weight_ref),
            )
        )
    ]
    for copy in local:
        copy.start()

    barrier = pltpu.get_barrier_semaphore()
    for k in range(1, tiles):
        pl.semaphore_signal(barrier, inc=1, device_id=other_tile(k), device_id_type=MESH)
    for k in range(1, groups):
        pl.semaphore_signal(barrier, inc=1, device_id=other_vec(k), device_id_type=MESH)
    pl.semaphore_wait(barrier, tiles + groups - 2)

    to_sibling = {"vec": sibling}
    own_half = pl.ds(pl.multiple_of(core * half, 16), half)
    far_half = pl.ds(pl.multiple_of((1 - core) * half, 16), half)

    traj_copies = [
        remote(("traj", i), traj_ref.at[part], sib_traj.at[part], to_sibling)
        for i, part in enumerate((far_half, own_half))
    ]
    traj_copies[0].start()
    cross = {}
    relay = {}
    for d in range(1, pairs):
        source = 2 * lax.rem(pair + pairs - d, pairs) + core
        for f in range(fields):
            chunk = pl.ds(f * per_field, per_field)
            cross[f, d] = remote(
                ("cross", f, d), basis_ref.at[chunk], allb.at[vec, chunk], partner(d)
            )
            relay[f, d] = remote(
                ("relay", f, d), allb.at[source, chunk], allb.at[source, chunk], to_sibling
            )
    for d in range(1, pairs):
        cross[0, d].start()
    traj_copies[1].start()
    basis_copy = remote("basis", basis_ref, allb.at[vec], to_sibling)
    basis_copy.start()

    lane = lax.broadcasted_iota(jnp.int32, (rows, lanes), 1)
    row = lax.broadcasted_iota(jnp.int32, (rows, lanes), 0)

    def edge_copies(kind, slot, t):
        east = {"lon": lax.rem(lon + 1, lons)}
        west = {"lon": lax.rem(lon + lons - 1, lons)}
        up = {"lat": lax.rem(lat + 1, lats)}
        down = {"lat": lax.rem(lat + lats - 1, lats)}
        source, target = lat_out.at[slot], lat_in.at[slot]
        return (
            remote((kind + "lon", t, 0), lon_out.at[slot], lon_in.at[slot, 0], east),
            remote((kind + "lon", t, 1), lon_out.at[slot], lon_in.at[slot, 1], west),
            remote((kind + "lat", t, 0), source.at[1], target.at[0], up),
            remote((kind + "lat", t, 1), source.at[0], target.at[1], down),
        )

    def start_edges(copies):
        copies[0].start()
        copies[1].start()

        @pl.when(lat < lats - 1)
        def _():
            copies[2].start()

        @pl.when(lat > 0)
        def _():
            copies[3].start()

    def await_edges(copies, slot):
        copies[0].wait_recv()
        copies[1].wait_recv()

        def settle(copy, side, present):
            @pl.when(present)
            def _():
                copy.wait_recv()
                lat_rows[slot, side] = lat_in[slot, side].astype(F32)

            @pl.when(jnp.logical_not(present))
            def _():
                lat_rows[slot, side] = jnp.zeros((fields * levels, lanes), F32)

        settle(copies[2], 0, lat > 0)
        settle(copies[3], 1, lat < lats - 1)

        for f in range(fields):
            lon_mix[slot, f] = jnp.where(
                lax.rem(lane, 2) == 0,
                pltpu.roll(lon_in[slot, 0, f], 1, 1),
                pltpu.roll(lon_in[slot, 1, f], lanes - 1, 1),
            )

    def await_edges_sent(copies):
        copies[0].wait_send()
        copies[1].wait_send()

        @pl.when(lat < lats - 1)
        def _():
            copies[2].wait_send()

        @pl.when(lat > 0)
        def _():
            copies[3].wait_send()

    def at(f, level):
        return pl.ds(pl.multiple_of(f * per_field + level * rows, rows), rows)

    def note_edges(level, tile, packed):
        spot = 2 * level
        here = (lane == spot) | (lane == lax.rem(spot + lanes - 1, lanes))
        return jnp.where(here, pltpu.roll(tile, spot, 1), packed)

    def pack_rows(tiles_ref, target):
        for f in range(fields):
            for side in range(2):
                first = f * per_field + side * (rows - 1)
                edge = tiles_ref[pl.ds(first, levels, stride=rows), :]
                target[side, f * levels : (f + 1) * levels, :] = edge.astype(target.dtype)

    no_tiles = tuple(jnp.zeros((rows, lanes), F32) for _ in range(fields))

    def spread(load, tiles_ref, slot):
        def body(m, packed):
            done = []
            for f in range(fields):
                first = pl.multiple_of(f * per_field + m * 2 * rows, 2 * rows)
                both = load(pl.ds(first, 2 * rows))
                tiles_ref[pl.ds(first, 2 * rows), :] = both
                p = packed[f]
                for i in range(2):
                    p = note_edges(2 * m + i, both[i * rows : (i + 1) * rows], p)
                done.append(p)
            return tuple(done)

        packed = lax.fori_loop(0, levels // 2, body, no_tiles, unroll=4)
        for f in range(fields):
            lon_out[slot, f] = packed[f]
        pack_rows(tiles_ref, lat_out.at[slot])

    for copy in local:
        copy.wait()
    traj_copies[0].wait_recv()
    slices = {}
    passes = {}
    for t in range(STEPS):
        sel[t] = jnp.where(
            owner_ref[t] == vec,
            own_traj[own_half, :].astype(F32),
            sib_traj[own_half, :].astype(F32),
        ).astype(BF16)
        for d in range(1, pairs):
            slices[t, d] = remote(
                ("slice", t, d), sel.at[t], rcv.at[t, d - 1, own_half], partner(d)
            )
            passes[t, d] = remote(
                ("pass", t, d), rcv.at[t, d - 1, own_half], rcv.at[t, d - 1, own_half], to_sibling
            )
        if t == 0:
            for d in range(1, pairs):
                slices[t, d].start()

    spread(lambda where: allb[vec, where, :].astype(F32), field, 0)
    field_edges = [edge_copies("f", t, t) for t in range(STEPS)]
    state_edges = [edge_copies("s", STEPS + t, t) for t in range(STEPS)]
    start_edges(field_edges[0])

    def pivots(level, carry):
        done = []
        for f in range(fields):
            above, ratio = carry[f]
            below = jnp.full((rows, lanes), diff_ref[f, level], F32)
            inv = 1.0 / (1.0 + below + above - above * ratio)
            coef[0, at(f, level), :] = inv
            coef[1, at(f, level), :] = above * inv
            coef[2, at(f, level), :] = below * inv
            done.append((below, below * inv))
        return tuple(done)

    zero = jnp.zeros((rows, lanes), F32)
    carry = lax.fori_loop(0, levels - 1, pivots, tuple((zero, zero) for _ in range(fields)))
    for f in range(fields):
        above, ratio = carry[f]
        inv = 1.0 / (1.0 + above - above * ratio)
        coef[0, at(f, levels - 1), :] = inv
        coef[1, at(f, levels - 1), :] = above * inv
        coef[2, at(f, levels - 1), :] = zero

    def take_state(t):
        for d in range(1, pairs):
            slices[t, d].wait_recv()
            if t + 1 < STEPS:
                slices[t + 1, d].start()
            passes[t, d].start()

    def build_state(t):
        for d in range(1, pairs):
            passes[t, d].wait_recv()
        holder = owner_ref[t] // 2
        mine = owner_ref[t] == vec

        def load_state(where):
            block = jnp.where(
                mine, own_traj[where, :].astype(F32), sib_traj[where, :].astype(F32)
            )
            for d in range(1, pairs):
                source = lax.rem(pair + pairs - d, pairs)
                block = jnp.where(holder == source, rcv[t, d - 1, where, :].astype(F32), block)
            return block

        spread(load_state, state.at[t], STEPS + t)
        start_edges(state_edges[t])

    def dlon(tile, mix, shift):
        mix = pltpu.roll(mix, shift, 1)
        after = jnp.where(lane == lanes - 1, mix, pltpu.roll(tile, lanes - 1, 1))
        before = jnp.where(lane == 0, mix, pltpu.roll(tile, 1, 1))
        return after - before

    def dlat(tile, slot, f, level):
        low = lat_rows[slot, 0, pl.ds(f * levels + level, 1), :]
        high = lat_rows[slot, 1, pl.ds(f * levels + level, 1), :]
        after = jnp.where(row == rows - 1, high, pltpu.roll(tile, rows - 1, 0))
        before = jnp.where(row == 0, low, pltpu.roll(tile, 1, 0))
        return after - before

    def step(t):
        fslot, sslot = t, STEPS + t

        def forward(level, solved):
            tiles = [field[at(f, level), :] for f in range(fields)]
            states = [state[t, at(f, level), :] for f in range(fields)]
            wind_u, wind_v = states[:2]
            pert_u, pert_v = tiles[:2]
            shift = lax.rem(lanes - 2 * level, lanes)
            done = []
            for f in range(fields):
                a, s = tiles[f], states[f]
                change = wind_u * dlon(a, lon_mix[fslot, f], shift)
                change += wind_v * dlat(a, fslot, f, level)
                change += pert_u * dlon(s, lon_mix[sslot, f], shift)
                change += pert_v * dlat(s, sslot, f, level)
                moved = a - (0.5 * COURANT) * change
                done.append(moved * coef[0, at(f, level), :] + solved[f] * coef[1, at(f, level), :])
            for f in range(fields):
                field[at(f, level), :] = done[f]
            return tuple(done)

        lax.fori_loop(0, levels, forward, no_tiles, unroll=8)
        if t + 1 < STEPS:
            take_state(t + 1)
        last = t == STEPS - 1

        def backward(k, carry):
            level = levels - 1 - k
            above, packed = carry
            done, edges = [], []
            for f in range(fields):
                x = field[at(f, level), :] + coef[2, at(f, level), :] * above[f]
                field[at(f, level), :] = x
                done.append(x)
                if not last:
                    edges.append(note_edges(level, x, packed[f]))
            return tuple(done), tuple(edges)

        _, packed = lax.fori_loop(0, levels, backward, (no_tiles, () if last else no_tiles), unroll=8)
        if not last:
            for f in range(fields):
                lon_out[t + 1, f] = packed[f]
            pack_rows(field, lat_out.at[t + 1])
            start_edges(field_edges[t + 1])

    def relay_field(f):
        for d in range(1, pairs):
            cross[f, d].wait_recv()
            relay[f, d].start()

    take_state(0)
    traj_copies[1].wait_recv()
    relayed = 0
    for t in range(STEPS):
        build_state(t)
        if t == 0:
            for d in range(1, pairs):
                for f in range(1, fields):
                    cross[f, d].start()
        if t == STEPS - 1:
            while relayed < fields - 1:
                relay_field(relayed)
                relayed += 1
        await_edges(field_edges[t], t)
        await_edges(state_edges[t], STEPS + t)
        step(t)
    while relayed < fields:
        relay_field(relayed)
        relayed += 1
    basis_copy.wait_recv()

    total_rows = rows * lats
    total = float(fields * levels * total_rows * lanes * lons)
    row_ids = (lat * rows + row).astype(F32)
    cosine = jnp.cos((row_ids + 0.5) * (math.pi / total_rows) - math.pi / 2)

    def load_vector(i, f, m):
        first = pl.multiple_of(f * per_field + m * 2 * rows, 2 * rows)
        return allb[i, pl.ds(first, 2 * rows), :].astype(F32)

    acc = tuple(zero for _ in range(groups))
    for f in range(fields):
        for d in range(1, pairs):
            relay[f, d].wait_recv()
        scale = weight_ref[f] * cosine / total

        def gram(m, acc):
            acc = list(acc)
            low = field[at(f, 2 * m), :] * scale
            high = field[at(f, 2 * m + 1), :] * scale
            for i in range(groups):
                b = load_vector(i, f, m)
                acc[i] += b[:rows] * low + b[rows:] * high
            return tuple(acc)

        acc = lax.fori_loop(0, levels // 2, gram, acc, unroll=8)
    part = jnp.zeros((8, lanes), F32)
    part_row = lax.broadcasted_iota(jnp.int32, (8, lanes), 0)
    for i in range(groups):
        part = jnp.where(part_row == i, jnp.sum(acc[i], axis=0, keepdims=True), part)
    sums[me] = part
    sum_copies = []
    for k in range(1, tiles):
        copy = remote(("sum", k), sums.at[me], sums.at[me], other_tile(k))
        copy.start()
        sum_copies.append(copy)
    for copy in sum_copies:
        copy.wait_recv()
    whole = sums[0]
    for k in range(1, tiles):
        whole += sums[k]
    column = jnp.sum(whole, axis=1, keepdims=True)
    cols[vec] = jnp.broadcast_to(column, (8, lanes))
    col_copies = []
    for k in range(1, groups):
        copy = remote(("col", k), cols.at[vec], cols.at[vec], other_vec(k))
        copy.start()
        col_copies.append(copy)
    factor = [jnp.broadcast_to(column[i : i + 1], (rows, lanes)) for i in range(groups)]

    out_copies = []
    for f in range(fields):

        def residual(m, carry):
            low, high = field[at(f, 2 * m), :], field[at(f, 2 * m + 1), :]
            for i in range(groups):
                b = load_vector(i, f, m)
                low -= b[:rows] * factor[i]
                high -= b[rows:] * factor[i]
            field[at(f, 2 * m), :] = low
            field[at(f, 2 * m + 1), :] = high
            return carry

        lax.fori_loop(0, levels // 2, residual, 0, unroll=8)
        chunk = pl.ds(f * per_field, per_field)
        copy = pltpu.make_async_copy(field.at[chunk], out_ref.at[chunk], local_sem.at[5 + f])
        copy.start()
        out_copies.append(copy)

    for copy in col_copies:
        copy.wait_recv()
    table = jnp.zeros((8, lanes), F32)
    wide_lane = lax.broadcasted_iota(jnp.int32, (8, lanes), 1)
    for j in range(groups):
        table = jnp.where(wide_lane == j, cols[j], table)
    coup_ref[...] = table[:groups, :groups]

    for copy in out_copies:
        copy.wait()
    for copy in traj_copies:
        copy.wait_send()
    basis_copy.wait_send()
    for d in range(1, pairs):
        for f in range(fields):
            cross[f, d].wait_send()
            relay[f, d].wait_send()
        for t in range(STEPS):
            slices[t, d].wait_send()
            passes[t, d].wait_send()
    for t in range(STEPS):
        await_edges_sent(field_edges[t])
        await_edges_sent(state_edges[t])
    for copy in sum_copies + col_copies:
        copy.wait_send()


def solution(mesh):
    groups, lats, lons = mesh.shape["vec"], mesh.shape["lat"], mesh.shape["lon"]

    def per_device(basis, trajectory, slice_owner, diffusion, energy_weight):
        _, fields, levels, rows, lanes = basis.shape
        size = fields * levels * rows
        pairs, tiles = groups // 2, lats * lons
        ids = copy_names(pairs, tiles, groups, fields)
        slots = 2 * STEPS
        vmem = pl.BlockSpec(memory_space=pltpu.VMEM)
        hbm = pl.BlockSpec(memory_space=pltpu.HBM)
        residual_block, coupling = pl.pallas_call(
            functools.partial(kernel, (fields, levels, rows, lanes), (groups, lats, lons), ids),
            out_shape=(
                jax.ShapeDtypeStruct((size, lanes), F32),
                jax.ShapeDtypeStruct((groups, groups), F32),
            ),
            in_specs=[hbm] * 5,
            out_specs=(hbm, vmem),
            scratch_shapes=[
                pltpu.SMEM(slice_owner.shape, jnp.int32),
                pltpu.SMEM(diffusion.shape, F32),
                pltpu.SMEM(energy_weight.shape, F32),
                pltpu.VMEM((size, lanes), BF16),
                pltpu.VMEM((size, lanes), BF16),
                pltpu.VMEM((STEPS, size // 2, lanes), BF16),
                pltpu.VMEM((STEPS, max(pairs - 1, 1), size, lanes), BF16),
                pltpu.VMEM((groups, size, lanes), BF16),
                pltpu.VMEM((size, lanes), F32),
                pltpu.VMEM((STEPS, size, lanes), F32),
                pltpu.VMEM((3, size, lanes), F32),
                pltpu.VMEM((slots, fields, rows, lanes), F32),
                pltpu.VMEM((slots, 2, fields, rows, lanes), F32),
                pltpu.VMEM((slots, 2, fields * levels, lanes), BF16),
                pltpu.VMEM((slots, 2, fields * levels, lanes), BF16),
                pltpu.VMEM((slots, fields, rows, lanes), F32),
                pltpu.VMEM((slots, 2, fields * levels, lanes), F32),
                pltpu.VMEM((tiles, 8, lanes), F32),
                pltpu.VMEM((groups, 8, lanes), F32),
                pltpu.SemaphoreType.DMA((5 + fields,)),
                pltpu.SemaphoreType.DMA((len(ids),)),
                pltpu.SemaphoreType.DMA((len(ids),)),
            ],
            compiler_params=pltpu.CompilerParams(
                collective_id=0, has_side_effects=True, vmem_limit_bytes=60 * 1024 * 1024
            ),
        )(
            basis.reshape(size, lanes),
            trajectory.reshape(size, lanes),
            slice_owner,
            diffusion,
            energy_weight,
        )
        return residual_block.reshape(basis.shape), coupling

    return jax.shard_map(
        per_device,
        mesh=mesh,
        in_specs=(
            P("vec", None, None, "lat", "lon"),
            P("vec", None, None, "lat", "lon"),
            P(),
            P(),
            P(),
        ),
        out_specs=(P("vec", None, None, "lat", "lon"), P()),
        check_vma=False,
    )
```

```python
import functools
import math

import jax
import jax.numpy as jnp
from jax import lax
from jax.experimental import pallas as pl
from jax.experimental.pallas import tpu as pltpu
from jax.sharding import PartitionSpec as P

STEPS = 2
PIECES = 2
CHUNKS = 4
COURANT = 0.25
MESH = pl.DeviceIdType.MESH
F32 = jnp.float32
BF16 = jnp.bfloat16


def copy_names(pairs, tiles, groups, fields):
    names = [("traj", 0), ("traj", 1), "basis"]
    for d in range(1, pairs):
        names += [(kind, k, d) for kind in ("cross", "relay") for k in range(fields)]
        names += [
            (kind, t, d, i) for kind in ("slice", "pass") for t in range(STEPS) for i in range(PIECES)
        ]
    for t in range(STEPS):
        names += [(kind, t, s) for kind in ("flon", "flat", "slon", "slat") for s in range(2)]
    names += [("sum", k) for k in range(1, tiles)]
    names += [("col", k) for k in range(1, groups)]
    return {name: i for i, name in enumerate(names)}


def kernel(
    shape,
    counts,
    ids,
    basis_ref,
    traj_ref,
    owner_in,
    diff_in,
    weight_in,
    out_ref,
    coup_ref,
    owner_ref,
    diff_ref,
    weight_ref,
    own_traj,
    sib_traj,
    sel,
    rcv,
    allb,
    field,
    state,
    moved,
    coef,
    lon_out,
    lon_in,
    lat_out,
    lat_in,
    lon_mix,
    lat_rows,
    sums,
    cols,
    local_sem,
    send_sem,
    recv_sem,
):
    fields, levels, rows, lanes = shape
    groups, lats, lons = counts
    pairs, tiles = groups // 2, lats * lons
    size = fields * levels * rows
    per_field = levels * rows
    half = size // 2
    piece = half // PIECES
    vec = lax.axis_index("vec")
    lat = lax.axis_index("lat")
    lon = lax.axis_index("lon")
    core = lax.rem(vec, 2)
    pair = vec // 2
    sibling = vec + 1 - 2 * core
    me = lat * lons + lon

    def other_tile(k):
        index = lax.rem(me + k, tiles)
        return {"lat": index // lons, "lon": lax.rem(index, lons)}

    def other_vec(k):
        return {"vec": lax.rem(vec + k, groups)}

    def partner(d):
        return {"vec": 2 * lax.rem(pair + d, pairs) + core}

    def remote(name, src, dst, device):
        return pltpu.make_async_remote_copy(
            src_ref=src,
            dst_ref=dst,
            send_sem=send_sem.at[ids[name]],
            recv_sem=recv_sem.at[ids[name]],
            device_id=device,
            device_id_type=MESH,
        )

    local = [
        pltpu.make_async_copy(source, target, local_sem.at[i])
        for i, (source, target) in enumerate(
            (
                (basis_ref, allb.at[vec]),
                (traj_ref, own_traj),
                (owner_in, owner_ref),
                (diff_in, diff_ref),
                (weight_in, weight_ref),
            )
        )
    ]
    for copy in local:
        copy.start()

    barrier = pltpu.get_barrier_semaphore()
    for k in range(1, tiles):
        pl.semaphore_signal(barrier, inc=1, device_id=other_tile(k), device_id_type=MESH)
    for k in range(1, groups):
        pl.semaphore_signal(barrier, inc=1, device_id=other_vec(k), device_id_type=MESH)
    pl.semaphore_wait(barrier, tiles + groups - 2)

    to_sibling = {"vec": sibling}
    own_half = pl.ds(pl.multiple_of(core * half, 16), half)
    far_half = pl.ds(pl.multiple_of((1 - core) * half, 16), half)

    traj_copies = [
        remote(("traj", i), traj_ref.at[part], sib_traj.at[part], to_sibling)
        for i, part in enumerate((far_half, own_half))
    ]
    traj_copies[0].start()
    cross = {}
    relay = {}
    for d in range(1, pairs):
        source = 2 * lax.rem(pair + pairs - d, pairs) + core
        for f in range(fields):
            chunk = pl.ds(f * per_field, per_field)
            cross[f, d] = remote(
                ("cross", f, d), basis_ref.at[chunk], allb.at[vec, chunk], partner(d)
            )
            relay[f, d] = remote(
                ("relay", f, d), allb.at[source, chunk], allb.at[source, chunk], to_sibling
            )
    for d in range(1, pairs):
        cross[0, d].start()
    traj_copies[1].start()
    basis_copy = remote("basis", basis_ref, allb.at[vec], to_sibling)
    basis_copy.start()

    lane = lax.broadcasted_iota(jnp.int32, (rows, lanes), 1)
    row = lax.broadcasted_iota(jnp.int32, (rows, lanes), 0)

    def edge_copies(kind, slot, t):
        east = {"lon": lax.rem(lon + 1, lons)}
        west = {"lon": lax.rem(lon + lons - 1, lons)}
        up = {"lat": lax.rem(lat + 1, lats)}
        down = {"lat": lax.rem(lat + lats - 1, lats)}
        source, target = lat_out.at[slot], lat_in.at[slot]
        return (
            remote((kind + "lon", t, 0), lon_out.at[slot], lon_in.at[slot, 0], east),
            remote((kind + "lon", t, 1), lon_out.at[slot], lon_in.at[slot, 1], west),
            remote((kind + "lat", t, 0), source.at[1], target.at[0], up),
            remote((kind + "lat", t, 1), source.at[0], target.at[1], down),
        )

    def start_edges(copies):
        copies[0].start()
        copies[1].start()

        @pl.when(lat < lats - 1)
        def _():
            copies[2].start()

        @pl.when(lat > 0)
        def _():
            copies[3].start()

    def await_edges(copies, slot):
        copies[0].wait_recv()
        copies[1].wait_recv()

        def settle(copy, side, present):
            @pl.when(present)
            def _():
                copy.wait_recv()
                lat_rows[slot, side] = lat_in[slot, side].astype(F32)

            @pl.when(jnp.logical_not(present))
            def _():
                lat_rows[slot, side] = jnp.zeros((fields * levels, lanes), F32)

        settle(copies[2], 0, lat > 0)
        settle(copies[3], 1, lat < lats - 1)

        for f in range(fields):
            lon_mix[slot, f] = jnp.where(
                lax.rem(lane, 2) == 0,
                pltpu.roll(lon_in[slot, 0, f], 1, 1),
                pltpu.roll(lon_in[slot, 1, f], lanes - 1, 1),
            )

    def await_edges_sent(copies):
        copies[0].wait_send()
        copies[1].wait_send()

        @pl.when(lat < lats - 1)
        def _():
            copies[2].wait_send()

        @pl.when(lat > 0)
        def _():
            copies[3].wait_send()

    def at(f, level):
        return pl.ds(pl.multiple_of(f * per_field + level * rows, rows), rows)

    def note_edges(level, tile, packed):
        spot = 2 * level
        here = (lane == spot) | (lane == lax.rem(spot + lanes - 1, lanes))
        return jnp.where(here, pltpu.roll(tile, spot, 1), packed)

    def pack_rows(tiles_ref, target):
        for f in range(fields):
            for side in range(2):
                first = f * per_field + side * (rows - 1)
                edge = tiles_ref[pl.ds(first, levels, stride=rows), :]
                target[side, f * levels : (f + 1) * levels, :] = edge.astype(target.dtype)

    no_tiles = tuple(jnp.zeros((rows, lanes), F32) for _ in range(fields))

    def spread(load, tiles_ref, slot):
        def body(m, packed):
            done = []
            for f in range(fields):
                first = pl.multiple_of(f * per_field + m * 2 * rows, 2 * rows)
                both = load(pl.ds(first, 2 * rows))
                tiles_ref[pl.ds(first, 2 * rows), :] = both
                p = packed[f]
                for i in range(2):
                    p = note_edges(2 * m + i, both[i * rows : (i + 1) * rows], p)
                done.append(p)
            return tuple(done)

        packed = lax.fori_loop(0, levels // 2, body, no_tiles, unroll=4)
        for f in range(fields):
            lon_out[slot, f] = packed[f]
        pack_rows(tiles_ref, lat_out.at[slot])

    for copy in local:
        copy.wait()
    traj_copies[0].wait_recv()
    slices = {}
    passes = {}
    for t in range(STEPS):
        sel[t] = jnp.where(
            owner_ref[t] == vec,
            own_traj[own_half, :].astype(F32),
            sib_traj[own_half, :].astype(F32),
        ).astype(BF16)
        for d in range(1, pairs):
            for i in range(PIECES):
                first = pl.multiple_of(core * half + i * piece, 16)
                there = rcv.at[t, d - 1, pl.ds(first, piece)]
                slices[t, d, i] = remote(
                    ("slice", t, d, i), sel.at[t, pl.ds(i * piece, piece)], there, partner(d)
                )
                passes[t, d, i] = remote(("pass", t, d, i), there, there, to_sibling)
                if t == 0:
                    slices[t, d, i].start()

    spread(lambda where: allb[vec, where, :].astype(F32), field, 0)
    field_edges = [edge_copies("f", t, t) for t in range(STEPS)]
    state_edges = [edge_copies("s", STEPS + t, t) for t in range(STEPS)]
    start_edges(field_edges[0])

    def pivots(level, carry):
        done = []
        for f in range(fields):
            above, ratio = carry[f]
            below = jnp.full((rows, lanes), diff_ref[f, level], F32)
            inv = 1.0 / (1.0 + below + above - above * ratio)
            coef[0, at(f, level), :] = inv
            coef[1, at(f, level), :] = above * inv
            coef[2, at(f, level), :] = below * inv
            done.append((below, below * inv))
        return tuple(done)

    zero = jnp.zeros((rows, lanes), F32)
    carry = lax.fori_loop(0, levels - 1, pivots, tuple((zero, zero) for _ in range(fields)))
    for f in range(fields):
        above, ratio = carry[f]
        inv = 1.0 / (1.0 + above - above * ratio)
        coef[0, at(f, levels - 1), :] = inv
        coef[1, at(f, levels - 1), :] = above * inv
        coef[2, at(f, levels - 1), :] = zero

    every = [(d, i) for i in range(PIECES) for d in range(1, pairs)]

    def take_state(t):
        for d, i in every:
            slices[t, d, i].wait_recv()
            passes[t, d, i].start()
        if t + 1 < STEPS:
            for d, i in every:
                slices[t + 1, d, i].start()

    def build_state(t):
        for d, i in every:
            passes[t, d, i].wait_recv()
        holder = owner_ref[t] // 2
        mine = owner_ref[t] == vec

        def load_state(where):
            block = jnp.where(
                mine, own_traj[where, :].astype(F32), sib_traj[where, :].astype(F32)
            )
            for d in range(1, pairs):
                source = lax.rem(pair + pairs - d, pairs)
                block = jnp.where(holder == source, rcv[t, d - 1, where, :].astype(F32), block)
            return block

        spread(load_state, state.at[t], STEPS + t)
        start_edges(state_edges[t])

    def dlon(tile):
        after = jnp.where(lane == lanes - 1, 0.0, pltpu.roll(tile, lanes - 1, 1))
        return after - jnp.where(lane == 0, 0.0, pltpu.roll(tile, 1, 1))

    def dlat(tile):
        after = jnp.where(row == rows - 1, 0.0, pltpu.roll(tile, rows - 1, 0))
        return after - jnp.where(row == 0, 0.0, pltpu.roll(tile, 1, 0))

    lon_sign = jnp.where(lane == lanes - 1, 1.0, jnp.where(lane == 0, -1.0, 0.0))
    lat_sign = jnp.where(row == rows - 1, 1.0, jnp.where(row == 0, -1.0, 0.0))
    weight = 0.5 * COURANT

    def interior(t):
        def body(level, carry):
            tiles = [field[at(f, level), :] for f in range(fields)]
            states = [state[t, at(f, level), :] for f in range(fields)]
            for f in range(fields):
                change = states[0] * dlon(tiles[f]) + states[1] * dlat(tiles[f])
                change += tiles[0] * dlon(states[f]) + tiles[1] * dlat(states[f])
                moved[at(f, level), :] = tiles[f] - weight * change
            return carry

        lax.fori_loop(0, levels, body, 0, unroll=4)

    def beyond(slot, f, level):
        place = pl.ds(f * levels + level, 1)
        return jnp.where(row == 0, lat_rows[slot, 0, place, :], lat_rows[slot, 1, place, :])

    relayed = []

    def relay_until(end):
        for f in range(len(relayed), end):
            for d in range(1, pairs):
                cross[f, d].wait_recv()
                relay[f, d].start()
            relayed.append(f)

    def step(t):
        fslot, sslot = t, STEPS + t

        def forward(level, solved):
            shift = lax.rem(lanes - 2 * level, lanes)
            wind_u = state[t, at(0, level), :] * (weight * lon_sign)
            wind_v = state[t, at(1, level), :] * (weight * lat_sign)
            pert_u = field[at(0, level), :] * (weight * lon_sign)
            pert_v = field[at(1, level), :] * (weight * lat_sign)
            done = []
            for f in range(fields):
                change = wind_u * pltpu.roll(lon_mix[fslot, f], shift, 1)
                change += pert_u * pltpu.roll(lon_mix[sslot, f], shift, 1)
                change += wind_v * beyond(fslot, f, level) + pert_v * beyond(sslot, f, level)
                all_moved = moved[at(f, level), :] - change
                done.append(all_moved * coef[0, at(f, level), :] + solved[f] * coef[1, at(f, level), :])
            for f in range(fields):
                field[at(f, level), :] = done[f]
            return tuple(done)

        lax.fori_loop(0, levels, forward, no_tiles, unroll=8)
        if t + 1 < STEPS:
            take_state(t + 1)
        last = t == STEPS - 1
        if last:
            relay_until(fields - 2)

        def backward(k, carry):
            level = levels - 1 - k
            above, packed = carry
            done, edges = [], []
            for f in range(fields):
                x = field[at(f, level), :] + coef[2, at(f, level), :] * above[f]
                field[at(f, level), :] = x
                done.append(x)
                if not last:
                    edges.append(note_edges(level, x, packed[f]))
            return tuple(done), tuple(edges)

        _, packed = lax.fori_loop(0, levels, backward, (no_tiles, () if last else no_tiles), unroll=8)
        if not last:
            for f in range(fields):
                lon_out[t + 1, f] = packed[f]
            pack_rows(field, lat_out.at[t + 1])
            start_edges(field_edges[t + 1])

    take_state(0)
    traj_copies[1].wait_recv()
    for t in range(STEPS):
        build_state(t)
        if t == 0:
            for d in range(1, pairs):
                for f in range(1, fields):
                    cross[f, d].start()
        interior(t)
        if t == STEPS - 1:
            relay_until(min(2, fields))
        await_edges(field_edges[t], t)
        await_edges(state_edges[t], STEPS + t)
        step(t)
    relay_until(fields)
    basis_copy.wait_recv()

    total_rows = rows * lats
    total = float(fields * levels * total_rows * lanes * lons)
    row_ids = (lat * rows + row).astype(F32)
    cosine = jnp.cos((row_ids + 0.5) * (math.pi / total_rows) - math.pi / 2)

    def load_vector(i, f, m):
        first = pl.multiple_of(f * per_field + m * 2 * rows, 2 * rows)
        return allb[i, pl.ds(first, 2 * rows), :].astype(F32)

    acc = tuple(zero for _ in range(groups))
    for f in range(fields):
        for d in range(1, pairs):
            relay[f, d].wait_recv()
        scale = weight_ref[f] * cosine / total

        def gram(m, acc):
            acc = list(acc)
            low = field[at(f, 2 * m), :] * scale
            high = field[at(f, 2 * m + 1), :] * scale
            for i in range(groups):
                b = load_vector(i, f, m)
                acc[i] += b[:rows] * low + b[rows:] * high
            return tuple(acc)

        acc = lax.fori_loop(0, levels // 2, gram, acc, unroll=8)
    part = jnp.zeros((8, lanes), F32)
    part_row = lax.broadcasted_iota(jnp.int32, (8, lanes), 0)
    for i in range(groups):
        part = jnp.where(part_row == i, jnp.sum(acc[i], axis=0, keepdims=True), part)
    sums[me] = part
    sum_copies = []
    for k in range(1, tiles):
        copy = remote(("sum", k), sums.at[me], sums.at[me], other_tile(k))
        copy.start()
        sum_copies.append(copy)
    for copy in sum_copies:
        copy.wait_recv()
    whole = sums[0]
    for k in range(1, tiles):
        whole += sums[k]
    column = jnp.sum(whole, axis=1, keepdims=True)
    cols[vec] = jnp.broadcast_to(column, (8, lanes))
    col_copies = []
    for k in range(1, groups):
        copy = remote(("col", k), cols.at[vec], cols.at[vec], other_vec(k))
        copy.start()
        col_copies.append(copy)
    factor = [jnp.broadcast_to(column[i : i + 1], (rows, lanes)) for i in range(groups)]

    out_copies = []
    for f in range(fields):

        def residual(m, carry):
            low, high = field[at(f, 2 * m), :], field[at(f, 2 * m + 1), :]
            for i in range(groups):
                b = load_vector(i, f, m)
                low -= b[:rows] * factor[i]
                high -= b[rows:] * factor[i]
            field[at(f, 2 * m), :] = low
            field[at(f, 2 * m + 1), :] = high
            return carry

        lax.fori_loop(0, levels // 2, residual, 0, unroll=8)
        chunk = pl.ds(f * per_field, per_field)
        copy = pltpu.make_async_copy(field.at[chunk], out_ref.at[chunk], local_sem.at[5 + f])
        copy.start()
        out_copies.append(copy)

    for copy in col_copies:
        copy.wait_recv()
    table = jnp.zeros((8, lanes), F32)
    wide_lane = lax.broadcasted_iota(jnp.int32, (8, lanes), 1)
    for j in range(groups):
        table = jnp.where(wide_lane == j, cols[j], table)
    coup_ref[...] = table[:groups, :groups]

    for copy in out_copies:
        copy.wait()
    for copy in traj_copies:
        copy.wait_send()
    basis_copy.wait_send()
    for d in range(1, pairs):
        for f in range(fields):
            cross[f, d].wait_send()
            relay[f, d].wait_send()
        for t in range(STEPS):
            for i in range(PIECES):
                slices[t, d, i].wait_send()
                passes[t, d, i].wait_send()
    for t in range(STEPS):
        await_edges_sent(field_edges[t])
        await_edges_sent(state_edges[t])
    for copy in sum_copies + col_copies:
        copy.wait_send()


def hand_over(block_ref, coup_ref, block_out, coup_out, sem):
    copies = [pltpu.make_async_copy(coup_ref, coup_out, sem.at[0])]
    chunk = block_ref.shape[0] // CHUNKS
    for i in range(CHUNKS):
        where = pl.ds(i * chunk, chunk)
        copies.append(
            pltpu.make_async_copy(block_ref.at[where], block_out.at[where], sem.at[1 + i])
        )
    for copy in copies:
        copy.start()
    for copy in copies:
        copy.wait()


def solution(mesh):
    groups, lats, lons = mesh.shape["vec"], mesh.shape["lat"], mesh.shape["lon"]

    def per_device(basis, trajectory, slice_owner, diffusion, energy_weight):
        _, fields, levels, rows, lanes = basis.shape
        size = fields * levels * rows
        pairs, tiles = groups // 2, lats * lons
        ids = copy_names(pairs, tiles, groups, fields)
        slots = 2 * STEPS
        vmem = pl.BlockSpec(memory_space=pltpu.VMEM)
        hbm = pl.BlockSpec(memory_space=pltpu.HBM)
        residual_block, coupling = pl.pallas_call(
            functools.partial(kernel, (fields, levels, rows, lanes), (groups, lats, lons), ids),
            out_shape=(
                jax.ShapeDtypeStruct((size, lanes), F32),
                jax.ShapeDtypeStruct((groups, groups), F32),
            ),
            in_specs=[hbm] * 5,
            out_specs=(hbm, vmem),
            scratch_shapes=[
                pltpu.SMEM(slice_owner.shape, jnp.int32),
                pltpu.SMEM(diffusion.shape, F32),
                pltpu.SMEM(energy_weight.shape, F32),
                pltpu.VMEM((size, lanes), BF16),
                pltpu.VMEM((size, lanes), BF16),
                pltpu.VMEM((STEPS, size // 2, lanes), BF16),
                pltpu.VMEM((STEPS, max(pairs - 1, 1), size, lanes), BF16),
                pltpu.VMEM((groups, size, lanes), BF16),
                pltpu.VMEM((size, lanes), F32),
                pltpu.VMEM((STEPS, size, lanes), F32),
                pltpu.VMEM((size, lanes), F32),
                pltpu.VMEM((3, size, lanes), F32),
                pltpu.VMEM((slots, fields, rows, lanes), F32),
                pltpu.VMEM((slots, 2, fields, rows, lanes), F32),
                pltpu.VMEM((slots, 2, fields * levels, lanes), BF16),
                pltpu.VMEM((slots, 2, fields * levels, lanes), BF16),
                pltpu.VMEM((slots, fields, rows, lanes), F32),
                pltpu.VMEM((slots, 2, fields * levels, lanes), F32),
                pltpu.VMEM((tiles, 8, lanes), F32),
                pltpu.VMEM((groups, 8, lanes), F32),
                pltpu.SemaphoreType.DMA((5 + fields,)),
                pltpu.SemaphoreType.DMA((len(ids),)),
                pltpu.SemaphoreType.DMA((len(ids),)),
            ],
            compiler_params=pltpu.CompilerParams(
                collective_id=0, has_side_effects=True, vmem_limit_bytes=60 * 1024 * 1024
            ),
        )(
            basis.reshape(size, lanes),
            trajectory.reshape(size, lanes),
            slice_owner,
            diffusion,
            energy_weight,
        )
        residual_block, coupling = pl.pallas_call(
            hand_over,
            out_shape=(
                jax.ShapeDtypeStruct((size, lanes), F32),
                jax.ShapeDtypeStruct((groups, groups), F32),
            ),
            in_specs=[hbm, hbm],
            out_specs=(hbm, hbm),
            scratch_shapes=[pltpu.SemaphoreType.DMA((1 + CHUNKS,))],
            compiler_params=pltpu.CompilerParams(vmem_limit_bytes=60 * 1024 * 1024),
        )(residual_block, coupling)
        return residual_block.reshape(basis.shape), coupling

    return jax.shard_map(
        per_device,
        mesh=mesh,
        in_specs=(
            P("vec", None, None, "lat", "lon"),
            P("vec", None, None, "lat", "lon"),
            P(),
            P(),
            P(),
        ),
        out_specs=(P("vec", None, None, "lat", "lon"), P()),
        check_vma=False,
    )
```

```python
import functools
import math

import jax
import jax.numpy as jnp
from jax import lax
from jax.experimental import pallas as pl
from jax.experimental.pallas import tpu as pltpu
from jax.sharding import PartitionSpec as P

STEPS = 2
PIECES = 2
CHUNKS = 4
COURANT = 0.25
MESH = pl.DeviceIdType.MESH
F32 = jnp.float32
BF16 = jnp.bfloat16


def copy_names(pairs, tiles, groups, fields):
    names = [("traj", 0), ("traj", 1), "basis"]
    for d in range(1, pairs):
        names += [(kind, k, d) for kind in ("cross", "relay") for k in range(fields)]
        names += [
            (kind, t, d, i) for kind in ("slice", "pass") for t in range(STEPS) for i in range(PIECES)
        ]
    for t in range(STEPS):
        names += [(kind, t, s) for kind in ("flon", "flat", "slon", "slat") for s in range(2)]
    names += [("sum", k) for k in range(1, tiles)]
    names += [("col", k) for k in range(1, groups)]
    return {name: i for i, name in enumerate(names)}


def kernel(
    shape,
    counts,
    ids,
    basis_ref,
    traj_ref,
    owner_in,
    diff_in,
    weight_in,
    out_ref,
    coup_ref,
    owner_ref,
    diff_ref,
    weight_ref,
    own_traj,
    sib_traj,
    sel,
    rcv,
    allb,
    field,
    state,
    moved,
    coef,
    lon_out,
    lon_in,
    lat_out,
    lat_in,
    lon_mix,
    lat_rows,
    sums,
    cols,
    local_sem,
    send_sem,
    recv_sem,
):
    fields, levels, rows, lanes = shape
    groups, lats, lons = counts
    pairs, tiles = groups // 2, lats * lons
    size = fields * levels * rows
    per_field = levels * rows
    half = size // 2
    piece = half // PIECES
    vec = lax.axis_index("vec")
    lat = lax.axis_index("lat")
    lon = lax.axis_index("lon")
    core = lax.rem(vec, 2)
    pair = vec // 2
    sibling = vec + 1 - 2 * core
    me = lat * lons + lon

    def other_tile(k):
        index = lax.rem(me + k, tiles)
        return {"lat": index // lons, "lon": lax.rem(index, lons)}

    def other_vec(k):
        return {"vec": lax.rem(vec + k, groups)}

    def partner(d):
        return {"vec": 2 * lax.rem(pair + d, pairs) + core}

    def remote(name, src, dst, device):
        return pltpu.make_async_remote_copy(
            src_ref=src,
            dst_ref=dst,
            send_sem=send_sem.at[ids[name]],
            recv_sem=recv_sem.at[ids[name]],
            device_id=device,
            device_id_type=MESH,
        )

    local = [
        pltpu.make_async_copy(source, target, local_sem.at[i])
        for i, (source, target) in enumerate(
            (
                (basis_ref, allb.at[vec]),
                (traj_ref, own_traj),
                (owner_in, owner_ref),
                (diff_in, diff_ref),
                (weight_in, weight_ref),
            )
        )
    ]
    for copy in local:
        copy.start()

    barrier = pltpu.get_barrier_semaphore()
    for k in range(1, tiles):
        pl.semaphore_signal(barrier, inc=1, device_id=other_tile(k), device_id_type=MESH)
    for k in range(1, groups):
        pl.semaphore_signal(barrier, inc=1, device_id=other_vec(k), device_id_type=MESH)
    local[1].wait()
    local[0].wait()
    pl.semaphore_wait(barrier, tiles + groups - 2)

    to_sibling = {"vec": sibling}
    own_half = pl.ds(pl.multiple_of(core * half, 16), half)
    far_half = pl.ds(pl.multiple_of((1 - core) * half, 16), half)

    traj_copies = [
        remote(("traj", i), own_traj.at[part], sib_traj.at[part], to_sibling)
        for i, part in enumerate((far_half, own_half))
    ]
    traj_copies[0].start()
    cross = {}
    relay = {}
    for d in range(1, pairs):
        source = 2 * lax.rem(pair + pairs - d, pairs) + core
        for f in range(fields):
            chunk = pl.ds(f * per_field, per_field)
            cross[f, d] = remote(
                ("cross", f, d), allb.at[vec, chunk], allb.at[vec, chunk], partner(d)
            )
            relay[f, d] = remote(
                ("relay", f, d), allb.at[source, chunk], allb.at[source, chunk], to_sibling
            )
    for d in range(1, pairs):
        cross[0, d].start()
    traj_copies[1].start()
    basis_copy = remote("basis", allb.at[vec], allb.at[vec], to_sibling)
    basis_copy.start()

    lane = lax.broadcasted_iota(jnp.int32, (rows, lanes), 1)
    row = lax.broadcasted_iota(jnp.int32, (rows, lanes), 0)

    def edge_copies(kind, slot, t):
        east = {"lon": lax.rem(lon + 1, lons)}
        west = {"lon": lax.rem(lon + lons - 1, lons)}
        up = {"lat": lax.rem(lat + 1, lats)}
        down = {"lat": lax.rem(lat + lats - 1, lats)}
        source, target = lat_out.at[slot], lat_in.at[slot]
        return (
            remote((kind + "lon", t, 0), lon_out.at[slot], lon_in.at[slot, 0], east),
            remote((kind + "lon", t, 1), lon_out.at[slot], lon_in.at[slot, 1], west),
            remote((kind + "lat", t, 0), source.at[1], target.at[0], up),
            remote((kind + "lat", t, 1), source.at[0], target.at[1], down),
        )

    def start_edges(copies):
        copies[0].start()
        copies[1].start()

        @pl.when(lat < lats - 1)
        def _():
            copies[2].start()

        @pl.when(lat > 0)
        def _():
            copies[3].start()

    def await_edges(copies, slot):
        copies[0].wait_recv()
        copies[1].wait_recv()

        def settle(copy, side, present):
            @pl.when(present)
            def _():
                copy.wait_recv()
                lat_rows[slot, side] = lat_in[slot, side].astype(F32)

            @pl.when(jnp.logical_not(present))
            def _():
                lat_rows[slot, side] = jnp.zeros((fields * levels, lanes), F32)

        settle(copies[2], 0, lat > 0)
        settle(copies[3], 1, lat < lats - 1)

        for f in range(fields):
            lon_mix[slot, f] = jnp.where(
                lax.rem(lane, 2) == 0,
                pltpu.roll(lon_in[slot, 0, f], 1, 1),
                pltpu.roll(lon_in[slot, 1, f], lanes - 1, 1),
            )

    def await_edges_sent(copies):
        copies[0].wait_send()
        copies[1].wait_send()

        @pl.when(lat < lats - 1)
        def _():
            copies[2].wait_send()

        @pl.when(lat > 0)
        def _():
            copies[3].wait_send()

    def at(f, level):
        return pl.ds(pl.multiple_of(f * per_field + level * rows, rows), rows)

    def note_edges(level, tile, packed):
        spot = 2 * level
        here = (lane == spot) | (lane == lax.rem(spot + lanes - 1, lanes))
        return jnp.where(here, pltpu.roll(tile, spot, 1), packed)

    def pack_rows(tiles_ref, target):
        for f in range(fields):
            for side in range(2):
                first = f * per_field + side * (rows - 1)
                edge = tiles_ref[pl.ds(first, levels, stride=rows), :]
                target[side, f * levels : (f + 1) * levels, :] = edge.astype(target.dtype)

    no_tiles = tuple(jnp.zeros((rows, lanes), F32) for _ in range(fields))

    def spread(load, tiles_ref, slot):
        def body(m, packed):
            done = []
            for f in range(fields):
                first = pl.multiple_of(f * per_field + m * 2 * rows, 2 * rows)
                both = load(pl.ds(first, 2 * rows))
                tiles_ref[pl.ds(first, 2 * rows), :] = both
                p = packed[f]
                for i in range(2):
                    p = note_edges(2 * m + i, both[i * rows : (i + 1) * rows], p)
                done.append(p)
            return tuple(done)

        packed = lax.fori_loop(0, levels // 2, body, no_tiles, unroll=4)
        for f in range(fields):
            lon_out[slot, f] = packed[f]
        pack_rows(tiles_ref, lat_out.at[slot])

    for copy in local[2:]:
        copy.wait()
    traj_copies[0].wait_recv()
    slices = {}
    passes = {}
    for t in range(STEPS):
        sel[t] = jnp.where(
            owner_ref[t] == vec,
            own_traj[own_half, :].astype(F32),
            sib_traj[own_half, :].astype(F32),
        ).astype(BF16)
        for d in range(1, pairs):
            for i in range(PIECES):
                first = pl.multiple_of(core * half + i * piece, 16)
                there = rcv.at[t, d - 1, pl.ds(first, piece)]
                slices[t, d, i] = remote(
                    ("slice", t, d, i), sel.at[t, pl.ds(i * piece, piece)], there, partner(d)
                )
                passes[t, d, i] = remote(("pass", t, d, i), there, there, to_sibling)
                if t == 0:
                    slices[t, d, i].start()

    spread(lambda where: allb[vec, where, :].astype(F32), field, 0)
    field_edges = [edge_copies("f", t, t) for t in range(STEPS)]
    state_edges = [edge_copies("s", STEPS + t, t) for t in range(STEPS)]
    start_edges(field_edges[0])

    def pivots(level, carry):
        done = []
        for f in range(fields):
            above, ratio = carry[f]
            below = jnp.full((rows, lanes), diff_ref[f, level], F32)
            inv = 1.0 / (1.0 + below + above - above * ratio)
            coef[0, at(f, level), :] = inv
            coef[1, at(f, level), :] = above * inv
            coef[2, at(f, level), :] = below * inv
            done.append((below, below * inv))
        return tuple(done)

    zero = jnp.zeros((rows, lanes), F32)
    carry = lax.fori_loop(0, levels - 1, pivots, tuple((zero, zero) for _ in range(fields)))
    for f in range(fields):
        above, ratio = carry[f]
        inv = 1.0 / (1.0 + above - above * ratio)
        coef[0, at(f, levels - 1), :] = inv
        coef[1, at(f, levels - 1), :] = above * inv
        coef[2, at(f, levels - 1), :] = zero

    every = [(d, i) for i in range(PIECES) for d in range(1, pairs)]

    def take_state(t):
        for d, i in every:
            slices[t, d, i].wait_recv()
            passes[t, d, i].start()
        if t + 1 < STEPS:
            for d, i in every:
                slices[t + 1, d, i].start()

    def build_state(t):
        for d, i in every:
            passes[t, d, i].wait_recv()
        holder = owner_ref[t] // 2
        mine = owner_ref[t] == vec

        def load_state(where):
            block = jnp.where(
                mine, own_traj[where, :].astype(F32), sib_traj[where, :].astype(F32)
            )
            for d in range(1, pairs):
                source = lax.rem(pair + pairs - d, pairs)
                block = jnp.where(holder == source, rcv[t, d - 1, where, :].astype(F32), block)
            return block

        spread(load_state, state.at[t], STEPS + t)
        start_edges(state_edges[t])

    def dlon(tile):
        after = jnp.where(lane == lanes - 1, 0.0, pltpu.roll(tile, lanes - 1, 1))
        return after - jnp.where(lane == 0, 0.0, pltpu.roll(tile, 1, 1))

    def dlat(tile):
        after = jnp.where(row == rows - 1, 0.0, pltpu.roll(tile, rows - 1, 0))
        return after - jnp.where(row == 0, 0.0, pltpu.roll(tile, 1, 0))

    lon_sign = jnp.where(lane == lanes - 1, 1.0, jnp.where(lane == 0, -1.0, 0.0))
    lat_sign = jnp.where(row == rows - 1, 1.0, jnp.where(row == 0, -1.0, 0.0))
    weight = 0.5 * COURANT

    def interior(t):
        def body(level, carry):
            tiles = [field[at(f, level), :] for f in range(fields)]
            states = [state[t, at(f, level), :] for f in range(fields)]
            for f in range(fields):
                change = states[0] * dlon(tiles[f]) + states[1] * dlat(tiles[f])
                change += tiles[0] * dlon(states[f]) + tiles[1] * dlat(states[f])
                moved[at(f, level), :] = tiles[f] - weight * change
            return carry

        lax.fori_loop(0, levels, body, 0, unroll=4)

    def beyond(slot, f, level):
        place = pl.ds(f * levels + level, 1)
        return jnp.where(row == 0, lat_rows[slot, 0, place, :], lat_rows[slot, 1, place, :])

    relayed = []

    def relay_until(end):
        for f in range(len(relayed), end):
            for d in range(1, pairs):
                cross[f, d].wait_recv()
                relay[f, d].start()
            relayed.append(f)

    def step(t):
        fslot, sslot = t, STEPS + t

        def forward(level, solved):
            shift = lax.rem(lanes - 2 * level, lanes)
            wind_u = state[t, at(0, level), :] * (weight * lon_sign)
            wind_v = state[t, at(1, level), :] * (weight * lat_sign)
            pert_u = field[at(0, level), :] * (weight * lon_sign)
            pert_v = field[at(1, level), :] * (weight * lat_sign)
            done = []
            for f in range(fields):
                change = wind_u * pltpu.roll(lon_mix[fslot, f], shift, 1)
                change += pert_u * pltpu.roll(lon_mix[sslot, f], shift, 1)
                change += wind_v * beyond(fslot, f, level) + pert_v * beyond(sslot, f, level)
                all_moved = moved[at(f, level), :] - change
                done.append(all_moved * coef[0, at(f, level), :] + solved[f] * coef[1, at(f, level), :])
            for f in range(fields):
                field[at(f, level), :] = done[f]
            return tuple(done)

        lax.fori_loop(0, levels, forward, no_tiles, unroll=8)
        if t + 1 < STEPS:
            take_state(t + 1)
        last = t == STEPS - 1
        if last:
            relay_until(fields - 2)

        def backward(k, carry):
            level = levels - 1 - k
            above, packed = carry
            done, edges = [], []
            for f in range(fields):
                x = field[at(f, level), :] + coef[2, at(f, level), :] * above[f]
                field[at(f, level), :] = x
                done.append(x)
                if not last:
                    edges.append(note_edges(level, x, packed[f]))
            return tuple(done), tuple(edges)

        _, packed = lax.fori_loop(0, levels, backward, (no_tiles, () if last else no_tiles), unroll=8)
        if not last:
            for f in range(fields):
                lon_out[t + 1, f] = packed[f]
            pack_rows(field, lat_out.at[t + 1])
            start_edges(field_edges[t + 1])

    take_state(0)
    traj_copies[1].wait_recv()
    for t in range(STEPS):
        build_state(t)
        if t == 0:
            for d in range(1, pairs):
                for f in range(1, fields):
                    cross[f, d].start()
        interior(t)
        if t == STEPS - 1:
            relay_until(min(2, fields))
        await_edges(field_edges[t], t)
        await_edges(state_edges[t], STEPS + t)
        step(t)
    relay_until(fields)
    basis_copy.wait_recv()

    total_rows = rows * lats
    total = float(fields * levels * total_rows * lanes * lons)
    row_ids = (lat * rows + row).astype(F32)
    cosine = jnp.cos((row_ids + 0.5) * (math.pi / total_rows) - math.pi / 2)

    def load_vector(i, f, m):
        first = pl.multiple_of(f * per_field + m * 2 * rows, 2 * rows)
        return allb[i, pl.ds(first, 2 * rows), :].astype(F32)

    acc = tuple(zero for _ in range(groups))
    for f in range(fields):
        for d in range(1, pairs):
            relay[f, d].wait_recv()
        scale = weight_ref[f] * cosine / total

        def gram(m, acc):
            acc = list(acc)
            low = field[at(f, 2 * m), :] * scale
            high = field[at(f, 2 * m + 1), :] * scale
            for i in range(groups):
                b = load_vector(i, f, m)
                acc[i] += b[:rows] * low + b[rows:] * high
            return tuple(acc)

        acc = lax.fori_loop(0, levels // 2, gram, acc, unroll=8)
    part = jnp.zeros((8, lanes), F32)
    part_row = lax.broadcasted_iota(jnp.int32, (8, lanes), 0)
    for i in range(groups):
        part = jnp.where(part_row == i, jnp.sum(acc[i], axis=0, keepdims=True), part)
    sums[me] = part
    sum_copies = []
    for k in range(1, tiles):
        copy = remote(("sum", k), sums.at[me], sums.at[me], other_tile(k))
        copy.start()
        sum_copies.append(copy)
    for copy in sum_copies:
        copy.wait_recv()
    whole = sums[0]
    for k in range(1, tiles):
        whole += sums[k]
    column = jnp.sum(whole, axis=1, keepdims=True)
    cols[vec] = jnp.broadcast_to(column, (8, lanes))
    col_copies = []
    for k in range(1, groups):
        copy = remote(("col", k), cols.at[vec], cols.at[vec], other_vec(k))
        copy.start()
        col_copies.append(copy)
    factor = [jnp.broadcast_to(column[i : i + 1], (rows, lanes)) for i in range(groups)]

    out_copies = []
    for f in range(fields):

        def residual(m, carry):
            low, high = field[at(f, 2 * m), :], field[at(f, 2 * m + 1), :]
            for i in range(groups):
                b = load_vector(i, f, m)
                low -= b[:rows] * factor[i]
                high -= b[rows:] * factor[i]
            field[at(f, 2 * m), :] = low
            field[at(f, 2 * m + 1), :] = high
            return carry

        lax.fori_loop(0, levels // 2, residual, 0, unroll=8)
        chunk = pl.ds(f * per_field, per_field)
        copy = pltpu.make_async_copy(field.at[chunk], out_ref.at[chunk], local_sem.at[5 + f])
        copy.start()
        out_copies.append(copy)

    for copy in col_copies:
        copy.wait_recv()
    table = jnp.zeros((8, lanes), F32)
    wide_lane = lax.broadcasted_iota(jnp.int32, (8, lanes), 1)
    for j in range(groups):
        table = jnp.where(wide_lane == j, cols[j], table)
    coup_ref[...] = table[:groups, :groups]

    for copy in out_copies:
        copy.wait()
    for copy in traj_copies:
        copy.wait_send()
    basis_copy.wait_send()
    for d in range(1, pairs):
        for f in range(fields):
            cross[f, d].wait_send()
            relay[f, d].wait_send()
        for t in range(STEPS):
            for i in range(PIECES):
                slices[t, d, i].wait_send()
                passes[t, d, i].wait_send()
    for t in range(STEPS):
        await_edges_sent(field_edges[t])
        await_edges_sent(state_edges[t])
    for copy in sum_copies + col_copies:
        copy.wait_send()


def hand_over(block_ref, coup_ref, block_out, coup_out, block, coup, in_sem, out_sem):
    chunk = block_ref.shape[0] // CHUNKS
    parts = [(coup_ref, coup, coup_out)]
    for i in range(CHUNKS):
        where = pl.ds(i * chunk, chunk)
        parts.append((block_ref.at[where], block.at[where], block_out.at[where]))
    loads, stores = [], []
    for i, (source, here, target) in enumerate(parts):
        loads.append(pltpu.make_async_copy(source, here, in_sem.at[i]))
        stores.append(pltpu.make_async_copy(here, target, out_sem.at[i]))
    for copy in loads:
        copy.start()
    for load, store in zip(loads, stores):
        load.wait()
        store.start()
    for copy in stores:
        copy.wait()


def solution(mesh):
    groups, lats, lons = mesh.shape["vec"], mesh.shape["lat"], mesh.shape["lon"]

    def per_device(basis, trajectory, slice_owner, diffusion, energy_weight):
        _, fields, levels, rows, lanes = basis.shape
        size = fields * levels * rows
        pairs, tiles = groups // 2, lats * lons
        ids = copy_names(pairs, tiles, groups, fields)
        slots = 2 * STEPS
        vmem = pl.BlockSpec(memory_space=pltpu.VMEM)
        hbm = pl.BlockSpec(memory_space=pltpu.HBM)
        residual_block, coupling = pl.pallas_call(
            functools.partial(kernel, (fields, levels, rows, lanes), (groups, lats, lons), ids),
            out_shape=(
                jax.ShapeDtypeStruct((size, lanes), F32),
                jax.ShapeDtypeStruct((groups, groups), F32),
            ),
            in_specs=[hbm] * 5,
            out_specs=(hbm, vmem),
            scratch_shapes=[
                pltpu.SMEM(slice_owner.shape, jnp.int32),
                pltpu.SMEM(diffusion.shape, F32),
                pltpu.SMEM(energy_weight.shape, F32),
                pltpu.VMEM((size, lanes), BF16),
                pltpu.VMEM((size, lanes), BF16),
                pltpu.VMEM((STEPS, size // 2, lanes), BF16),
                pltpu.VMEM((STEPS, max(pairs - 1, 1), size, lanes), BF16),
                pltpu.VMEM((groups, size, lanes), BF16),
                pltpu.VMEM((size, lanes), F32),
                pltpu.VMEM((STEPS, size, lanes), F32),
                pltpu.VMEM((size, lanes), F32),
                pltpu.VMEM((3, size, lanes), F32),
                pltpu.VMEM((slots, fields, rows, lanes), F32),
                pltpu.VMEM((slots, 2, fields, rows, lanes), F32),
                pltpu.VMEM((slots, 2, fields * levels, lanes), BF16),
                pltpu.VMEM((slots, 2, fields * levels, lanes), BF16),
                pltpu.VMEM((slots, fields, rows, lanes), F32),
                pltpu.VMEM((slots, 2, fields * levels, lanes), F32),
                pltpu.VMEM((tiles, 8, lanes), F32),
                pltpu.VMEM((groups, 8, lanes), F32),
                pltpu.SemaphoreType.DMA((5 + fields,)),
                pltpu.SemaphoreType.DMA((len(ids),)),
                pltpu.SemaphoreType.DMA((len(ids),)),
            ],
            compiler_params=pltpu.CompilerParams(
                collective_id=0, has_side_effects=True, vmem_limit_bytes=60 * 1024 * 1024
            ),
        )(
            basis.reshape(size, lanes),
            trajectory.reshape(size, lanes),
            slice_owner,
            diffusion,
            energy_weight,
        )
        residual_block, coupling = pl.pallas_call(
            hand_over,
            out_shape=(
                jax.ShapeDtypeStruct((size, lanes), F32),
                jax.ShapeDtypeStruct((groups, groups), F32),
            ),
            in_specs=[hbm, hbm],
            out_specs=(hbm, hbm),
            scratch_shapes=[
                pltpu.VMEM((size, lanes), F32),
                pltpu.VMEM((groups, groups), F32),
                pltpu.SemaphoreType.DMA((1 + CHUNKS,)),
                pltpu.SemaphoreType.DMA((1 + CHUNKS,)),
            ],
            compiler_params=pltpu.CompilerParams(vmem_limit_bytes=60 * 1024 * 1024),
        )(residual_block, coupling)
        return residual_block.reshape(basis.shape), coupling

    return jax.shard_map(
        per_device,
        mesh=mesh,
        in_specs=(
            P("vec", None, None, "lat", "lon"),
            P("vec", None, None, "lat", "lon"),
            P(),
            P(),
            P(),
        ),
        out_specs=(P("vec", None, None, "lat", "lon"), P()),
        check_vma=False,
    )
```

```python
import functools
import math

import jax
import jax.numpy as jnp
from jax import lax
from jax.experimental import pallas as pl
from jax.experimental.pallas import tpu as pltpu
from jax.sharding import PartitionSpec as P

STEPS = 2
PIECES = 2
SPLIT = 2
COURANT = 0.25
MESH = pl.DeviceIdType.MESH
F32 = jnp.float32
BF16 = jnp.bfloat16


def copy_names(pairs, tiles, groups, fields):
    names = [("traj", 0), ("traj", 1), "basis"]
    for d in range(1, pairs):
        names += [(kind, k, d) for kind in ("cross", "relay") for k in range(SPLIT * fields)]
        names += [
            (kind, t, d, i) for kind in ("slice", "pass") for t in range(STEPS) for i in range(PIECES)
        ]
    for t in range(STEPS):
        names += [(kind, t, s) for kind in ("flon", "flat", "slon", "slat") for s in range(2)]
    names += [("sum", k) for k in range(1, tiles)]
    names += [("col", k) for k in range(1, groups)]
    return {name: i for i, name in enumerate(names)}


def kernel(
    shape,
    counts,
    ids,
    basis_ref,
    traj_ref,
    owner_in,
    diff_in,
    weight_in,
    field_out,
    allb_out,
    column_out,
    coup_ref,
    owner_ref,
    diff_ref,
    weight_ref,
    own_traj,
    sib_traj,
    sel,
    rcv,
    allb,
    field,
    state,
    moved,
    coef,
    lon_out,
    lon_in,
    lat_out,
    lat_in,
    lon_mix,
    lat_rows,
    sums,
    cols,
    local_sem,
    send_sem,
    recv_sem,
):
    fields, levels, rows, lanes = shape
    groups, lats, lons = counts
    pairs, tiles = groups // 2, lats * lons
    size = fields * levels * rows
    per_field = levels * rows
    half = size // 2
    piece = half // PIECES
    chunks = SPLIT * fields
    chunk = per_field // SPLIT
    vec = lax.axis_index("vec")
    lat = lax.axis_index("lat")
    lon = lax.axis_index("lon")
    core = lax.rem(vec, 2)
    pair = vec // 2
    sibling = vec + 1 - 2 * core
    me = lat * lons + lon

    def other_tile(k):
        index = lax.rem(me + k, tiles)
        return {"lat": index // lons, "lon": lax.rem(index, lons)}

    def other_vec(k):
        return {"vec": lax.rem(vec + k, groups)}

    def partner(d):
        return {"vec": 2 * lax.rem(pair + d, pairs) + core}

    def remote(name, src, dst, device):
        return pltpu.make_async_remote_copy(
            src_ref=src,
            dst_ref=dst,
            send_sem=send_sem.at[ids[name]],
            recv_sem=recv_sem.at[ids[name]],
            device_id=device,
            device_id_type=MESH,
        )

    local = [
        pltpu.make_async_copy(source, target, local_sem.at[i])
        for i, (source, target) in enumerate(
            (
                (basis_ref, allb.at[vec]),
                (traj_ref, own_traj),
                (owner_in, owner_ref),
                (diff_in, diff_ref),
                (weight_in, weight_ref),
            )
        )
    ]
    for copy in local:
        copy.start()

    barrier = pltpu.get_barrier_semaphore()
    for k in range(1, tiles):
        pl.semaphore_signal(barrier, inc=1, device_id=other_tile(k), device_id_type=MESH)
    for k in range(1, groups):
        pl.semaphore_signal(barrier, inc=1, device_id=other_vec(k), device_id_type=MESH)
    local[1].wait()
    local[0].wait()
    pl.semaphore_wait(barrier, tiles + groups - 2)

    to_sibling = {"vec": sibling}
    own_half = pl.ds(pl.multiple_of(core * half, 16), half)
    far_half = pl.ds(pl.multiple_of((1 - core) * half, 16), half)

    traj_copies = [
        remote(("traj", i), own_traj.at[part], sib_traj.at[part], to_sibling)
        for i, part in enumerate((far_half, own_half))
    ]
    traj_copies[0].start()
    cross = {}
    relay = {}
    for d in range(1, pairs):
        source = 2 * lax.rem(pair + pairs - d, pairs) + core
        for k in range(chunks):
            part = pl.ds(k * chunk, chunk)
            cross[k, d] = remote(
                ("cross", k, d), allb.at[vec, part], allb.at[vec, part], partner(d)
            )
            relay[k, d] = remote(
                ("relay", k, d), allb.at[source, part], allb.at[source, part], to_sibling
            )
    sent, relayed = [], []

    def send_until(end):
        for k in range(len(sent), min(end, chunks)):
            for d in range(1, pairs):
                cross[k, d].start()
            sent.append(k)

    def relay_until(end):
        for k in range(len(relayed), min(end, chunks)):
            for d in range(1, pairs):
                cross[k, d].wait_recv()
                relay[k, d].start()
            relayed.append(k)
            send_until(len(sent) + 1)

    send_until(SPLIT)
    traj_copies[1].start()
    basis_copy = remote("basis", allb.at[vec], allb.at[vec], to_sibling)
    basis_copy.start()

    lane = lax.broadcasted_iota(jnp.int32, (rows, lanes), 1)
    row = lax.broadcasted_iota(jnp.int32, (rows, lanes), 0)

    def edge_copies(kind, slot, t):
        east = {"lon": lax.rem(lon + 1, lons)}
        west = {"lon": lax.rem(lon + lons - 1, lons)}
        up = {"lat": lax.rem(lat + 1, lats)}
        down = {"lat": lax.rem(lat + lats - 1, lats)}
        source, target = lat_out.at[slot], lat_in.at[slot]
        return (
            remote((kind + "lon", t, 0), lon_out.at[slot], lon_in.at[slot, 0], east),
            remote((kind + "lon", t, 1), lon_out.at[slot], lon_in.at[slot, 1], west),
            remote((kind + "lat", t, 0), source.at[1], target.at[0], up),
            remote((kind + "lat", t, 1), source.at[0], target.at[1], down),
        )

    def start_edges(copies):
        copies[0].start()
        copies[1].start()

        @pl.when(lat < lats - 1)
        def _():
            copies[2].start()

        @pl.when(lat > 0)
        def _():
            copies[3].start()

    def await_edges(copies, slot):
        copies[0].wait_recv()
        copies[1].wait_recv()

        def settle(copy, side, present):
            @pl.when(present)
            def _():
                copy.wait_recv()
                lat_rows[slot, side] = lat_in[slot, side].astype(F32)

            @pl.when(jnp.logical_not(present))
            def _():
                lat_rows[slot, side] = jnp.zeros((fields * levels, lanes), F32)

        settle(copies[2], 0, lat > 0)
        settle(copies[3], 1, lat < lats - 1)

        for f in range(fields):
            lon_mix[slot, f] = jnp.where(
                lax.rem(lane, 2) == 0,
                pltpu.roll(lon_in[slot, 0, f], 1, 1),
                pltpu.roll(lon_in[slot, 1, f], lanes - 1, 1),
            )

    def await_edges_sent(copies):
        copies[0].wait_send()
        copies[1].wait_send()

        @pl.when(lat < lats - 1)
        def _():
            copies[2].wait_send()

        @pl.when(lat > 0)
        def _():
            copies[3].wait_send()

    def at(f, level):
        return pl.ds(pl.multiple_of(f * per_field + level * rows, rows), rows)

    def note_edges(level, tile, packed):
        spot = 2 * level
        here = (lane == spot) | (lane == lax.rem(spot + lanes - 1, lanes))
        return jnp.where(here, pltpu.roll(tile, spot, 1), packed)

    def pack_rows(tiles_ref, target):
        for f in range(fields):
            for side in range(2):
                first = f * per_field + side * (rows - 1)
                edge = tiles_ref[pl.ds(first, levels, stride=rows), :]
                target[side, f * levels : (f + 1) * levels, :] = edge.astype(target.dtype)

    no_tiles = tuple(jnp.zeros((rows, lanes), F32) for _ in range(fields))

    def spread(load, tiles_ref, slot):
        def body(m, packed):
            done = []
            for f in range(fields):
                first = pl.multiple_of(f * per_field + m * 2 * rows, 2 * rows)
                both = load(pl.ds(first, 2 * rows))
                tiles_ref[pl.ds(first, 2 * rows), :] = both
                p = packed[f]
                for i in range(2):
                    p = note_edges(2 * m + i, both[i * rows : (i + 1) * rows], p)
                done.append(p)
            return tuple(done)

        packed = lax.fori_loop(0, levels // 2, body, no_tiles, unroll=4)
        for f in range(fields):
            lon_out[slot, f] = packed[f]
        pack_rows(tiles_ref, lat_out.at[slot])

    for copy in local[2:]:
        copy.wait()
    traj_copies[0].wait_recv()
    slices = {}
    passes = {}
    for t in range(STEPS):
        sel[t] = jnp.where(
            owner_ref[t] == vec,
            own_traj[own_half, :].astype(F32),
            sib_traj[own_half, :].astype(F32),
        ).astype(BF16)
        for d in range(1, pairs):
            for i in range(PIECES):
                first = pl.multiple_of(core * half + i * piece, 16)
                there = rcv.at[t, d - 1, pl.ds(first, piece)]
                slices[t, d, i] = remote(
                    ("slice", t, d, i), sel.at[t, pl.ds(i * piece, piece)], there, partner(d)
                )
                passes[t, d, i] = remote(("pass", t, d, i), there, there, to_sibling)
                if t == 0:
                    slices[t, d, i].start()

    spread(lambda where: allb[vec, where, :].astype(F32), field, 0)
    field_edges = [edge_copies("f", t, t) for t in range(STEPS)]
    state_edges = [edge_copies("s", STEPS + t, t) for t in range(STEPS)]
    start_edges(field_edges[0])

    def pivots(level, carry):
        done = []
        for f in range(fields):
            above, ratio = carry[f]
            below = jnp.full((rows, lanes), diff_ref[f, level], F32)
            inv = 1.0 / (1.0 + below + above - above * ratio)
            coef[0, at(f, level), :] = inv
            coef[1, at(f, level), :] = above * inv
            coef[2, at(f, level), :] = below * inv
            done.append((below, below * inv))
        return tuple(done)

    zero = jnp.zeros((rows, lanes), F32)
    carry = lax.fori_loop(0, levels - 1, pivots, tuple((zero, zero) for _ in range(fields)))
    for f in range(fields):
        above, ratio = carry[f]
        inv = 1.0 / (1.0 + above - above * ratio)
        coef[0, at(f, levels - 1), :] = inv
        coef[1, at(f, levels - 1), :] = above * inv
        coef[2, at(f, levels - 1), :] = zero

    every = [(d, i) for i in range(PIECES) for d in range(1, pairs)]

    def take_state(t):
        for d, i in every:
            slices[t, d, i].wait_recv()
            passes[t, d, i].start()
            if t + 1 < STEPS:
                slices[t + 1, d, i].start()

    def build_state(t):
        for d, i in every:
            passes[t, d, i].wait_recv()
        holder = owner_ref[t] // 2
        mine = owner_ref[t] == vec

        def load_state(where):
            block = jnp.where(
                mine, own_traj[where, :].astype(F32), sib_traj[where, :].astype(F32)
            )
            for d in range(1, pairs):
                source = lax.rem(pair + pairs - d, pairs)
                block = jnp.where(holder == source, rcv[t, d - 1, where, :].astype(F32), block)
            return block

        spread(load_state, state.at[t], STEPS + t)
        start_edges(state_edges[t])

    def dlon(tile):
        after = jnp.where(lane == lanes - 1, 0.0, pltpu.roll(tile, lanes - 1, 1))
        return after - jnp.where(lane == 0, 0.0, pltpu.roll(tile, 1, 1))

    def dlat(tile):
        after = jnp.where(row == rows - 1, 0.0, pltpu.roll(tile, rows - 1, 0))
        return after - jnp.where(row == 0, 0.0, pltpu.roll(tile, 1, 0))

    lon_sign = jnp.where(lane == lanes - 1, 1.0, jnp.where(lane == 0, -1.0, 0.0))
    lat_sign = jnp.where(row == rows - 1, 1.0, jnp.where(row == 0, -1.0, 0.0))
    weight = 0.5 * COURANT

    def interior(t):
        def body(level, carry):
            tiles = [field[at(f, level), :] for f in range(fields)]
            states = [state[t, at(f, level), :] for f in range(fields)]
            for f in range(fields):
                change = states[0] * dlon(tiles[f]) + states[1] * dlat(tiles[f])
                change += tiles[0] * dlon(states[f]) + tiles[1] * dlat(states[f])
                moved[at(f, level), :] = tiles[f] - weight * change
            return carry

        lax.fori_loop(0, levels, body, 0, unroll=4)

    def beyond(slot, f, level):
        place = pl.ds(f * levels + level, 1)
        return jnp.where(row == 0, lat_rows[slot, 0, place, :], lat_rows[slot, 1, place, :])

    def step(t):
        fslot, sslot = t, STEPS + t

        def forward(level, solved):
            shift = lax.rem(lanes - 2 * level, lanes)
            wind_u = state[t, at(0, level), :] * (weight * lon_sign)
            wind_v = state[t, at(1, level), :] * (weight * lat_sign)
            pert_u = field[at(0, level), :] * (weight * lon_sign)
            pert_v = field[at(1, level), :] * (weight * lat_sign)
            done = []
            for f in range(fields):
                change = wind_u * pltpu.roll(lon_mix[fslot, f], shift, 1)
                change += pert_u * pltpu.roll(lon_mix[sslot, f], shift, 1)
                change += wind_v * beyond(fslot, f, level) + pert_v * beyond(sslot, f, level)
                all_moved = moved[at(f, level), :] - change
                done.append(all_moved * coef[0, at(f, level), :] + solved[f] * coef[1, at(f, level), :])
            for f in range(fields):
                field[at(f, level), :] = done[f]
            return tuple(done)

        lax.fori_loop(0, levels, forward, no_tiles, unroll=8)
        if t + 1 < STEPS:
            take_state(t + 1)
            relay_until(SPLIT)
        last = t == STEPS - 1
        if last:
            relay_until(2 * SPLIT + 1)

        def backward(k, carry):
            level = levels - 1 - k
            above, packed = carry
            done, edges = [], []
            for f in range(fields):
                x = field[at(f, level), :] + coef[2, at(f, level), :] * above[f]
                field[at(f, level), :] = x
                done.append(x)
                if not last:
                    edges.append(note_edges(level, x, packed[f]))
            return tuple(done), tuple(edges)

        _, packed = lax.fori_loop(0, levels, backward, (no_tiles, () if last else no_tiles), unroll=8)
        if not last:
            for f in range(fields):
                lon_out[t + 1, f] = packed[f]
            pack_rows(field, lat_out.at[t + 1])
            start_edges(field_edges[t + 1])

    take_state(0)
    traj_copies[1].wait_recv()
    for t in range(STEPS):
        build_state(t)
        if t == 0:
            send_until(2 * SPLIT)
        interior(t)
        if t == STEPS - 1:
            relay_until(2 * SPLIT)
        await_edges(field_edges[t], t)
        await_edges(state_edges[t], STEPS + t)
        step(t)
    field_copy = pltpu.make_async_copy(field, field_out, local_sem.at[5])
    field_copy.start()
    basis_copy.wait_recv()

    total_rows = rows * lats
    total = float(fields * levels * total_rows * lanes * lons)
    row_ids = (lat * rows + row).astype(F32)
    cosine = jnp.cos((row_ids + 0.5) * (math.pi / total_rows) - math.pi / 2)

    acc = tuple(zero for _ in range(groups))
    base_copies = []
    for k in range(chunks):
        relay_until(k + 2)
        for d in range(1, pairs):
            relay[k, d].wait_recv()
        scale = weight_ref[k // SPLIT] * cosine / total
        part = pl.ds(k * chunk, chunk)
        copy = pltpu.make_async_copy(allb.at[:, part], allb_out.at[:, part], local_sem.at[6 + k])
        copy.start()
        base_copies.append(copy)

        def gram(m, acc):
            acc = list(acc)
            first = pl.multiple_of(k * chunk + m * 2 * rows, 2 * rows)
            both = pl.ds(first, 2 * rows)
            weighted = field[both, :]
            low, high = weighted[:rows] * scale, weighted[rows:] * scale
            for i in range(groups):
                b = allb[i, both, :].astype(F32)
                acc[i] += b[:rows] * low + b[rows:] * high
            return tuple(acc)

        acc = lax.fori_loop(0, chunk // (2 * rows), gram, acc, unroll=6)
    part = jnp.zeros((8, lanes), F32)
    part_row = lax.broadcasted_iota(jnp.int32, (8, lanes), 0)
    for i in range(groups):
        part = jnp.where(part_row == i, jnp.sum(acc[i], axis=0, keepdims=True), part)
    sums[me] = part
    sum_copies = []
    for k in range(1, tiles):
        copy = remote(("sum", k), sums.at[me], sums.at[me], other_tile(k))
        copy.start()
        sum_copies.append(copy)
    for copy in sum_copies:
        copy.wait_recv()
    whole = sums[0]
    for k in range(1, tiles):
        whole += sums[k]
    column = jnp.sum(whole, axis=1, keepdims=True)
    cols[vec] = jnp.broadcast_to(column, (8, lanes))
    col_copies = []
    for k in range(1, groups):
        copy = remote(("col", k), cols.at[vec], cols.at[vec], other_vec(k))
        copy.start()
        col_copies.append(copy)
    column_out[...] = jnp.broadcast_to(column, (8, lanes))
    for copy in col_copies:
        copy.wait_recv()
    table = jnp.zeros((8, lanes), F32)
    wide_lane = lax.broadcasted_iota(jnp.int32, (8, lanes), 1)
    for j in range(groups):
        table = jnp.where(wide_lane == j, cols[j], table)
    coup_ref[...] = table[:groups, :groups]

    field_copy.wait()
    for copy in base_copies:
        copy.wait()
    for copy in traj_copies:
        copy.wait_send()
    basis_copy.wait_send()
    for d in range(1, pairs):
        for k in range(chunks):
            cross[k, d].wait_send()
            relay[k, d].wait_send()
        for t in range(STEPS):
            for i in range(PIECES):
                slices[t, d, i].wait_send()
                passes[t, d, i].wait_send()
    for t in range(STEPS):
        await_edges_sent(field_edges[t])
        await_edges_sent(state_edges[t])
    for copy in sum_copies + col_copies:
        copy.wait_send()


def residual_kernel(
    shape,
    column_ref,
    field_ref,
    allb_ref,
    coup_ref,
    out_ref,
    coup_out,
    field,
    allb,
    coup,
    load_sem,
    store_sem,
):
    fields, levels, rows, lanes = shape
    per_field = levels * rows
    groups = allb_ref.shape[0]
    loads, stores = [], []
    for f in range(fields):
        part = pl.ds(f * per_field, per_field)
        loads.append(
            (
                pltpu.make_async_copy(field_ref.at[part], field.at[part], load_sem.at[2 * f]),
                pltpu.make_async_copy(
                    allb_ref.at[:, part], allb.at[:, part], load_sem.at[2 * f + 1]
                ),
            )
        )
        stores.append(pltpu.make_async_copy(field.at[part], out_ref.at[part], store_sem.at[f]))
    coup_load = pltpu.make_async_copy(coup_ref, coup, load_sem.at[2 * fields])
    coup_store = pltpu.make_async_copy(coup, coup_out, store_sem.at[fields])
    for pair in loads:
        pair[0].start()
        pair[1].start()
    coup_load.start()
    factor = [jnp.broadcast_to(column_ref[i : i + 1, :], (2 * rows, lanes)) for i in range(groups)]
    coup_load.wait()
    coup_store.start()
    for f in range(fields):
        loads[f][0].wait()
        loads[f][1].wait()

        def body(m, carry):
            both = pl.ds(pl.multiple_of(f * per_field + m * 2 * rows, 2 * rows), 2 * rows)
            rest = field[both, :]
            for i in range(groups):
                rest -= allb[i, both, :].astype(F32) * factor[i]
            field[both, :] = rest
            return carry

        lax.fori_loop(0, levels // 2, body, 0, unroll=8)
        stores[f].start()
    for store in stores:
        store.wait()
    coup_store.wait()


def solution(mesh):
    groups, lats, lons = mesh.shape["vec"], mesh.shape["lat"], mesh.shape["lon"]

    def per_device(basis, trajectory, slice_owner, diffusion, energy_weight):
        _, fields, levels, rows, lanes = basis.shape
        size = fields * levels * rows
        pairs, tiles = groups // 2, lats * lons
        ids = copy_names(pairs, tiles, groups, fields)
        slots = 2 * STEPS
        vmem = pl.BlockSpec(memory_space=pltpu.VMEM)
        hbm = pl.BlockSpec(memory_space=pltpu.HBM)
        field, all_basis, column, coupling = pl.pallas_call(
            functools.partial(kernel, (fields, levels, rows, lanes), (groups, lats, lons), ids),
            out_shape=(
                jax.ShapeDtypeStruct((size, lanes), F32),
                jax.ShapeDtypeStruct((groups, size, lanes), BF16),
                jax.ShapeDtypeStruct((8, lanes), F32),
                jax.ShapeDtypeStruct((groups, groups), F32),
            ),
            in_specs=[hbm] * 5,
            out_specs=(hbm, hbm, vmem, vmem),
            scratch_shapes=[
                pltpu.SMEM(slice_owner.shape, jnp.int32),
                pltpu.SMEM(diffusion.shape, F32),
                pltpu.SMEM(energy_weight.shape, F32),
                pltpu.VMEM((size, lanes), BF16),
                pltpu.VMEM((size, lanes), BF16),
                pltpu.VMEM((STEPS, size // 2, lanes), BF16),
                pltpu.VMEM((STEPS, max(pairs - 1, 1), size, lanes), BF16),
                pltpu.VMEM((groups, size, lanes), BF16),
                pltpu.VMEM((size, lanes), F32),
                pltpu.VMEM((STEPS, size, lanes), F32),
                pltpu.VMEM((size, lanes), F32),
                pltpu.VMEM((3, size, lanes), F32),
                pltpu.VMEM((slots, fields, rows, lanes), F32),
                pltpu.VMEM((slots, 2, fields, rows, lanes), F32),
                pltpu.VMEM((slots, 2, fields * levels, lanes), BF16),
                pltpu.VMEM((slots, 2, fields * levels, lanes), BF16),
                pltpu.VMEM((slots, fields, rows, lanes), F32),
                pltpu.VMEM((slots, 2, fields * levels, lanes), F32),
                pltpu.VMEM((tiles, 8, lanes), F32),
                pltpu.VMEM((groups, 8, lanes), F32),
                pltpu.SemaphoreType.DMA((6 + SPLIT * fields,)),
                pltpu.SemaphoreType.DMA((len(ids),)),
                pltpu.SemaphoreType.DMA((len(ids),)),
            ],
            compiler_params=pltpu.CompilerParams(
                collective_id=0, has_side_effects=True, vmem_limit_bytes=60 * 1024 * 1024
            ),
        )(
            basis.reshape(size, lanes),
            trajectory.reshape(size, lanes),
            slice_owner,
            diffusion,
            energy_weight,
        )
        residual_block, coupling = pl.pallas_call(
            functools.partial(residual_kernel, (fields, levels, rows, lanes)),
            out_shape=(
                jax.ShapeDtypeStruct((size, lanes), F32),
                jax.ShapeDtypeStruct((groups, groups), F32),
            ),
            in_specs=[vmem, hbm, hbm, hbm],
            out_specs=(hbm, hbm),
            scratch_shapes=[
                pltpu.VMEM((size, lanes), F32),
                pltpu.VMEM((groups, size, lanes), BF16),
                pltpu.VMEM((groups, groups), F32),
                pltpu.SemaphoreType.DMA((2 * fields + 1,)),
                pltpu.SemaphoreType.DMA((fields + 1,)),
            ],
            compiler_params=pltpu.CompilerParams(vmem_limit_bytes=60 * 1024 * 1024),
        )(column, field, all_basis, coupling)
        return residual_block.reshape(basis.shape), coupling

    return jax.shard_map(
        per_device,
        mesh=mesh,
        in_specs=(
            P("vec", None, None, "lat", "lon"),
            P("vec", None, None, "lat", "lon"),
            P(),
            P(),
            P(),
        ),
        out_specs=(P("vec", None, None, "lat", "lon"), P()),
        check_vma=False,
    )
```

```python
import functools
import math

import jax
import jax.numpy as jnp
from jax import lax
from jax.experimental import pallas as pl
from jax.experimental.pallas import tpu as pltpu
from jax.sharding import PartitionSpec as P

STEPS = 2
PIECES = 2
CHUNKS = 4
COURANT = 0.25
MESH = pl.DeviceIdType.MESH
F32 = jnp.float32
BF16 = jnp.bfloat16


def copy_names(pairs, tiles, groups, fields):
    names = [("traj", 0), ("traj", 1), "basis"]
    for d in range(1, pairs):
        names += [(kind, k, d) for kind in ("cross", "relay") for k in range(fields)]
        names += [
            (kind, t, d, i) for kind in ("slice", "pass") for t in range(STEPS) for i in range(PIECES)
        ]
    for t in range(STEPS):
        names += [(kind, t, s) for kind in ("flon", "flat", "slon", "slat") for s in range(2)]
    names += [("sum", k) for k in range(1, tiles)]
    names += [("col", k) for k in range(1, groups)]
    return {name: i for i, name in enumerate(names)}


def kernel(
    shape,
    counts,
    ids,
    basis_ref,
    traj_ref,
    owner_in,
    diff_in,
    weight_in,
    out_ref,
    coup_ref,
    owner_ref,
    diff_ref,
    weight_ref,
    own_traj,
    sib_traj,
    sel,
    rcv,
    allb,
    field,
    state,
    moved,
    coef,
    lon_out,
    lon_in,
    lat_out,
    lat_in,
    lon_mix,
    lat_rows,
    sums,
    cols,
    local_sem,
    send_sem,
    recv_sem,
):
    fields, levels, rows, lanes = shape
    groups, lats, lons = counts
    pairs, tiles = groups // 2, lats * lons
    size = fields * levels * rows
    per_field = levels * rows
    half = size // 2
    piece = half // PIECES
    vec = lax.axis_index("vec")
    lat = lax.axis_index("lat")
    lon = lax.axis_index("lon")
    core = lax.rem(vec, 2)
    pair = vec // 2
    sibling = vec + 1 - 2 * core
    me = lat * lons + lon

    def other_tile(k):
        index = lax.rem(me + k, tiles)
        return {"lat": index // lons, "lon": lax.rem(index, lons)}

    def other_vec(k):
        return {"vec": lax.rem(vec + k, groups)}

    def partner(d):
        return {"vec": 2 * lax.rem(pair + d, pairs) + core}

    def remote(name, src, dst, device):
        return pltpu.make_async_remote_copy(
            src_ref=src,
            dst_ref=dst,
            send_sem=send_sem.at[ids[name]],
            recv_sem=recv_sem.at[ids[name]],
            device_id=device,
            device_id_type=MESH,
        )

    local = [
        pltpu.make_async_copy(source, target, local_sem.at[i])
        for i, (source, target) in enumerate(
            (
                (basis_ref, allb.at[vec]),
                (traj_ref, own_traj),
                (owner_in, owner_ref),
                (diff_in, diff_ref),
                (weight_in, weight_ref),
            )
        )
    ]
    for copy in local:
        copy.start()

    barrier = pltpu.get_barrier_semaphore()
    for k in range(1, tiles):
        pl.semaphore_signal(barrier, inc=1, device_id=other_tile(k), device_id_type=MESH)
    for k in range(1, groups):
        pl.semaphore_signal(barrier, inc=1, device_id=other_vec(k), device_id_type=MESH)
    local[1].wait()
    local[0].wait()
    pl.semaphore_wait(barrier, tiles + groups - 2)

    to_sibling = {"vec": sibling}
    own_half = pl.ds(pl.multiple_of(core * half, 16), half)
    far_half = pl.ds(pl.multiple_of((1 - core) * half, 16), half)

    traj_copies = [
        remote(("traj", i), own_traj.at[part], sib_traj.at[part], to_sibling)
        for i, part in enumerate((far_half, own_half))
    ]
    traj_copies[0].start()
    cross = {}
    relay = {}
    for d in range(1, pairs):
        source = 2 * lax.rem(pair + pairs - d, pairs) + core
        for f in range(fields):
            chunk = pl.ds(f * per_field, per_field)
            cross[f, d] = remote(
                ("cross", f, d), allb.at[vec, chunk], allb.at[vec, chunk], partner(d)
            )
            relay[f, d] = remote(
                ("relay", f, d), allb.at[source, chunk], allb.at[source, chunk], to_sibling
            )
    for d in range(1, pairs):
        cross[0, d].start()
    traj_copies[1].start()
    basis_copy = remote("basis", allb.at[vec], allb.at[vec], to_sibling)

    lane = lax.broadcasted_iota(jnp.int32, (rows, lanes), 1)
    row = lax.broadcasted_iota(jnp.int32, (rows, lanes), 0)

    def edge_copies(kind, slot, t):
        east = {"lon": lax.rem(lon + 1, lons)}
        west = {"lon": lax.rem(lon + lons - 1, lons)}
        up = {"lat": lax.rem(lat + 1, lats)}
        down = {"lat": lax.rem(lat + lats - 1, lats)}
        source, target = lat_out.at[slot], lat_in.at[slot]
        return (
            remote((kind + "lon", t, 0), lon_out.at[slot], lon_in.at[slot, 0], east),
            remote((kind + "lon", t, 1), lon_out.at[slot], lon_in.at[slot, 1], west),
            remote((kind + "lat", t, 0), source.at[1], target.at[0], up),
            remote((kind + "lat", t, 1), source.at[0], target.at[1], down),
        )

    def start_edges(copies):
        copies[0].start()
        copies[1].start()

        @pl.when(lat < lats - 1)
        def _():
            copies[2].start()

        @pl.when(lat > 0)
        def _():
            copies[3].start()

    def await_edges(copies, slot):
        copies[0].wait_recv()
        copies[1].wait_recv()

        def settle(copy, side, present):
            @pl.when(present)
            def _():
                copy.wait_recv()
                lat_rows[slot, side] = lat_in[slot, side].astype(F32)

            @pl.when(jnp.logical_not(present))
            def _():
                lat_rows[slot, side] = jnp.zeros((fields * levels, lanes), F32)

        settle(copies[2], 0, lat > 0)
        settle(copies[3], 1, lat < lats - 1)

        for f in range(fields):
            lon_mix[slot, f] = jnp.where(
                lax.rem(lane, 2) == 0,
                pltpu.roll(lon_in[slot, 0, f], 1, 1),
                pltpu.roll(lon_in[slot, 1, f], lanes - 1, 1),
            )

    def await_edges_sent(copies):
        copies[0].wait_send()
        copies[1].wait_send()

        @pl.when(lat < lats - 1)
        def _():
            copies[2].wait_send()

        @pl.when(lat > 0)
        def _():
            copies[3].wait_send()

    def at(f, level):
        return pl.ds(pl.multiple_of(f * per_field + level * rows, rows), rows)

    def note_edges(level, tile, packed):
        spot = 2 * level
        here = (lane == spot) | (lane == lax.rem(spot + lanes - 1, lanes))
        return jnp.where(here, pltpu.roll(tile, spot, 1), packed)

    def pack_rows(tiles_ref, target):
        for f in range(fields):
            for side in range(2):
                first = f * per_field + side * (rows - 1)
                edge = tiles_ref[pl.ds(first, levels, stride=rows), :]
                target[side, f * levels : (f + 1) * levels, :] = edge.astype(target.dtype)

    no_tiles = tuple(jnp.zeros((rows, lanes), F32) for _ in range(fields))

    def spread(load, tiles_ref, slot):
        def body(m, packed):
            done = []
            for f in range(fields):
                first = pl.multiple_of(f * per_field + m * 2 * rows, 2 * rows)
                both = load(pl.ds(first, 2 * rows))
                tiles_ref[pl.ds(first, 2 * rows), :] = both
                p = packed[f]
                for i in range(2):
                    p = note_edges(2 * m + i, both[i * rows : (i + 1) * rows], p)
                done.append(p)
            return tuple(done)

        packed = lax.fori_loop(0, levels // 2, body, no_tiles, unroll=8)
        for f in range(fields):
            lon_out[slot, f] = packed[f]
        pack_rows(tiles_ref, lat_out.at[slot])

    for copy in local[2:]:
        copy.wait()
    traj_copies[0].wait_recv()
    slices = {}
    passes = {}
    for t in range(STEPS):
        sel[t] = jnp.where(
            owner_ref[t] == vec,
            own_traj[own_half, :].astype(F32),
            sib_traj[own_half, :].astype(F32),
        ).astype(BF16)
        for d in range(1, pairs):
            for i in range(PIECES):
                first = pl.multiple_of(core * half + i * piece, 16)
                there = rcv.at[t, d - 1, pl.ds(first, piece)]
                slices[t, d, i] = remote(
                    ("slice", t, d, i), sel.at[t, pl.ds(i * piece, piece)], there, partner(d)
                )
                passes[t, d, i] = remote(("pass", t, d, i), there, there, to_sibling)
                slices[t, d, i].start()

    spread(lambda where: allb[vec, where, :].astype(F32), field, 0)
    field_edges = [edge_copies("f", t, t) for t in range(STEPS)]
    state_edges = [edge_copies("s", STEPS + t, t) for t in range(STEPS)]
    start_edges(field_edges[0])

    def pivots(level, carry):
        done = []
        for f in range(fields):
            above, ratio = carry[f]
            below = jnp.full((rows, lanes), diff_ref[f, level], F32)
            inv = 1.0 / (1.0 + below + above - above * ratio)
            coef[0, at(f, level), :] = inv
            coef[1, at(f, level), :] = above * inv
            coef[2, at(f, level), :] = below * inv
            done.append((below, below * inv))
        return tuple(done)

    zero = jnp.zeros((rows, lanes), F32)
    carry = lax.fori_loop(0, levels - 1, pivots, tuple((zero, zero) for _ in range(fields)))
    for f in range(fields):
        above, ratio = carry[f]
        inv = 1.0 / (1.0 + above - above * ratio)
        coef[0, at(f, levels - 1), :] = inv
        coef[1, at(f, levels - 1), :] = above * inv
        coef[2, at(f, levels - 1), :] = zero

    every = [(d, i) for i in range(PIECES) for d in range(1, pairs)]

    def take_state(t):
        for d, i in every:
            slices[t, d, i].wait_recv()
            passes[t, d, i].start()

    def build_state(t):
        for d, i in every:
            passes[t, d, i].wait_recv()
        holder = owner_ref[t] // 2
        mine = owner_ref[t] == vec

        def load_state(where):
            block = jnp.where(
                mine, own_traj[where, :].astype(F32), sib_traj[where, :].astype(F32)
            )
            for d in range(1, pairs):
                source = lax.rem(pair + pairs - d, pairs)
                block = jnp.where(holder == source, rcv[t, d - 1, where, :].astype(F32), block)
            return block

        spread(load_state, state.at[t], STEPS + t)
        start_edges(state_edges[t])

    def dlon(tile):
        after = jnp.where(lane == lanes - 1, 0.0, pltpu.roll(tile, lanes - 1, 1))
        return after - jnp.where(lane == 0, 0.0, pltpu.roll(tile, 1, 1))

    def dlat(tile):
        after = jnp.where(row == rows - 1, 0.0, pltpu.roll(tile, rows - 1, 0))
        return after - jnp.where(row == 0, 0.0, pltpu.roll(tile, 1, 0))

    lon_sign = jnp.where(lane == lanes - 1, 1.0, jnp.where(lane == 0, -1.0, 0.0))
    lat_sign = jnp.where(row == rows - 1, 1.0, jnp.where(row == 0, -1.0, 0.0))
    weight = 0.5 * COURANT

    def interior(t):
        def body(level, carry):
            tiles = [field[at(f, level), :] for f in range(fields)]
            states = [state[t, at(f, level), :] for f in range(fields)]
            for f in range(fields):
                change = states[0] * dlon(tiles[f]) + states[1] * dlat(tiles[f])
                change += tiles[0] * dlon(states[f]) + tiles[1] * dlat(states[f])
                moved[at(f, level), :] = tiles[f] - weight * change
            return carry

        lax.fori_loop(0, levels, body, 0, unroll=8)

    def beyond(slot, f, level):
        place = pl.ds(f * levels + level, 1)
        return jnp.where(row == 0, lat_rows[slot, 0, place, :], lat_rows[slot, 1, place, :])

    relayed = []

    def relay_until(end):
        for f in range(len(relayed), end):
            for d in range(1, pairs):
                cross[f, d].wait_recv()
                relay[f, d].start()
            relayed.append(f)

    def step(t):
        fslot, sslot = t, STEPS + t

        def forward(level, solved):
            shift = lax.rem(lanes - 2 * level, lanes)
            wind_u = state[t, at(0, level), :] * (weight * lon_sign)
            wind_v = state[t, at(1, level), :] * (weight * lat_sign)
            pert_u = field[at(0, level), :] * (weight * lon_sign)
            pert_v = field[at(1, level), :] * (weight * lat_sign)
            done = []
            for f in range(fields):
                change = wind_u * pltpu.roll(lon_mix[fslot, f], shift, 1)
                change += pert_u * pltpu.roll(lon_mix[sslot, f], shift, 1)
                change += wind_v * beyond(fslot, f, level) + pert_v * beyond(sslot, f, level)
                all_moved = moved[at(f, level), :] - change
                done.append(all_moved * coef[0, at(f, level), :] + solved[f] * coef[1, at(f, level), :])
            for f in range(fields):
                field[at(f, level), :] = done[f]
            return tuple(done)

        lax.fori_loop(0, levels, forward, no_tiles, unroll=16)
        if t + 1 < STEPS:
            take_state(t + 1)
        last = t == STEPS - 1
        if last:
            relay_until(fields - 2)

        def backward(k, carry):
            level = levels - 1 - k
            above, packed = carry
            done, edges = [], []
            for f in range(fields):
                x = field[at(f, level), :] + coef[2, at(f, level), :] * above[f]
                field[at(f, level), :] = x
                done.append(x)
                if not last:
                    edges.append(note_edges(level, x, packed[f]))
            return tuple(done), tuple(edges)

        _, packed = lax.fori_loop(0, levels, backward, (no_tiles, () if last else no_tiles), unroll=16)
        if not last:
            for f in range(fields):
                lon_out[t + 1, f] = packed[f]
            pack_rows(field, lat_out.at[t + 1])
            start_edges(field_edges[t + 1])

    take_state(0)
    traj_copies[1].wait_recv()
    for t in range(STEPS):
        build_state(t)
        if t == 0:
            for d in range(1, pairs):
                for f in range(1, fields):
                    cross[f, d].start()
            basis_copy.start()
        interior(t)
        if t == STEPS - 1:
            relay_until(min(2, fields))
        await_edges(field_edges[t], t)
        await_edges(state_edges[t], STEPS + t)
        step(t)
    relay_until(fields)
    basis_copy.wait_recv()

    total_rows = rows * lats
    total = float(fields * levels * total_rows * lanes * lons)
    row_ids = (lat * rows + row).astype(F32)
    cosine = jnp.cos((row_ids + 0.5) * (math.pi / total_rows) - math.pi / 2)

    def load_vector(i, f, m):
        first = pl.multiple_of(f * per_field + m * 2 * rows, 2 * rows)
        return allb[i, pl.ds(first, 2 * rows), :].astype(F32)

    acc = tuple(zero for _ in range(groups))
    for f in range(fields):
        for d in range(1, pairs):
            relay[f, d].wait_recv()
        scale = weight_ref[f] * cosine / total

        def gram(m, acc):
            acc = list(acc)
            low = field[at(f, 2 * m), :] * scale
            high = field[at(f, 2 * m + 1), :] * scale
            for i in range(groups):
                b = load_vector(i, f, m)
                acc[i] += b[:rows] * low + b[rows:] * high
            return tuple(acc)

        acc = lax.fori_loop(0, levels // 2, gram, acc, unroll=12)
    part = jnp.zeros((8, lanes), F32)
    part_row = lax.broadcasted_iota(jnp.int32, (8, lanes), 0)
    for i in range(groups):
        part = jnp.where(part_row == i, jnp.sum(acc[i], axis=0, keepdims=True), part)
    sums[me] = part
    sum_copies = []
    for k in range(1, tiles):
        copy = remote(("sum", k), sums.at[me], sums.at[me], other_tile(k))
        copy.start()
        sum_copies.append(copy)
    for copy in sum_copies:
        copy.wait_recv()
    whole = sums[0]
    for k in range(1, tiles):
        whole += sums[k]
    column = jnp.sum(whole, axis=1, keepdims=True)
    cols[vec] = jnp.broadcast_to(column, (8, lanes))
    col_copies = []
    for k in range(1, groups):
        copy = remote(("col", k), cols.at[vec], cols.at[vec], other_vec(k))
        copy.start()
        col_copies.append(copy)
    factor = [jnp.broadcast_to(column[i : i + 1], (rows, lanes)) for i in range(groups)]

    out_copies = []
    for f in range(fields):

        def residual(m, carry):
            low, high = field[at(f, 2 * m), :], field[at(f, 2 * m + 1), :]
            for i in range(groups):
                b = load_vector(i, f, m)
                low -= b[:rows] * factor[i]
                high -= b[rows:] * factor[i]
            field[at(f, 2 * m), :] = low
            field[at(f, 2 * m + 1), :] = high
            return carry

        lax.fori_loop(0, levels // 2, residual, 0, unroll=12)
        chunk = pl.ds(f * per_field, per_field)
        copy = pltpu.make_async_copy(field.at[chunk], out_ref.at[chunk], local_sem.at[5 + f])
        copy.start()
        out_copies.append(copy)

    for copy in col_copies:
        copy.wait_recv()
    table = jnp.zeros((8, lanes), F32)
    wide_lane = lax.broadcasted_iota(jnp.int32, (8, lanes), 1)
    for j in range(groups):
        table = jnp.where(wide_lane == j, cols[j], table)
    coup_ref[...] = table[:groups, :groups]

    for copy in out_copies:
        copy.wait()
    for copy in traj_copies:
        copy.wait_send()
    basis_copy.wait_send()
    for d in range(1, pairs):
        for f in range(fields):
            cross[f, d].wait_send()
            relay[f, d].wait_send()
        for t in range(STEPS):
            for i in range(PIECES):
                slices[t, d, i].wait_send()
                passes[t, d, i].wait_send()
    for t in range(STEPS):
        await_edges_sent(field_edges[t])
        await_edges_sent(state_edges[t])
    for copy in sum_copies + col_copies:
        copy.wait_send()


def hand_over(block_ref, coup_ref, block_out, coup_out, block, coup, in_sem, out_sem):
    chunk = block_ref.shape[0] // CHUNKS
    parts = [(coup_ref, coup, coup_out)]
    for i in range(CHUNKS):
        where = pl.ds(i * chunk, chunk)
        parts.append((block_ref.at[where], block.at[where], block_out.at[where]))
    loads, stores = [], []
    for i, (source, here, target) in enumerate(parts):
        loads.append(pltpu.make_async_copy(source, here, in_sem.at[i]))
        stores.append(pltpu.make_async_copy(here, target, out_sem.at[i]))
    for copy in loads:
        copy.start()
    for load, store in zip(loads, stores):
        load.wait()
        store.start()
    for copy in stores:
        copy.wait()


def solution(mesh):
    groups, lats, lons = mesh.shape["vec"], mesh.shape["lat"], mesh.shape["lon"]

    def per_device(basis, trajectory, slice_owner, diffusion, energy_weight):
        _, fields, levels, rows, lanes = basis.shape
        size = fields * levels * rows
        pairs, tiles = groups // 2, lats * lons
        ids = copy_names(pairs, tiles, groups, fields)
        slots = 2 * STEPS
        vmem = pl.BlockSpec(memory_space=pltpu.VMEM)
        hbm = pl.BlockSpec(memory_space=pltpu.HBM)
        residual_block, coupling = pl.pallas_call(
            functools.partial(kernel, (fields, levels, rows, lanes), (groups, lats, lons), ids),
            out_shape=(
                jax.ShapeDtypeStruct((size, lanes), F32),
                jax.ShapeDtypeStruct((groups, groups), F32),
            ),
            in_specs=[hbm] * 5,
            out_specs=(hbm, vmem),
            scratch_shapes=[
                pltpu.SMEM(slice_owner.shape, jnp.int32),
                pltpu.SMEM(diffusion.shape, F32),
                pltpu.SMEM(energy_weight.shape, F32),
                pltpu.VMEM((size, lanes), BF16),
                pltpu.VMEM((size, lanes), BF16),
                pltpu.VMEM((STEPS, size // 2, lanes), BF16),
                pltpu.VMEM((STEPS, max(pairs - 1, 1), size, lanes), BF16),
                pltpu.VMEM((groups, size, lanes), BF16),
                pltpu.VMEM((size, lanes), F32),
                pltpu.VMEM((STEPS, size, lanes), F32),
                pltpu.VMEM((size, lanes), F32),
                pltpu.VMEM((3, size, lanes), F32),
                pltpu.VMEM((slots, fields, rows, lanes), F32),
                pltpu.VMEM((slots, 2, fields, rows, lanes), F32),
                pltpu.VMEM((slots, 2, fields * levels, lanes), BF16),
                pltpu.VMEM((slots, 2, fields * levels, lanes), BF16),
                pltpu.VMEM((slots, fields, rows, lanes), F32),
                pltpu.VMEM((slots, 2, fields * levels, lanes), F32),
                pltpu.VMEM((tiles, 8, lanes), F32),
                pltpu.VMEM((groups, 8, lanes), F32),
                pltpu.SemaphoreType.DMA((5 + fields,)),
                pltpu.SemaphoreType.DMA((len(ids),)),
                pltpu.SemaphoreType.DMA((len(ids),)),
            ],
            compiler_params=pltpu.CompilerParams(
                collective_id=0, has_side_effects=True, vmem_limit_bytes=60 * 1024 * 1024
            ),
        )(
            basis.reshape(size, lanes),
            trajectory.reshape(size, lanes),
            slice_owner,
            diffusion,
            energy_weight,
        )
        residual_block, coupling = pl.pallas_call(
            hand_over,
            out_shape=(
                jax.ShapeDtypeStruct((size, lanes), F32),
                jax.ShapeDtypeStruct((groups, groups), F32),
            ),
            in_specs=[hbm, hbm],
            out_specs=(hbm, hbm),
            scratch_shapes=[
                pltpu.VMEM((size, lanes), F32),
                pltpu.VMEM((groups, groups), F32),
                pltpu.SemaphoreType.DMA((1 + CHUNKS,)),
                pltpu.SemaphoreType.DMA((1 + CHUNKS,)),
            ],
            compiler_params=pltpu.CompilerParams(vmem_limit_bytes=60 * 1024 * 1024),
        )(residual_block, coupling)
        return residual_block.reshape(basis.shape), coupling

    return jax.shard_map(
        per_device,
        mesh=mesh,
        in_specs=(
            P("vec", None, None, "lat", "lon"),
            P("vec", None, None, "lat", "lon"),
            P(),
            P(),
            P(),
        ),
        out_specs=(P("vec", None, None, "lat", "lon"), P()),
        check_vma=False,
    )
```

```python
import functools
import math

import jax
import jax.numpy as jnp
from jax import lax
from jax.experimental import pallas as pl
from jax.experimental.pallas import tpu as pltpu
from jax.sharding import PartitionSpec as P

STEPS = 2
PIECES = 4
CHUNKS = 4
COURANT = 0.25
MESH = pl.DeviceIdType.MESH
F32 = jnp.float32
BF16 = jnp.bfloat16


def copy_names(pairs, tiles, groups, fields):
    names = [("traj", 0), ("traj", 1), "basis"]
    for d in range(1, pairs):
        names += [(kind, k, d) for kind in ("cross", "relay") for k in range(fields)]
        names += [
            (kind, t, d, i) for kind in ("slice", "pass") for t in range(STEPS) for i in range(PIECES)
        ]
    for t in range(STEPS):
        names += [(kind, t, s) for kind in ("flon", "flat", "slon", "slat") for s in range(2)]
    names += [("sum", k) for k in range(1, tiles)]
    names += [("col", k) for k in range(1, groups)]
    return {name: i for i, name in enumerate(names)}


def kernel(
    shape,
    counts,
    ids,
    basis_ref,
    traj_ref,
    owner_in,
    diff_in,
    weight_in,
    out_ref,
    coup_ref,
    owner_ref,
    diff_ref,
    weight_ref,
    own_traj,
    sib_traj,
    sel,
    rcv,
    allb,
    field,
    state,
    moved,
    coef,
    lon_out,
    lon_in,
    lat_out,
    lat_in,
    lon_mix,
    lat_rows,
    sums,
    cols,
    local_sem,
    send_sem,
    recv_sem,
):
    fields, levels, rows, lanes = shape
    groups, lats, lons = counts
    pairs, tiles = groups // 2, lats * lons
    size = fields * levels * rows
    per_field = levels * rows
    half = size // 2
    piece = half // PIECES
    vec = lax.axis_index("vec")
    lat = lax.axis_index("lat")
    lon = lax.axis_index("lon")
    core = lax.rem(vec, 2)
    pair = vec // 2
    sibling = vec + 1 - 2 * core
    me = lat * lons + lon

    def other_tile(k):
        index = lax.rem(me + k, tiles)
        return {"lat": index // lons, "lon": lax.rem(index, lons)}

    def other_vec(k):
        return {"vec": lax.rem(vec + k, groups)}

    def partner(d):
        return {"vec": 2 * lax.rem(pair + d, pairs) + core}

    def remote(name, src, dst, device):
        return pltpu.make_async_remote_copy(
            src_ref=src,
            dst_ref=dst,
            send_sem=send_sem.at[ids[name]],
            recv_sem=recv_sem.at[ids[name]],
            device_id=device,
            device_id_type=MESH,
        )

    local = [
        pltpu.make_async_copy(source, target, local_sem.at[i])
        for i, (source, target) in enumerate(
            (
                (basis_ref, allb.at[vec]),
                (traj_ref, own_traj),
                (owner_in, owner_ref),
                (diff_in, diff_ref),
                (weight_in, weight_ref),
            )
        )
    ]
    for copy in local:
        copy.start()

    barrier = pltpu.get_barrier_semaphore()
    for k in range(1, tiles):
        pl.semaphore_signal(barrier, inc=1, device_id=other_tile(k), device_id_type=MESH)
    for k in range(1, groups):
        pl.semaphore_signal(barrier, inc=1, device_id=other_vec(k), device_id_type=MESH)
    local[1].wait()
    local[0].wait()
    pl.semaphore_wait(barrier, tiles + groups - 2)

    to_sibling = {"vec": sibling}
    own_half = pl.ds(pl.multiple_of(core * half, 16), half)
    far_half = pl.ds(pl.multiple_of((1 - core) * half, 16), half)

    traj_copies = [
        remote(("traj", i), own_traj.at[part], sib_traj.at[part], to_sibling)
        for i, part in enumerate((far_half, own_half))
    ]
    traj_copies[0].start()
    cross = {}
    relay = {}
    for d in range(1, pairs):
        source = 2 * lax.rem(pair + pairs - d, pairs) + core
        for f in range(fields):
            chunk = pl.ds(f * per_field, per_field)
            cross[f, d] = remote(
                ("cross", f, d), allb.at[vec, chunk], allb.at[vec, chunk], partner(d)
            )
            relay[f, d] = remote(
                ("relay", f, d), allb.at[source, chunk], allb.at[source, chunk], to_sibling
            )
    for d in range(1, pairs):
        cross[0, d].start()
    traj_copies[1].start()
    basis_copy = remote("basis", allb.at[vec], allb.at[vec], to_sibling)

    lane = lax.broadcasted_iota(jnp.int32, (rows, lanes), 1)
    row = lax.broadcasted_iota(jnp.int32, (rows, lanes), 0)

    def edge_copies(kind, slot, t):
        east = {"lon": lax.rem(lon + 1, lons)}
        west = {"lon": lax.rem(lon + lons - 1, lons)}
        up = {"lat": lax.rem(lat + 1, lats)}
        down = {"lat": lax.rem(lat + lats - 1, lats)}
        source, target = lat_out.at[slot], lat_in.at[slot]
        return (
            remote((kind + "lon", t, 0), lon_out.at[slot], lon_in.at[slot, 0], east),
            remote((kind + "lon", t, 1), lon_out.at[slot], lon_in.at[slot, 1], west),
            remote((kind + "lat", t, 0), source.at[1], target.at[0], up),
            remote((kind + "lat", t, 1), source.at[0], target.at[1], down),
        )

    def start_edges(copies):
        copies[0].start()
        copies[1].start()

        @pl.when(lat < lats - 1)
        def _():
            copies[2].start()

        @pl.when(lat > 0)
        def _():
            copies[3].start()

    def await_edges(copies, slot):
        copies[0].wait_recv()
        copies[1].wait_recv()

        def settle(copy, side, present):
            @pl.when(present)
            def _():
                copy.wait_recv()
                lat_rows[slot, side] = lat_in[slot, side].astype(F32)

            @pl.when(jnp.logical_not(present))
            def _():
                lat_rows[slot, side] = jnp.zeros((fields * levels, lanes), F32)

        settle(copies[2], 0, lat > 0)
        settle(copies[3], 1, lat < lats - 1)

        for f in range(fields):
            lon_mix[slot, f] = jnp.where(
                lax.rem(lane, 2) == 0,
                pltpu.roll(lon_in[slot, 0, f], 1, 1),
                pltpu.roll(lon_in[slot, 1, f], lanes - 1, 1),
            )

    def await_edges_sent(copies):
        copies[0].wait_send()
        copies[1].wait_send()

        @pl.when(lat < lats - 1)
        def _():
            copies[2].wait_send()

        @pl.when(lat > 0)
        def _():
            copies[3].wait_send()

    def at(f, level):
        return pl.ds(pl.multiple_of(f * per_field + level * rows, rows), rows)

    def note_edges(level, tile, packed):
        spot = 2 * level
        here = (lane == spot) | (lane == lax.rem(spot + lanes - 1, lanes))
        return jnp.where(here, pltpu.roll(tile, spot, 1), packed)

    def pack_rows(tiles_ref, target):
        for f in range(fields):
            for side in range(2):
                first = f * per_field + side * (rows - 1)
                edge = tiles_ref[pl.ds(first, levels, stride=rows), :]
                target[side, f * levels : (f + 1) * levels, :] = edge.astype(target.dtype)

    no_tiles = tuple(jnp.zeros((rows, lanes), F32) for _ in range(fields))

    def spread(load, tiles_ref, slot):
        def body(m, packed):
            done = []
            for f in range(fields):
                first = pl.multiple_of(f * per_field + m * 2 * rows, 2 * rows)
                both = load(pl.ds(first, 2 * rows))
                tiles_ref[pl.ds(first, 2 * rows), :] = both
                p = packed[f]
                for i in range(2):
                    p = note_edges(2 * m + i, both[i * rows : (i + 1) * rows], p)
                done.append(p)
            return tuple(done)

        packed = lax.fori_loop(0, levels // 2, body, no_tiles, unroll=12)
        for f in range(fields):
            lon_out[slot, f] = packed[f]
        pack_rows(tiles_ref, lat_out.at[slot])

    for copy in local[2:]:
        copy.wait()
    traj_copies[0].wait_recv()
    slices = {}
    passes = {}
    for t in range(STEPS):
        sel[t] = jnp.where(
            owner_ref[t] == vec,
            own_traj[own_half, :].astype(F32),
            sib_traj[own_half, :].astype(F32),
        ).astype(BF16)
        for d in range(1, pairs):
            for i in range(PIECES):
                first = pl.multiple_of(core * half + i * piece, 16)
                there = rcv.at[t, d - 1, pl.ds(first, piece)]
                slices[t, d, i] = remote(
                    ("slice", t, d, i), sel.at[t, pl.ds(i * piece, piece)], there, partner(d)
                )
                passes[t, d, i] = remote(("pass", t, d, i), there, there, to_sibling)
                slices[t, d, i].start()

    spread(lambda where: allb[vec, where, :].astype(F32), field, 0)
    field_edges = [edge_copies("f", t, t) for t in range(STEPS)]
    state_edges = [edge_copies("s", STEPS + t, t) for t in range(STEPS)]
    start_edges(field_edges[0])

    def pivots(level, carry):
        done = []
        for f in range(fields):
            above, ratio = carry[f]
            below = jnp.full((rows, lanes), diff_ref[f, level], F32)
            inv = 1.0 / (1.0 + below + above - above * ratio)
            coef[0, at(f, level), :] = inv
            coef[1, at(f, level), :] = above * inv
            coef[2, at(f, level), :] = below * inv
            done.append((below, below * inv))
        return tuple(done)

    zero = jnp.zeros((rows, lanes), F32)
    carry = lax.fori_loop(0, levels - 1, pivots, tuple((zero, zero) for _ in range(fields)))
    for f in range(fields):
        above, ratio = carry[f]
        inv = 1.0 / (1.0 + above - above * ratio)
        coef[0, at(f, levels - 1), :] = inv
        coef[1, at(f, levels - 1), :] = above * inv
        coef[2, at(f, levels - 1), :] = zero

    every = [(d, i) for i in range(PIECES) for d in range(1, pairs)]

    def take_state(t):
        for d, i in every:
            slices[t, d, i].wait_recv()
            passes[t, d, i].start()

    def build_state(t):
        for d, i in every:
            passes[t, d, i].wait_recv()
        holder = owner_ref[t] // 2
        mine = owner_ref[t] == vec

        def load_state(where):
            block = jnp.where(
                mine, own_traj[where, :].astype(F32), sib_traj[where, :].astype(F32)
            )
            for d in range(1, pairs):
                source = lax.rem(pair + pairs - d, pairs)
                block = jnp.where(holder == source, rcv[t, d - 1, where, :].astype(F32), block)
            return block

        spread(load_state, state.at[t], STEPS + t)
        start_edges(state_edges[t])

    def dlon(tile):
        after = jnp.where(lane == lanes - 1, 0.0, pltpu.roll(tile, lanes - 1, 1))
        return after - jnp.where(lane == 0, 0.0, pltpu.roll(tile, 1, 1))

    def dlat(tile):
        after = jnp.where(row == rows - 1, 0.0, pltpu.roll(tile, rows - 1, 0))
        return after - jnp.where(row == 0, 0.0, pltpu.roll(tile, 1, 0))

    lon_sign = jnp.where(lane == lanes - 1, 1.0, jnp.where(lane == 0, -1.0, 0.0))
    lat_sign = jnp.where(row == rows - 1, 1.0, jnp.where(row == 0, -1.0, 0.0))
    weight = 0.5 * COURANT

    def interior(t):
        def body(level, carry):
            tiles = [field[at(f, level), :] for f in range(fields)]
            states = [state[t, at(f, level), :] for f in range(fields)]
            for f in range(fields):
                change = states[0] * dlon(tiles[f]) + states[1] * dlat(tiles[f])
                change += tiles[0] * dlon(states[f]) + tiles[1] * dlat(states[f])
                moved[at(f, level), :] = tiles[f] - weight * change
            return carry

        lax.fori_loop(0, levels, body, 0, unroll=12)

    def beyond(slot, f, level):
        place = pl.ds(f * levels + level, 1)
        return jnp.where(row == 0, lat_rows[slot, 0, place, :], lat_rows[slot, 1, place, :])

    relayed = []

    def relay_until(end):
        for f in range(len(relayed), end):
            for d in range(1, pairs):
                cross[f, d].wait_recv()
                relay[f, d].start()
            relayed.append(f)

    def step(t):
        fslot, sslot = t, STEPS + t

        def forward(level, solved):
            shift = lax.rem(lanes - 2 * level, lanes)
            wind_u = state[t, at(0, level), :] * (weight * lon_sign)
            wind_v = state[t, at(1, level), :] * (weight * lat_sign)
            pert_u = field[at(0, level), :] * (weight * lon_sign)
            pert_v = field[at(1, level), :] * (weight * lat_sign)
            done = []
            for f in range(fields):
                change = wind_u * pltpu.roll(lon_mix[fslot, f], shift, 1)
                change += pert_u * pltpu.roll(lon_mix[sslot, f], shift, 1)
                change += wind_v * beyond(fslot, f, level) + pert_v * beyond(sslot, f, level)
                all_moved = moved[at(f, level), :] - change
                done.append(all_moved * coef[0, at(f, level), :] + solved[f] * coef[1, at(f, level), :])
            for f in range(fields):
                field[at(f, level), :] = done[f]
            return tuple(done)

        lax.fori_loop(0, levels, forward, no_tiles, unroll=24)
        if t + 1 < STEPS:
            take_state(t + 1)
        last = t == STEPS - 1
        if last:
            relay_until(fields - 2)

        def backward(k, carry):
            level = levels - 1 - k
            above, packed = carry
            done, edges = [], []
            for f in range(fields):
                x = field[at(f, level), :] + coef[2, at(f, level), :] * above[f]
                field[at(f, level), :] = x
                done.append(x)
                if not last:
                    edges.append(note_edges(level, x, packed[f]))
            return tuple(done), tuple(edges)

        _, packed = lax.fori_loop(0, levels, backward, (no_tiles, () if last else no_tiles), unroll=24)
        if not last:
            for f in range(fields):
                lon_out[t + 1, f] = packed[f]
            pack_rows(field, lat_out.at[t + 1])
            start_edges(field_edges[t + 1])

    take_state(0)
    traj_copies[1].wait_recv()
    for t in range(STEPS):
        build_state(t)
        if t == 0:
            for d in range(1, pairs):
                for f in range(1, fields):
                    cross[f, d].start()
            basis_copy.start()
        interior(t)
        if t == STEPS - 1:
            relay_until(min(2, fields))
        await_edges(field_edges[t], t)
        await_edges(state_edges[t], STEPS + t)
        step(t)
    relay_until(fields)
    basis_copy.wait_recv()

    total_rows = rows * lats
    total = float(fields * levels * total_rows * lanes * lons)
    row_ids = (lat * rows + row).astype(F32)
    cosine = jnp.cos((row_ids + 0.5) * (math.pi / total_rows) - math.pi / 2)

    def load_vector(i, f, m):
        first = pl.multiple_of(f * per_field + m * 2 * rows, 2 * rows)
        return allb[i, pl.ds(first, 2 * rows), :].astype(F32)

    acc = tuple(zero for _ in range(groups))
    for f in range(fields):
        for d in range(1, pairs):
            relay[f, d].wait_recv()
        scale = weight_ref[f] * cosine / total

        def gram(m, acc):
            acc = list(acc)
            low = field[at(f, 2 * m), :] * scale
            high = field[at(f, 2 * m + 1), :] * scale
            for i in range(groups):
                b = load_vector(i, f, m)
                acc[i] += b[:rows] * low + b[rows:] * high
            return tuple(acc)

        acc = lax.fori_loop(0, levels // 2, gram, acc, unroll=24)
    part = jnp.zeros((8, lanes), F32)
    part_row = lax.broadcasted_iota(jnp.int32, (8, lanes), 0)
    for i in range(groups):
        part = jnp.where(part_row == i, jnp.sum(acc[i], axis=0, keepdims=True), part)
    sums[me] = part
    sum_copies = []
    for k in range(1, tiles):
        copy = remote(("sum", k), sums.at[me], sums.at[me], other_tile(k))
        copy.start()
        sum_copies.append(copy)
    for copy in sum_copies:
        copy.wait_recv()
    whole = sums[0]
    for k in range(1, tiles):
        whole += sums[k]
    column = jnp.sum(whole, axis=1, keepdims=True)
    cols[vec] = jnp.broadcast_to(column, (8, lanes))
    col_copies = []
    for k in range(1, groups):
        copy = remote(("col", k), cols.at[vec], cols.at[vec], other_vec(k))
        copy.start()
        col_copies.append(copy)
    factor = [jnp.broadcast_to(column[i : i + 1], (rows, lanes)) for i in range(groups)]

    out_copies = []
    for f in range(fields):

        def residual(m, carry):
            low, high = field[at(f, 2 * m), :], field[at(f, 2 * m + 1), :]
            for i in range(groups):
                b = load_vector(i, f, m)
                low -= b[:rows] * factor[i]
                high -= b[rows:] * factor[i]
            field[at(f, 2 * m), :] = low
            field[at(f, 2 * m + 1), :] = high
            return carry

        lax.fori_loop(0, levels // 2, residual, 0, unroll=24)
        chunk = pl.ds(f * per_field, per_field)
        copy = pltpu.make_async_copy(field.at[chunk], out_ref.at[chunk], local_sem.at[5 + f])
        copy.start()
        out_copies.append(copy)

    for copy in col_copies:
        copy.wait_recv()
    table = jnp.zeros((8, lanes), F32)
    wide_lane = lax.broadcasted_iota(jnp.int32, (8, lanes), 1)
    for j in range(groups):
        table = jnp.where(wide_lane == j, cols[j], table)
    coup_ref[...] = table[:groups, :groups]

    for copy in out_copies:
        copy.wait()
    for copy in traj_copies:
        copy.wait_send()
    basis_copy.wait_send()
    for d in range(1, pairs):
        for f in range(fields):
            cross[f, d].wait_send()
            relay[f, d].wait_send()
        for t in range(STEPS):
            for i in range(PIECES):
                slices[t, d, i].wait_send()
                passes[t, d, i].wait_send()
    for t in range(STEPS):
        await_edges_sent(field_edges[t])
        await_edges_sent(state_edges[t])
    for copy in sum_copies + col_copies:
        copy.wait_send()


def hand_over(block_ref, coup_ref, block_out, coup_out, block, coup, in_sem, out_sem):
    chunk = block_ref.shape[0] // CHUNKS
    parts = [(coup_ref, coup, coup_out)]
    for i in range(CHUNKS):
        where = pl.ds(i * chunk, chunk)
        parts.append((block_ref.at[where], block.at[where], block_out.at[where]))
    loads, stores = [], []
    for i, (source, here, target) in enumerate(parts):
        loads.append(pltpu.make_async_copy(source, here, in_sem.at[i]))
        stores.append(pltpu.make_async_copy(here, target, out_sem.at[i]))
    for copy in loads:
        copy.start()
    for load, store in zip(loads, stores):
        load.wait()
        store.start()
    for copy in stores:
        copy.wait()


def solution(mesh):
    groups, lats, lons = mesh.shape["vec"], mesh.shape["lat"], mesh.shape["lon"]

    def per_device(basis, trajectory, slice_owner, diffusion, energy_weight):
        _, fields, levels, rows, lanes = basis.shape
        size = fields * levels * rows
        pairs, tiles = groups // 2, lats * lons
        ids = copy_names(pairs, tiles, groups, fields)
        slots = 2 * STEPS
        vmem = pl.BlockSpec(memory_space=pltpu.VMEM)
        hbm = pl.BlockSpec(memory_space=pltpu.HBM)
        residual_block, coupling = pl.pallas_call(
            functools.partial(kernel, (fields, levels, rows, lanes), (groups, lats, lons), ids),
            out_shape=(
                jax.ShapeDtypeStruct((size, lanes), F32),
                jax.ShapeDtypeStruct((groups, groups), F32),
            ),
            in_specs=[hbm] * 5,
            out_specs=(hbm, vmem),
            scratch_shapes=[
                pltpu.SMEM(slice_owner.shape, jnp.int32),
                pltpu.SMEM(diffusion.shape, F32),
                pltpu.SMEM(energy_weight.shape, F32),
                pltpu.VMEM((size, lanes), BF16),
                pltpu.VMEM((size, lanes), BF16),
                pltpu.VMEM((STEPS, size // 2, lanes), BF16),
                pltpu.VMEM((STEPS, max(pairs - 1, 1), size, lanes), BF16),
                pltpu.VMEM((groups, size, lanes), BF16),
                pltpu.VMEM((size, lanes), F32),
                pltpu.VMEM((STEPS, size, lanes), F32),
                pltpu.VMEM((size, lanes), F32),
                pltpu.VMEM((3, size, lanes), F32),
                pltpu.VMEM((slots, fields, rows, lanes), F32),
                pltpu.VMEM((slots, 2, fields, rows, lanes), F32),
                pltpu.VMEM((slots, 2, fields * levels, lanes), BF16),
                pltpu.VMEM((slots, 2, fields * levels, lanes), BF16),
                pltpu.VMEM((slots, fields, rows, lanes), F32),
                pltpu.VMEM((slots, 2, fields * levels, lanes), F32),
                pltpu.VMEM((tiles, 8, lanes), F32),
                pltpu.VMEM((groups, 8, lanes), F32),
                pltpu.SemaphoreType.DMA((5 + fields,)),
                pltpu.SemaphoreType.DMA((len(ids),)),
                pltpu.SemaphoreType.DMA((len(ids),)),
            ],
            compiler_params=pltpu.CompilerParams(
                collective_id=0, has_side_effects=True, vmem_limit_bytes=60 * 1024 * 1024
            ),
        )(
            basis.reshape(size, lanes),
            trajectory.reshape(size, lanes),
            slice_owner,
            diffusion,
            energy_weight,
        )
        residual_block, coupling = pl.pallas_call(
            hand_over,
            out_shape=(
                jax.ShapeDtypeStruct((size, lanes), F32),
                jax.ShapeDtypeStruct((groups, groups), F32),
            ),
            in_specs=[hbm, hbm],
            out_specs=(hbm, hbm),
            scratch_shapes=[
                pltpu.VMEM((size, lanes), F32),
                pltpu.VMEM((groups, groups), F32),
                pltpu.SemaphoreType.DMA((1 + CHUNKS,)),
                pltpu.SemaphoreType.DMA((1 + CHUNKS,)),
            ],
            compiler_params=pltpu.CompilerParams(vmem_limit_bytes=60 * 1024 * 1024),
        )(residual_block, coupling)
        return residual_block.reshape(basis.shape), coupling

    return jax.shard_map(
        per_device,
        mesh=mesh,
        in_specs=(
            P("vec", None, None, "lat", "lon"),
            P("vec", None, None, "lat", "lon"),
            P(),
            P(),
            P(),
        ),
        out_specs=(P("vec", None, None, "lat", "lon"), P()),
        check_vma=False,
    )
```

```python
import functools
import math

import jax
import jax.numpy as jnp
from jax import lax
from jax.experimental import pallas as pl
from jax.experimental.pallas import tpu as pltpu
from jax.sharding import PartitionSpec as P

STEPS = 2
PIECES = 2
CHUNKS = 4
COURANT = 0.25
MESH = pl.DeviceIdType.MESH
F32 = jnp.float32
BF16 = jnp.bfloat16


def copy_names(pairs, tiles, groups, fields):
    names = [("traj", 0), ("traj", 1), "basis"]
    for d in range(1, pairs):
        names += [(kind, k, d) for kind in ("cross", "relay") for k in range(fields)]
        names += [
            (kind, t, d, i) for kind in ("slice", "pass") for t in range(STEPS) for i in range(PIECES)
        ]
    for t in range(STEPS):
        names += [(kind, t, s) for kind in ("flon", "flat", "slon", "slat") for s in range(2)]
    names += [("sum", k) for k in range(1, tiles)]
    names += [("col", k) for k in range(1, groups)]
    return {name: i for i, name in enumerate(names)}


def kernel(
    shape,
    counts,
    ids,
    basis_ref,
    traj_ref,
    owner_in,
    diff_in,
    weight_in,
    out_ref,
    coup_out,
    coup_ref,
    owner_ref,
    diff_ref,
    weight_ref,
    own_traj,
    sib_traj,
    sel,
    rcv,
    allb,
    field,
    state,
    moved,
    coef,
    lon_out,
    lon_in,
    lat_out,
    lat_in,
    lon_mix,
    lat_rows,
    sums,
    cols,
    local_sem,
    send_sem,
    recv_sem,
):
    fields, levels, rows, lanes = shape
    groups, lats, lons = counts
    pairs, tiles = groups // 2, lats * lons
    size = fields * levels * rows
    per_field = levels * rows
    half = size // 2
    piece = half // PIECES
    vec = lax.axis_index("vec")
    lat = lax.axis_index("lat")
    lon = lax.axis_index("lon")
    core = lax.rem(vec, 2)
    pair = vec // 2
    sibling = vec + 1 - 2 * core
    me = lat * lons + lon

    def other_tile(k):
        index = lax.rem(me + k, tiles)
        return {"lat": index // lons, "lon": lax.rem(index, lons)}

    def other_vec(k):
        return {"vec": lax.rem(vec + k, groups)}

    def partner(d):
        return {"vec": 2 * lax.rem(pair + d, pairs) + core}

    def remote(name, src, dst, device):
        return pltpu.make_async_remote_copy(
            src_ref=src,
            dst_ref=dst,
            send_sem=send_sem.at[ids[name]],
            recv_sem=recv_sem.at[ids[name]],
            device_id=device,
            device_id_type=MESH,
        )

    local = [
        pltpu.make_async_copy(source, target, local_sem.at[i])
        for i, (source, target) in enumerate(
            (
                (basis_ref, allb.at[vec]),
                (traj_ref, own_traj),
                (owner_in, owner_ref),
                (diff_in, diff_ref),
                (weight_in, weight_ref),
            )
        )
    ]
    for copy in local:
        copy.start()

    barrier = pltpu.get_barrier_semaphore()
    for k in range(1, tiles):
        pl.semaphore_signal(barrier, inc=1, device_id=other_tile(k), device_id_type=MESH)
    for k in range(1, groups):
        pl.semaphore_signal(barrier, inc=1, device_id=other_vec(k), device_id_type=MESH)
    local[1].wait()
    local[0].wait()
    pl.semaphore_wait(barrier, tiles + groups - 2)

    to_sibling = {"vec": sibling}
    own_half = pl.ds(pl.multiple_of(core * half, 16), half)
    far_half = pl.ds(pl.multiple_of((1 - core) * half, 16), half)

    traj_copies = [
        remote(("traj", i), own_traj.at[part], sib_traj.at[part], to_sibling)
        for i, part in enumerate((far_half, own_half))
    ]
    traj_copies[0].start()
    cross = {}
    relay = {}
    for d in range(1, pairs):
        source = 2 * lax.rem(pair + pairs - d, pairs) + core
        for f in range(fields):
            chunk = pl.ds(f * per_field, per_field)
            cross[f, d] = remote(
                ("cross", f, d), allb.at[vec, chunk], allb.at[vec, chunk], partner(d)
            )
            relay[f, d] = remote(
                ("relay", f, d), allb.at[source, chunk], allb.at[source, chunk], to_sibling
            )
    for d in range(1, pairs):
        cross[0, d].start()
    traj_copies[1].start()
    basis_copy = remote("basis", allb.at[vec], allb.at[vec], to_sibling)

    lane = lax.broadcasted_iota(jnp.int32, (rows, lanes), 1)
    row = lax.broadcasted_iota(jnp.int32, (rows, lanes), 0)

    def edge_copies(kind, slot, t):
        east = {"lon": lax.rem(lon + 1, lons)}
        west = {"lon": lax.rem(lon + lons - 1, lons)}
        up = {"lat": lax.rem(lat + 1, lats)}
        down = {"lat": lax.rem(lat + lats - 1, lats)}
        source, target = lat_out.at[slot], lat_in.at[slot]
        return (
            remote((kind + "lon", t, 0), lon_out.at[slot], lon_in.at[slot, 0], east),
            remote((kind + "lon", t, 1), lon_out.at[slot], lon_in.at[slot, 1], west),
            remote((kind + "lat", t, 0), source.at[1], target.at[0], up),
            remote((kind + "lat", t, 1), source.at[0], target.at[1], down),
        )

    def start_edges(copies):
        copies[0].start()
        copies[1].start()

        @pl.when(lat < lats - 1)
        def _():
            copies[2].start()

        @pl.when(lat > 0)
        def _():
            copies[3].start()

    def await_edges(copies, slot):
        copies[0].wait_recv()
        copies[1].wait_recv()

        def settle(copy, side, present):
            @pl.when(present)
            def _():
                copy.wait_recv()
                lat_rows[slot, side] = lat_in[slot, side].astype(F32)

            @pl.when(jnp.logical_not(present))
            def _():
                lat_rows[slot, side] = jnp.zeros((fields * levels, lanes), F32)

        settle(copies[2], 0, lat > 0)
        settle(copies[3], 1, lat < lats - 1)

        for f in range(fields):
            lon_mix[slot, f] = jnp.where(
                lax.rem(lane, 2) == 0,
                pltpu.roll(lon_in[slot, 0, f], 1, 1),
                pltpu.roll(lon_in[slot, 1, f], lanes - 1, 1),
            )

    def await_edges_sent(copies):
        copies[0].wait_send()
        copies[1].wait_send()

        @pl.when(lat < lats - 1)
        def _():
            copies[2].wait_send()

        @pl.when(lat > 0)
        def _():
            copies[3].wait_send()

    def at(f, level):
        return pl.ds(pl.multiple_of(f * per_field + level * rows, rows), rows)

    def note_edges(level, tile, packed):
        spot = 2 * level
        here = (lane == spot) | (lane == lax.rem(spot + lanes - 1, lanes))
        return jnp.where(here, pltpu.roll(tile, spot, 1), packed)

    def pack_rows(tiles_ref, target):
        for f in range(fields):
            for side in range(2):
                first = f * per_field + side * (rows - 1)
                edge = tiles_ref[pl.ds(first, levels, stride=rows), :]
                target[side, f * levels : (f + 1) * levels, :] = edge.astype(target.dtype)

    no_tiles = tuple(jnp.zeros((rows, lanes), F32) for _ in range(fields))

    def spread(load, tiles_ref, slot):
        def body(m, packed):
            done = []
            for f in range(fields):
                first = pl.multiple_of(f * per_field + m * 2 * rows, 2 * rows)
                both = load(pl.ds(first, 2 * rows))
                tiles_ref[pl.ds(first, 2 * rows), :] = both
                p = packed[f]
                for i in range(2):
                    p = note_edges(2 * m + i, both[i * rows : (i + 1) * rows], p)
                done.append(p)
            return tuple(done)

        packed = lax.fori_loop(0, levels // 2, body, no_tiles, unroll=8)
        for f in range(fields):
            lon_out[slot, f] = packed[f]
        pack_rows(tiles_ref, lat_out.at[slot])

    for copy in local[2:]:
        copy.wait()
    traj_copies[0].wait_recv()
    slices = {}
    passes = {}
    for t in range(STEPS):
        sel[t] = jnp.where(
            owner_ref[t] == vec,
            own_traj[own_half, :].astype(F32),
            sib_traj[own_half, :].astype(F32),
        ).astype(BF16)
        for d in range(1, pairs):
            for i in range(PIECES):
                first = pl.multiple_of(core * half + i * piece, 16)
                there = rcv.at[t, d - 1, pl.ds(first, piece)]
                slices[t, d, i] = remote(
                    ("slice", t, d, i), sel.at[t, pl.ds(i * piece, piece)], there, partner(d)
                )
                passes[t, d, i] = remote(("pass", t, d, i), there, there, to_sibling)
                slices[t, d, i].start()

    spread(lambda where: allb[vec, where, :].astype(F32), field, 0)
    field_edges = [edge_copies("f", t, t) for t in range(STEPS)]
    state_edges = [edge_copies("s", STEPS + t, t) for t in range(STEPS)]
    start_edges(field_edges[0])

    def pivots(level, carry):
        done = []
        for f in range(fields):
            above, ratio = carry[f]
            below = jnp.full((rows, lanes), diff_ref[f, level], F32)
            inv = 1.0 / (1.0 + below + above - above * ratio)
            coef[0, at(f, level), :] = inv
            coef[1, at(f, level), :] = above * inv
            coef[2, at(f, level), :] = below * inv
            done.append((below, below * inv))
        return tuple(done)

    zero = jnp.zeros((rows, lanes), F32)
    carry = lax.fori_loop(0, levels - 1, pivots, tuple((zero, zero) for _ in range(fields)))
    for f in range(fields):
        above, ratio = carry[f]
        inv = 1.0 / (1.0 + above - above * ratio)
        coef[0, at(f, levels - 1), :] = inv
        coef[1, at(f, levels - 1), :] = above * inv
        coef[2, at(f, levels - 1), :] = zero

    every = [(d, i) for i in range(PIECES) for d in range(1, pairs)]

    def take_state(t):
        for d, i in every:
            slices[t, d, i].wait_recv()
            passes[t, d, i].start()

    def build_state(t):
        for d, i in every:
            passes[t, d, i].wait_recv()
        holder = owner_ref[t] // 2
        mine = owner_ref[t] == vec

        def load_state(where):
            block = jnp.where(
                mine, own_traj[where, :].astype(F32), sib_traj[where, :].astype(F32)
            )
            for d in range(1, pairs):
                source = lax.rem(pair + pairs - d, pairs)
                block = jnp.where(holder == source, rcv[t, d - 1, where, :].astype(F32), block)
            return block

        spread(load_state, state.at[t], STEPS + t)
        start_edges(state_edges[t])

    def dlon(tile):
        after = jnp.where(lane == lanes - 1, 0.0, pltpu.roll(tile, lanes - 1, 1))
        return after - jnp.where(lane == 0, 0.0, pltpu.roll(tile, 1, 1))

    def dlat(tile):
        after = jnp.where(row == rows - 1, 0.0, pltpu.roll(tile, rows - 1, 0))
        return after - jnp.where(row == 0, 0.0, pltpu.roll(tile, 1, 0))

    lon_sign = jnp.where(lane == lanes - 1, 1.0, jnp.where(lane == 0, -1.0, 0.0))
    lat_sign = jnp.where(row == rows - 1, 1.0, jnp.where(row == 0, -1.0, 0.0))
    weight = 0.5 * COURANT

    def interior(t):
        def body(level, carry):
            tiles = [field[at(f, level), :] for f in range(fields)]
            states = [state[t, at(f, level), :] for f in range(fields)]
            for f in range(fields):
                change = states[0] * dlon(tiles[f]) + states[1] * dlat(tiles[f])
                change += tiles[0] * dlon(states[f]) + tiles[1] * dlat(states[f])
                moved[at(f, level), :] = tiles[f] - weight * change
            return carry

        lax.fori_loop(0, levels, body, 0, unroll=8)

    def beyond(slot, f, level):
        place = pl.ds(f * levels + level, 1)
        return jnp.where(row == 0, lat_rows[slot, 0, place, :], lat_rows[slot, 1, place, :])

    relayed = []

    def relay_until(end):
        for f in range(len(relayed), end):
            for d in range(1, pairs):
                cross[f, d].wait_recv()
                relay[f, d].start()
            relayed.append(f)

    def step(t):
        fslot, sslot = t, STEPS + t

        def forward(level, solved):
            shift = lax.rem(lanes - 2 * level, lanes)
            wind_u = state[t, at(0, level), :] * (weight * lon_sign)
            wind_v = state[t, at(1, level), :] * (weight * lat_sign)
            pert_u = field[at(0, level), :] * (weight * lon_sign)
            pert_v = field[at(1, level), :] * (weight * lat_sign)
            done = []
            for f in range(fields):
                change = wind_u * pltpu.roll(lon_mix[fslot, f], shift, 1)
                change += pert_u * pltpu.roll(lon_mix[sslot, f], shift, 1)
                change += wind_v * beyond(fslot, f, level) + pert_v * beyond(sslot, f, level)
                all_moved = moved[at(f, level), :] - change
                done.append(all_moved * coef[0, at(f, level), :] + solved[f] * coef[1, at(f, level), :])
            for f in range(fields):
                field[at(f, level), :] = done[f]
            return tuple(done)

        lax.fori_loop(0, levels, forward, no_tiles, unroll=16)
        if t + 1 < STEPS:
            take_state(t + 1)
        last = t == STEPS - 1
        if last:
            relay_until(fields - 2)

        def backward(k, carry):
            level = levels - 1 - k
            above, packed = carry
            done, edges = [], []
            for f in range(fields):
                x = field[at(f, level), :] + coef[2, at(f, level), :] * above[f]
                field[at(f, level), :] = x
                done.append(x)
                if not last:
                    edges.append(note_edges(level, x, packed[f]))
            return tuple(done), tuple(edges)

        _, packed = lax.fori_loop(0, levels, backward, (no_tiles, () if last else no_tiles), unroll=16)
        if not last:
            for f in range(fields):
                lon_out[t + 1, f] = packed[f]
            pack_rows(field, lat_out.at[t + 1])
            start_edges(field_edges[t + 1])

    take_state(0)
    traj_copies[1].wait_recv()
    for t in range(STEPS):
        build_state(t)
        if t == 0:
            for d in range(1, pairs):
                for f in range(1, fields):
                    cross[f, d].start()
            basis_copy.start()
        interior(t)
        if t == STEPS - 1:
            relay_until(min(2, fields))
        await_edges(field_edges[t], t)
        await_edges(state_edges[t], STEPS + t)
        step(t)
    relay_until(fields)
    basis_copy.wait_recv()

    total_rows = rows * lats
    total = float(fields * levels * total_rows * lanes * lons)
    row_ids = (lat * rows + row).astype(F32)
    cosine = jnp.cos((row_ids + 0.5) * (math.pi / total_rows) - math.pi / 2)

    def load_vector(i, f, m):
        first = pl.multiple_of(f * per_field + m * 2 * rows, 2 * rows)
        return allb[i, pl.ds(first, 2 * rows), :].astype(F32)

    acc = tuple(zero for _ in range(groups))
    for f in range(fields):
        for d in range(1, pairs):
            relay[f, d].wait_recv()
        scale = weight_ref[f] * cosine / total

        def gram(m, acc):
            acc = list(acc)
            low = field[at(f, 2 * m), :] * scale
            high = field[at(f, 2 * m + 1), :] * scale
            for i in range(groups):
                b = load_vector(i, f, m)
                acc[i] += b[:rows] * low + b[rows:] * high
            return tuple(acc)

        acc = lax.fori_loop(0, levels // 2, gram, acc, unroll=12)
    part = jnp.zeros((8, lanes), F32)
    part_row = lax.broadcasted_iota(jnp.int32, (8, lanes), 0)
    for i in range(groups):
        part = jnp.where(part_row == i, jnp.sum(acc[i], axis=0, keepdims=True), part)
    sums[me] = part
    sum_copies = []
    for k in range(1, tiles):
        copy = remote(("sum", k), sums.at[me], sums.at[me], other_tile(k))
        copy.start()
        sum_copies.append(copy)
    for copy in sum_copies:
        copy.wait_recv()
    whole = sums[0]
    for k in range(1, tiles):
        whole += sums[k]
    column = jnp.sum(whole, axis=1, keepdims=True)
    cols[vec] = jnp.broadcast_to(column, (8, lanes))
    col_copies = []
    for k in range(1, groups):
        copy = remote(("col", k), cols.at[vec], cols.at[vec], other_vec(k))
        copy.start()
        col_copies.append(copy)
    factor = [jnp.broadcast_to(column[i : i + 1], (rows, lanes)) for i in range(groups)]

    out_copies = []
    for f in range(fields):

        def residual(m, carry):
            low, high = field[at(f, 2 * m), :], field[at(f, 2 * m + 1), :]
            for i in range(groups):
                b = load_vector(i, f, m)
                low -= b[:rows] * factor[i]
                high -= b[rows:] * factor[i]
            field[at(f, 2 * m), :] = low
            field[at(f, 2 * m + 1), :] = high
            return carry

        lax.fori_loop(0, levels // 2, residual, 0, unroll=12)
        chunk = pl.ds(f * per_field, per_field)
        copy = pltpu.make_async_copy(field.at[chunk], out_ref.at[chunk], local_sem.at[5 + f])
        copy.start()
        out_copies.append(copy)

    for copy in col_copies:
        copy.wait_recv()
    table = jnp.zeros((8, lanes), F32)
    wide_lane = lax.broadcasted_iota(jnp.int32, (8, lanes), 1)
    for j in range(groups):
        table = jnp.where(wide_lane == j, cols[j], table)
    coup_ref[...] = table[:groups, :groups]

    coup_copy = pltpu.make_async_copy(coup_ref, coup_out, local_sem.at[5 + fields])
    coup_copy.start()
    out_copies.append(coup_copy)
    for copy in traj_copies:
        copy.wait_send()
    basis_copy.wait_send()
    for d in range(1, pairs):
        for f in range(fields):
            cross[f, d].wait_send()
            relay[f, d].wait_send()
        for t in range(STEPS):
            for i in range(PIECES):
                slices[t, d, i].wait_send()
                passes[t, d, i].wait_send()
    for t in range(STEPS):
        await_edges_sent(field_edges[t])
        await_edges_sent(state_edges[t])
    for copy in sum_copies + col_copies:
        copy.wait_send()
    for copy in out_copies:
        copy.wait()


def hand_over(block_ref, coup_ref, block_out, coup_out, block, coup, in_sem, out_sem):
    chunk = block_ref.shape[0] // CHUNKS
    parts = [(coup_ref, coup, coup_out)]
    for i in range(CHUNKS):
        where = pl.ds(i * chunk, chunk)
        parts.append((block_ref.at[where], block.at[where], block_out.at[where]))
    loads, stores = [], []
    for i, (source, here, target) in enumerate(parts):
        loads.append(pltpu.make_async_copy(source, here, in_sem.at[i]))
        stores.append(pltpu.make_async_copy(here, target, out_sem.at[i]))
    for copy in loads:
        copy.start()
    for load, store in zip(loads, stores):
        load.wait()
        store.start()
    for copy in stores:
        copy.wait()


def solution(mesh):
    groups, lats, lons = mesh.shape["vec"], mesh.shape["lat"], mesh.shape["lon"]

    def per_device(basis, trajectory, slice_owner, diffusion, energy_weight):
        _, fields, levels, rows, lanes = basis.shape
        size = fields * levels * rows
        pairs, tiles = groups // 2, lats * lons
        ids = copy_names(pairs, tiles, groups, fields)
        slots = 2 * STEPS
        hbm = pl.BlockSpec(memory_space=pltpu.HBM)
        residual_block, coupling = pl.pallas_call(
            functools.partial(kernel, (fields, levels, rows, lanes), (groups, lats, lons), ids),
            out_shape=(
                jax.ShapeDtypeStruct((size, lanes), F32),
                jax.ShapeDtypeStruct((groups, groups), F32),
            ),
            in_specs=[hbm] * 5,
            out_specs=(hbm, hbm),
            scratch_shapes=[
                pltpu.VMEM((groups, groups), F32),
                pltpu.SMEM(slice_owner.shape, jnp.int32),
                pltpu.SMEM(diffusion.shape, F32),
                pltpu.SMEM(energy_weight.shape, F32),
                pltpu.VMEM((size, lanes), BF16),
                pltpu.VMEM((size, lanes), BF16),
                pltpu.VMEM((STEPS, size // 2, lanes), BF16),
                pltpu.VMEM((STEPS, max(pairs - 1, 1), size, lanes), BF16),
                pltpu.VMEM((groups, size, lanes), BF16),
                pltpu.VMEM((size, lanes), F32),
                pltpu.VMEM((STEPS, size, lanes), F32),
                pltpu.VMEM((size, lanes), F32),
                pltpu.VMEM((3, size, lanes), F32),
                pltpu.VMEM((slots, fields, rows, lanes), F32),
                pltpu.VMEM((slots, 2, fields, rows, lanes), F32),
                pltpu.VMEM((slots, 2, fields * levels, lanes), BF16),
                pltpu.VMEM((slots, 2, fields * levels, lanes), BF16),
                pltpu.VMEM((slots, fields, rows, lanes), F32),
                pltpu.VMEM((slots, 2, fields * levels, lanes), F32),
                pltpu.VMEM((tiles, 8, lanes), F32),
                pltpu.VMEM((groups, 8, lanes), F32),
                pltpu.SemaphoreType.DMA((6 + fields,)),
                pltpu.SemaphoreType.DMA((len(ids),)),
                pltpu.SemaphoreType.DMA((len(ids),)),
            ],
            compiler_params=pltpu.CompilerParams(
                collective_id=0, has_side_effects=True, vmem_limit_bytes=60 * 1024 * 1024
            ),
        )(
            basis.reshape(size, lanes),
            trajectory.reshape(size, lanes),
            slice_owner,
            diffusion,
            energy_weight,
        )
        residual_block, coupling = pl.pallas_call(
            hand_over,
            out_shape=(
                jax.ShapeDtypeStruct((size, lanes), F32),
                jax.ShapeDtypeStruct((groups, groups), F32),
            ),
            in_specs=[hbm, hbm],
            out_specs=(hbm, hbm),
            scratch_shapes=[
                pltpu.VMEM((size, lanes), F32),
                pltpu.VMEM((groups, groups), F32),
                pltpu.SemaphoreType.DMA((1 + CHUNKS,)),
                pltpu.SemaphoreType.DMA((1 + CHUNKS,)),
            ],
            compiler_params=pltpu.CompilerParams(vmem_limit_bytes=60 * 1024 * 1024),
        )(residual_block, coupling)
        return residual_block.reshape(basis.shape), coupling

    return jax.shard_map(
        per_device,
        mesh=mesh,
        in_specs=(
            P("vec", None, None, "lat", "lon"),
            P("vec", None, None, "lat", "lon"),
            P(),
            P(),
            P(),
        ),
        out_specs=(P("vec", None, None, "lat", "lon"), P()),
        check_vma=False,
    )
```
